32 devices in a mesh: img: 8 (over y, x, core), lat: 4 (over z).
Axes of the slice: x: 2, y: 2, z: 4, core: 2. Of those that a mesh axis runs over, the one named last changes fastest.
Arguments:
- latents: bfloat16 [48, 512, 1024], P('img', 'lat'), may hold values from -6 to 6
- pixels: bfloat16 [48, 4096, 261], P('img', 'lat'), may hold values from -6 to 6
- keep_mask: int32 [48, 4096], P('img', 'lat'), may hold values from 0 to 1, as said below
- cotangent: bfloat16 [48, 512, 1024], P('img', 'lat'), may hold values from -6 to 6
- gain_latent: float32 [1024], replicated, may hold values from 0.1 to 1.9
- gain_pixel: float32 [261], replicated, may hold values from 0.1 to 1.9
- gain_mlp: float32 [1024], replicated, may hold values from 0.1 to 1.9
- w_query: bfloat16 [1024, 1024], P(('img', 'lat')), may hold values from -0.1875 to 0.1875
- w_key: bfloat16 [261, 1024], P(None, ('img', 'lat')), may hold values from -0.375 to 0.375
- w_value: bfloat16 [261, 1024], P(None, ('img', 'lat')), may hold values from -0.375 to 0.375
- w_output: bfloat16 [1024, 1024], P(('img', 'lat')), may hold values from -6 to 6
- w_hidden: bfloat16 [1024, 1024], P(('img', 'lat')), may hold values from -0.1875 to 0.1875
- w_return: bfloat16 [1024, 1024], P(('img', 'lat')), may hold values from -0.1875 to 0.1875
Outputs:
- output: bfloat16 [48, 512, 1024], P('img', 'lat')
- grad_latents: bfloat16 [48, 512, 1024], P('img', 'lat')
- grad_pixels: bfloat16 [48, 4096, 261], P('img', 'lat')
- grad_query: float32 [1024, 1024], P(('img', 'lat'))
- grad_key: float32 [261, 1024], P(None, ('img', 'lat'))
- grad_value: float32 [261, 1024], P(None, ('img', 'lat'))
- grad_output: float32 [1024, 1024], P(('img', 'lat'))
- grad_hidden: float32 [1024, 1024], P(('img', 'lat'))
- grad_return: float32 [1024, 1024], P(('img', 'lat'))
- grad_gain_latent: float32 [1024], replicated
- grad_gain_pixel: float32 [261], replicated
- grad_gain_mlp: float32 [1024], replicated
The draws below stay inside these ranges and needn't reach their ends.
Inputs may be any that keep to these rules, and one draw needn't show every extreme that they name: `keep_mask`: values 0 or 1; each image keeps between 30 and 95 percent of its 4096 pixels.
All inputs are finite; a program needn't handle non-finite values.
Results may differ from the reference program's by a relative error of at most 0.017.
Values may be sent and summed in bfloat16 or wider, within the bound.
No kernel may reach another device: no remote copies, remote signals or barrier semaphores. Data moves between devices by JAX's collectives and lax.ppermute only.
A program may use at most 320 MiB of HBM per device.

```python
import jax
import jax.numpy as jnp
from jax import lax

D = 1024
LATENTS = 512
C = 261
PIX = 4096
IMAGES = 48


def draw_keep_mask(key, part):
    key = jax.random.fold_in(key, 7)
    count_key, order_key = jax.random.split(key)
    lowest = (3 * PIX + 9) // 10
    highest = 95 * PIX // 100
    counts = jax.random.randint(count_key, (IMAGES,), lowest, highest + 1)
    image_keys = jax.random.split(order_key, IMAGES)
    ranks = jax.vmap(lambda k: jax.random.permutation(k, PIX))(image_keys)
    return (ranks < counts[:, None]).astype(jnp.int32)


def shard_levels(key, extent, shards, least, largest):
    level, own = 1.0, jax.random.fold_in(key, 6)
    for axis_at, parts in shards:
        heights = jnp.exp(jax.random.uniform(jax.random.fold_in(own, axis_at), (parts,), jnp.float32, least / len(shards), largest / len(shards)))
        level = level * jnp.repeat(heights, extent[axis_at] // parts).reshape([-1 if axis == axis_at else 1 for axis in range(len(extent))])
    return level


def normal_values(key, shape, width, most, pieces=(), kind=jnp.bfloat16):
    level = shard_levels(key, shape, pieces, -0.22, 0.18) if pieces else 1.0
    drawn = jax.random.normal(key, shape, jnp.float32) * width * level
    return jnp.minimum(jnp.maximum(drawn, -most), most).astype(kind)


def setup_inputs(seed: int = 0) -> dict:
    arg_keys = jax.random.split(jax.random.key(seed), 14)
    latents = normal_values(arg_keys[0], (IMAGES, LATENTS, D), 1.0, 6.0, ((0, 8), (1, 4)))
    pixels = normal_values(arg_keys[1], (IMAGES, PIX, C), 1.0, 6.0, ((0, 8), (1, 4)))
    keep_mask = draw_keep_mask(jax.random.fold_in(arg_keys[13], 71), 0)
    cotangent = normal_values(arg_keys[3], (IMAGES, LATENTS, D), 1.0, 6.0, ((0, 8), (1, 4)))
    gain_latent = jnp.clip(1.0 + 0.18 * jax.random.normal(arg_keys[4], (D,), jnp.float32), 0.1, 1.9)
    gain_pixel = jnp.clip(1.0 + 0.18 * jax.random.normal(arg_keys[5], (C,), jnp.float32), 0.1, 1.9)
    gain_mlp = jnp.clip(1.0 + 0.18 * jax.random.normal(arg_keys[6], (D,), jnp.float32), 0.1, 1.9)
    w_query = normal_values(arg_keys[7], (D, D), D ** -0.5, 0.1875, ((0, 32),))
    w_key = normal_values(arg_keys[8], (C, D), C ** -0.5, 0.375, ((1, 32),))
    w_value = normal_values(arg_keys[9], (C, D), C ** -0.5, 0.375, ((1, 32),))
    w_output = normal_values(arg_keys[10], (D, D), (max(1, 2 * D // PIX)) ** -0.5, 6.0, ((0, 32),))
    w_hidden = normal_values(arg_keys[11], (D, D), D ** -0.5, 0.1875, ((0, 32),))
    w_return = normal_values(arg_keys[12], (D, D), D ** -0.5, 0.1875, ((0, 32),))
    return dict(latents=latents, pixels=pixels, keep_mask=keep_mask, cotangent=cotangent, gain_latent=gain_latent, gain_pixel=gain_pixel, gain_mlp=gain_mlp, w_query=w_query, w_key=w_key, w_value=w_value, w_output=w_output, w_hidden=w_hidden, w_return=w_return)


@jax.custom_vjp
def low(v):
    return lax.optimization_barrier(v.astype(jnp.bfloat16)).astype(jnp.float32)

@jax.custom_vjp
def low_back(v):
    return v

def low_keep(v):
    return (low(v), None)

def low_pass(kept, grad):
    return (grad,)

def back_keep(v):
    return (v, None)

def back_low(kept, grad):
    return (low(grad),)
low.defvjp(low_keep, low_pass)
low_back.defvjp(back_keep, back_low)

def matmul(left, right):
    return jnp.dot(left, right, precision=lax.Precision.HIGHEST, preferred_element_type=jnp.float32)

def layer_norm(values, gain):
    centered = values - lax.optimization_barrier(jnp.mean(values, -1, keepdims=True))
    rstd = lax.rsqrt(lax.optimization_barrier(jnp.mean(centered * centered, -1, keepdims=True)) + 1e-05)
    return centered * rstd * gain

def single_image(item, params):
    lat, pix, keep = item
    gain_lat, gain_pix, gain_mid, wq, wk, wv, wo, w1, w2 = params
    lat_in = low(layer_norm(lat, gain_lat))
    pix_in = low(layer_norm(pix, gain_pix))
    query = low(low_back(matmul(lat_in, wq)))
    keys = low(matmul(pix_in, wk))
    vals = low(matmul(pix_in, wv))
    scores = matmul(query, keys.T) * D ** (-0.5)
    scores = low_back(jnp.where(keep[None, :] > 0, scores, -jnp.inf))
    top = lax.optimization_barrier(jnp.max(scores, -1, keepdims=True))
    expo = jnp.exp(scores - top)
    probs = low(expo / lax.optimization_barrier(jnp.sum(expo, -1, keepdims=True)))
    attended = low(low_back(matmul(probs, vals)))
    middle = lat + low_back(matmul(attended, wo))
    mlp_in = low(layer_norm(middle, gain_mid))
    act = low(jax.nn.gelu(low_back(matmul(mlp_in, w1)), approximate=False))
    return middle + low_back(matmul(act, w2))

def reference(latents, pixels, keep_mask, cotangent, gain_latent, gain_pixel, gain_mlp, w_query, w_key, w_value, w_output, w_hidden, w_return):
    params = tuple((arr.astype(jnp.float32) for arr in (gain_latent, gain_pixel, gain_mlp, w_query, w_key, w_value, w_output, w_hidden, w_return)))
    lat_f = latents.astype(jnp.float32)
    pix_f = pixels.astype(jnp.float32)

    def forward(lat_all, pix_all, *weights):
        step = jax.checkpoint(lambda item: single_image(item, weights))
        return lax.map(step, (lat_all, pix_all, keep_mask))
    result, pullback = jax.vjp(forward, lat_f, pix_f, *params)
    grads = pullback(cotangent.astype(jnp.float32))
    return (result.astype(jnp.bfloat16), grads[0].astype(jnp.bfloat16), grads[1].astype(jnp.bfloat16), grads[5], grads[6], grads[7], grads[8], grads[9], grads[10], grads[2], grads[3], grads[4])
```

```python
from functools import partial

import jax
import jax.numpy as jnp
from jax import lax
from jax.experimental import pallas as pl
from jax.experimental.pallas import tpu as pltpu
from jax.sharding import PartitionSpec as P

F32 = jnp.float32
BF16 = jnp.bfloat16
AXES = ("img", "lat")
OUT_OF_SIGHT = -1e30
VMEM = 56 * 1024 * 1024


def round_up(value, unit):
    return -(-value // unit) * unit


def normalize(values):
    centered = values - jnp.mean(values, -1, keepdims=True)
    rstd = lax.rsqrt(jnp.mean(centered * centered, -1, keepdims=True) + 1e-05)
    return (centered * rstd, rstd)


def norm_back(upstream, normed, rstd):
    return rstd * (
        upstream
        - jnp.mean(upstream, -1, keepdims=True)
        - normed * jnp.mean(upstream * normed, -1, keepdims=True)
    )


def dot(left, right, contract):
    return lax.dot_general(left, right, (contract, ((), ())), preferred_element_type=F32)


def img_bits(parts):
    return parts.bit_length() - 1


def swap_img(value, bit, parts):
    return lax.ppermute(value, "img", [(i, i ^ (1 << bit)) for i in range(parts)])


def bit_of(bit):
    return (lax.axis_index("img") >> bit) & 1


def ordered(own, other, bit, axis):
    is_low = bit_of(bit) == 0
    return jnp.concatenate(
        [jnp.where(is_low, own, other), jnp.where(is_low, other, own)], axis=axis
    )


def lat_blocks(value, size):
    blocks = [value]
    for step in range(1, size):
        pairs = [(i, i ^ step) for i in range(size)]
        blocks.append(lax.ppermute(value, "lat", pairs))
    return blocks


def lat_ordered(blocks):
    stacked = jnp.stack(blocks)
    me = lax.axis_index("lat")
    return jnp.concatenate(
        [lax.dynamic_index_in_dim(stacked, me ^ j, 0, False) for j in range(len(blocks))], axis=0
    )


def gather_rows(shard, imgs, lats):
    rows = lat_ordered(lat_blocks(shard, lats))
    span = rows.shape[0]
    for bit in reversed(range(img_bits(imgs))):
        other = swap_img(rows, bit, imgs)
        grouped = rows.reshape(-1, 1, span, rows.shape[-1])
        grouped_other = other.reshape(-1, 1, span, rows.shape[-1])
        rows = ordered(grouped, grouped_other, bit, 1).reshape(-1, rows.shape[-1])
    return rows


def scatter_rows(total, imgs, lats):
    columns = total.shape[-1]
    span = total.shape[0] // imgs
    for bit in range(img_bits(imgs)):
        halves = total.reshape(-1, 2, span, columns)
        is_low = bit_of(bit) == 0
        mine = jnp.where(is_low, halves[:, 0], halves[:, 1])
        sent = jnp.where(is_low, halves[:, 1], halves[:, 0]).astype(BF16)
        total = mine + swap_img(sent, bit, imgs).astype(F32)
    blocks = total.reshape(lats, span // lats, columns)
    me = lax.axis_index("lat")
    result = lax.dynamic_index_in_dim(blocks, me, 0, False)
    for step in range(1, lats):
        sent = lax.dynamic_index_in_dim(blocks, me ^ step, 0, False).astype(BF16)
        pairs = [(i, i ^ step) for i in range(lats)]
        result = result + lax.ppermute(sent, "lat", pairs).astype(F32)
    return result


def sum_everywhere(total, imgs, lats):
    for bit in range(img_bits(imgs)):
        half = total.shape[-1] // 2
        is_low = bit_of(bit) == 0
        mine = jnp.where(is_low, total[:, :half], total[:, half:])
        sent = jnp.where(is_low, total[:, half:], total[:, :half]).astype(BF16)
        total = mine + swap_img(sent, bit, imgs).astype(F32)
    terms = [block.astype(F32) for block in lat_blocks(total.astype(BF16), lats)]
    while len(terms) > 1:
        terms = [terms[i] + terms[i + 1] for i in range(0, len(terms), 2)]
    whole = terms[0].astype(BF16)
    for bit in reversed(range(img_bits(imgs))):
        whole = ordered(whole, swap_img(whole, bit, imgs), bit, 1)
    return whole


def lat_gather(value, size):
    return lat_blocks(value, size)


def lat_return(blocks, size):
    out = [blocks[0]]
    for step in range(1, size):
        pairs = [(i, i ^ step) for i in range(size)]
        out.append(lax.ppermute(blocks[step], "lat", pairs))
    return out


def pixel_kernel(channels, raw_ref, bias_ref, gain_ref, wide_ref, tall_ref, work):
    raw = raw_ref[0].astype(F32)
    rows = work.shape[0]
    centered = raw - jnp.sum(raw, 0, keepdims=True) * (1.0 / channels)
    rstd = lax.rsqrt(jnp.sum(centered * centered, 0, keepdims=True) * (1.0 / channels) + 1e-05)
    base = channels // 8 * 8
    row = lax.broadcasted_iota(jnp.int32, (rows - base, raw.shape[1]), 0) + base
    work[base:rows] = jnp.where((row > channels) & (row < channels + 6), 1.0, 0.0).astype(F32)
    work[0:channels] = centered * rstd * gain_ref[...]
    work[channels : channels + 1] = bias_ref[0]
    whole = work[...]
    wide_ref[0] = whole[: wide_ref.shape[1]].astype(BF16)
    tall_ref[0] = whole.T.astype(BF16)


def pixel_prep(raw, bias, gain, rows):
    images, channels, pixels = raw.shape
    lanes = round_up(rows, 128)
    return pl.pallas_call(
        partial(pixel_kernel, channels),
        grid=(images,),
        in_specs=[
            pl.BlockSpec((1, channels, pixels), lambda b: (b, 0, 0)),
            pl.BlockSpec((1, 1, pixels), lambda b: (b, 0, 0)),
            pl.BlockSpec((channels, 1), lambda b: (0, 0)),
        ],
        out_specs=[
            pl.BlockSpec((1, rows, pixels), lambda b: (b, 0, 0)),
            pl.BlockSpec((1, pixels, lanes), lambda b: (b, 0, 0)),
        ],
        out_shape=[
            jax.ShapeDtypeStruct((images, rows, pixels), BF16),
            jax.ShapeDtypeStruct((images, pixels, lanes), BF16),
        ],
        scratch_shapes=[pltpu.VMEM((lanes, pixels), F32)],
        compiler_params=pltpu.CompilerParams(vmem_limit_bytes=VMEM),
        cost_estimate=pl.CostEstimate(
            flops=images * channels * pixels * 10,
            bytes_accessed=images * pixels * (channels + rows + lanes) * 2,
            transcendentals=0,
        ),
    )(raw, bias, gain)


def split3(value):
    first = lax.reduce_precision(value, 8, 7)
    second = lax.reduce_precision(value - first, 8, 7)
    return (first.astype(BF16), second.astype(BF16), (value - first - second).astype(BF16))


def attend_kernel(channels, blocks, tile, *refs):
    wide_ref, tall_ref = refs[:2]
    query_refs = refs[2 : 2 + blocks]
    out_refs = refs[2 + blocks : 2 + 2 * blocks]
    weight, scores = refs[2 + 2 * blocks :]
    rows = wide_ref.shape[1]
    pixels = wide_ref.shape[2]
    span = query_refs[0].shape[2]
    weight[:rows] = jnp.concatenate([ref[0] for ref in query_refs], axis=1)
    weight[rows:] = jnp.zeros((weight.shape[0] - rows, weight.shape[1]), BF16)
    top = None
    for at in range(0, pixels, tile):
        part = dot(tall_ref[0, at : at + tile], weight[...], ((1,), (0,)))
        scores[at : at + tile] = part
        part_top = jnp.max(part, 0, keepdims=True)
        top = part_top if top is None else jnp.maximum(top, part_top)
    total = jnp.zeros((rows, weight.shape[1]), F32)
    for at in range(0, pixels, tile):
        expo = jnp.exp(scores[at : at + tile] - top).astype(BF16)
        total += dot(wide_ref[0, :, at : at + tile], expo, ((1,), (0,)))
    mass = total[channels + 1 : channels + 2]
    attended = total * (1.0 / mass)
    log_mass = top + jnp.log(mass)
    first = log_mass.astype(BF16).astype(F32)
    second = (log_mass - first).astype(BF16).astype(F32)
    parts = [first, second, log_mass - first - second]
    row = lax.broadcasted_iota(jnp.int32, total.shape, 0)
    attended = jnp.where(row < channels, attended, 0.0)
    for k, part in enumerate(parts):
        attended = jnp.where(row == channels + 1 + k, part, attended)
    attended = attended.astype(BF16)
    for k, ref in enumerate(out_refs):
        ref[0] = attended[:, k * span : (k + 1) * span]


def attend(wide, tall, queries, channels, span):
    images, rows, pixels = wide.shape
    lanes = tall.shape[2]
    blocks = len(queries)
    tile = min(256, pixels)
    block = pl.BlockSpec((1, rows, span), lambda b: (b, 0, 0))
    return pl.pallas_call(
        partial(attend_kernel, channels, blocks, tile),
        grid=(images,),
        in_specs=[
            pl.BlockSpec((1, rows, pixels), lambda b: (b, 0, 0)),
            pl.BlockSpec((1, pixels, lanes), lambda b: (b, 0, 0)),
        ]
        + [block] * blocks,
        out_specs=[block] * blocks,
        out_shape=[jax.ShapeDtypeStruct((images, rows, span), BF16)] * blocks,
        scratch_shapes=[
            pltpu.VMEM((lanes, blocks * span), BF16),
            pltpu.VMEM((pixels, blocks * span), F32),
        ],
        compiler_params=pltpu.CompilerParams(vmem_limit_bytes=VMEM),
        cost_estimate=pl.CostEstimate(
            flops=images * pixels * blocks * span * rows * 4,
            bytes_accessed=images * pixels * (rows + lanes) * 2 + images * rows * blocks * span * 4,
            transcendentals=images * pixels * blocks * span,
        ),
    )(wide, tall, *queries)


def attend_back_kernel(channels, blocks, tile, *refs):
    wide_ref, tall_ref, raw_ref, gain_ref = refs[:4]
    query_refs = refs[4 : 4 + blocks]
    att_refs = refs[4 + blocks : 4 + 2 * blocks]
    grad_ref = refs[4 + 2 * blocks]
    out_refs = refs[5 + 2 * blocks : 5 + 3 * blocks]
    query_weight, att_weight = refs[5 + 3 * blocks :]
    rows = wide_ref.shape[1]
    pixels = wide_ref.shape[2]
    span = query_refs[0].shape[2]
    width = blocks * span
    queries = jnp.concatenate([ref[0] for ref in query_refs], axis=1)
    atts = jnp.concatenate([ref[0] for ref in att_refs], axis=1)
    row = lax.broadcasted_iota(jnp.int32, (rows, width), 0)
    shifts = (row > channels) & (row < channels + 4)
    query_weight[:rows] = jnp.where(shifts, atts.astype(F32), queries.astype(F32)).astype(BF16)
    att_weight[:rows] = jnp.where(shifts, 0.0, atts.astype(F32)).astype(BF16)
    fill = jnp.zeros((query_weight.shape[0] - rows, width), BF16)
    query_weight[rows:] = fill
    att_weight[rows:] = fill
    total = jnp.zeros((rows, width), F32)
    for at in range(0, pixels, tile):
        tall = tall_ref[0, at : at + tile]
        probs = jnp.exp(dot(tall, query_weight[...], ((1,), (0,))))
        grad = probs * dot(tall, att_weight[...], ((1,), (0,)))
        grad_low = grad.astype(BF16)
        probs_low = probs.astype(BF16)
        total += dot(wide_ref[0, :, at : at + tile], grad_low, ((1,), (0,)))
        into = dot(query_weight[:rows], grad_low, ((1,), (1,)))
        into += dot(att_weight[:rows], probs_low, ((1,), (1,)))
        raw = raw_ref[0, :, at : at + tile].astype(F32)
        centered = raw - jnp.sum(raw, 0, keepdims=True) * (1.0 / channels)
        rstd = lax.rsqrt(
            jnp.sum(centered * centered, 0, keepdims=True) * (1.0 / channels) + 1e-05
        )
        hat = centered * rstd
        upstream = into[:channels] * gain_ref[...]
        mean = jnp.sum(upstream, 0, keepdims=True) * (1.0 / channels)
        along = jnp.sum(upstream * hat, 0, keepdims=True) * (1.0 / channels)
        grad_ref[0, :, at : at + tile] = (rstd * (upstream - mean - hat * along)).astype(BF16)
    total = total.astype(BF16)
    for k, ref in enumerate(out_refs):
        ref[0] = total[:, k * span : (k + 1) * span]


def attend_back(wide, tall, raw, gain, queries, atts, channels, span):
    images, rows, pixels = wide.shape
    lanes = tall.shape[2]
    blocks = len(queries)
    tile = min(256, pixels)
    block = pl.BlockSpec((1, rows, span), lambda b: (b, 0, 0))
    whole = pl.BlockSpec((1, channels, pixels), lambda b: (b, 0, 0))
    results = pl.pallas_call(
        partial(attend_back_kernel, channels, blocks, tile),
        grid=(images,),
        in_specs=[
            pl.BlockSpec((1, rows, pixels), lambda b: (b, 0, 0)),
            pl.BlockSpec((1, pixels, lanes), lambda b: (b, 0, 0)),
            whole,
            pl.BlockSpec((channels, 1), lambda b: (0, 0)),
        ]
        + [block] * (2 * blocks),
        out_specs=[whole] + [block] * blocks,
        out_shape=[jax.ShapeDtypeStruct((images, channels, pixels), BF16)]
        + [jax.ShapeDtypeStruct((images, rows, span), BF16)] * blocks,
        scratch_shapes=[
            pltpu.VMEM((lanes, blocks * span), BF16),
            pltpu.VMEM((lanes, blocks * span), BF16),
        ],
        compiler_params=pltpu.CompilerParams(vmem_limit_bytes=VMEM),
        cost_estimate=pl.CostEstimate(
            flops=images * pixels * blocks * span * rows * 10,
            bytes_accessed=images * pixels * (rows * 3 + lanes) * 2
            + images * rows * blocks * span * 6,
            transcendentals=images * pixels * blocks * span,
        ),
    )(wide, tall, raw, gain, *queries, *atts)
    return results[0], results[1:]


def local(
    imgs,
    lats,
    latents,
    pixels,
    keep_mask,
    cotangent,
    gain_latent,
    gain_pixel,
    gain_mlp,
    w_query,
    w_key,
    w_value,
    w_output,
    w_hidden,
    w_return,
):
    images, span, depth = latents.shape
    channels = pixels.shape[2]
    devices = imgs * lats
    share = depth // devices
    rows = round_up(channels + 6, 16)
    scale = depth ** (-0.5)
    count = images * span
    me = lax.axis_index("img") * lats + lax.axis_index("lat")

    raw = jnp.swapaxes(pixels, 1, 2)
    bias = jnp.where(keep_mask > 0, 0.0, OUT_OF_SIGHT).astype(F32)[:, None, :]
    gain_column = gain_pixel[:, None]
    wide, tall = pixel_prep(raw, bias, gain_column, rows)

    key_rows = gather_rows(w_key.T, imgs, lats)
    query_rows = gather_rows(w_query, imgs, lats)
    query_key = (dot(key_rows, query_rows, ((0,), (1,))) * scale).astype(BF16)
    value_out = dot(w_value, w_output, ((1,), (0,)))
    value_out = sum_everywhere(value_out, imgs, lats)
    hidden = gather_rows(w_hidden, imgs, lats)
    back = gather_rows(w_return, imgs, lats)
    query_columns = lax.all_to_all(
        w_query.reshape(share, devices, share), AXES, 1, 0, tiled=True
    ).reshape(depth, share)

    lat_f = latents.reshape(count, depth).astype(F32)
    cot = cotangent.reshape(count, depth)
    lat_hat, lat_rstd = normalize(lat_f)
    lat_in = (lat_hat * gain_latent).astype(BF16)
    query = jnp.einsum(
        "cd,bld->bcl", query_key, lat_in.reshape(images, span, depth), preferred_element_type=F32
    ).astype(BF16)
    ones = jnp.ones((images, 1, span), BF16)
    zeros = jnp.zeros((images, rows - channels - 1, span), BF16)
    query = jnp.concatenate([query, ones, zeros], axis=1)
    queries = lat_gather(query, lats)

    parts = attend(wide, tall, queries, channels, span)
    parts = [part.astype(F32) for part in lat_return(parts, lats)]
    logs = [
        part[:, channels + 1] + part[:, channels + 2] + part[:, channels + 3] for part in parts
    ]
    top = logs[0]
    for log in logs[1:]:
        top = jnp.maximum(top, log)
    shares = [jnp.exp(log - top) for log in logs]
    mass = sum(shares)
    log_mass = top + jnp.log(mass)
    pooled = sum(
        part[:, :channels] * (weight / mass)[:, None] for part, weight in zip(parts, shares)
    )
    pooled_low = pooled.astype(BF16)

    attended = jnp.einsum("bcl,cd->bld", pooled_low, value_out, preferred_element_type=F32)
    middle = lat_f + attended.reshape(count, depth)
    mid_hat, mid_rstd = normalize(middle)
    mlp_in = (mid_hat * gain_mlp).astype(BF16)
    pre = dot(mlp_in, hidden, ((1,), (0,)))
    act, gelu_back = jax.vjp(partial(jax.nn.gelu, approximate=False), pre)
    act_low = act.astype(BF16)
    output = (middle + dot(act_low, back, ((1,), (0,)))).astype(BF16)

    grad_return = dot(act_low, cot, ((0,), (0,)))
    shard_r = scatter_rows(grad_return, imgs, lats)
    grad_act = dot(cot, back, ((1,), (1,)))
    grad_pre = gelu_back(grad_act)[0].astype(BF16)
    grad_hidden = dot(mlp_in, grad_pre, ((0,), (0,)))
    shard_h = scatter_rows(grad_hidden, imgs, lats)
    grad_mlp_in = dot(grad_pre, hidden, ((1,), (1,)))
    grad_gain_mlp = jnp.sum(grad_mlp_in * mid_hat, 0, keepdims=True)
    grad_middle = cot.astype(F32) + norm_back(grad_mlp_in * gain_mlp, mid_hat, mid_rstd)
    grad_branch = grad_middle.astype(BF16)

    branch = grad_branch.reshape(images, span, depth)
    att = jnp.einsum("cd,bld->bcl", value_out, branch, preferred_element_type=F32).astype(BF16)
    inner = jnp.sum(att.astype(F32) * pooled, 1)
    log_rows = [part[:, None] for part in split3(-log_mass)]
    inner_rows = [part[:, None] for part in split3(-inner)[:2]]
    empty = jnp.zeros((images, 1, span), BF16)
    filler = jnp.zeros((images, rows - channels - 6, span), BF16)
    att = jnp.concatenate([att, empty, *log_rows, *inner_rows, filler], axis=1)
    atts = lat_gather(att, lats)

    pooled_grad = jnp.einsum("bcl,bld->cd", pooled_low, branch, preferred_element_type=F32)
    pooled_grad = jnp.concatenate([pooled_grad, grad_gain_mlp], axis=0)
    pooled_grad = sum_everywhere(pooled_grad, imgs, lats)
    sum_mlp = pooled_grad[channels].astype(F32)
    pooled_grad = pooled_grad[:channels]
    shard_o = dot(w_value, pooled_grad, ((0,), (0,)))
    shard_v = dot(pooled_grad, w_output, ((1,), (1,)))

    grad_raw, terms = attend_back(wide, tall, raw, gain_column, queries, atts, channels, span)
    terms = [term.astype(F32) for term in lat_return(terms, lats)]
    grad_query_key = sum(terms)[:, :channels].astype(BF16)
    grad_lat_in = jnp.einsum("bcl,cd->bld", grad_query_key, query_key, preferred_element_type=F32)
    grad_lat_in = grad_lat_in.reshape(count, depth)
    grad_latents = (
        grad_middle + norm_back(grad_lat_in * gain_latent, lat_hat, lat_rstd)
    ).astype(BF16)

    latent_grad = jnp.einsum(
        "bcl,bld->cd", grad_query_key, lat_in.reshape(images, span, depth),
        preferred_element_type=F32,
    )
    latent_grad = sum_everywhere(latent_grad, imgs, lats)
    mine = lax.dynamic_slice_in_dim(latent_grad, me * share, share, 1)
    shard_q = dot(mine, key_rows, ((0,), (1,))) * scale
    shard_k = dot(latent_grad, query_columns, ((1,), (0,))) * scale
    with_key = query_key.astype(F32) * latent_grad.astype(F32)
    with_value = value_out.astype(F32) * pooled_grad.astype(F32)
    sum_lat = jnp.sum(with_key, 0) / gain_latent
    sum_pix = jnp.sum(with_key + with_value, 1) / gain_pixel
    return (
        output.reshape(images, span, depth),
        grad_latents.reshape(images, span, depth),
        jnp.swapaxes(grad_raw, 1, 2),
        shard_q,
        shard_k,
        shard_v,
        shard_o,
        shard_h,
        shard_r,
        sum_lat,
        sum_pix,
        sum_mlp,
    )


def solution(mesh):
    in_specs = (
        P("img", "lat", None),
        P("img", "lat", None),
        P("img", "lat"),
        P("img", "lat", None),
        P(),
        P(),
        P(),
        P(("img", "lat"), None),
        P(None, ("img", "lat")),
        P(None, ("img", "lat")),
        P(("img", "lat"), None),
        P(("img", "lat"), None),
        P(("img", "lat"), None),
    )
    out_specs = (
        P("img", "lat", None),
        P("img", "lat", None),
        P("img", "lat", None),
        P(("img", "lat"), None),
        P(None, ("img", "lat")),
        P(None, ("img", "lat")),
        P(("img", "lat"), None),
        P(("img", "lat"), None),
        P(("img", "lat"), None),
        P(),
        P(),
        P(),
    )
    step = partial(local, mesh.shape["img"], mesh.shape["lat"])
    return jax.shard_map(step, mesh=mesh, in_specs=in_specs, out_specs=out_specs, check_vma=False)
```

```python
from functools import partial

import jax
import jax.numpy as jnp
from jax import lax
from jax.experimental import pallas as pl
from jax.experimental.pallas import tpu as pltpu
from jax.sharding import PartitionSpec as P

F32 = jnp.float32
BF16 = jnp.bfloat16
AXES = ("img", "lat")
OUT_OF_SIGHT = -1e30
VMEM = 56 * 1024 * 1024
LESS_VMEM = 28 * 1024 * 1024


def round_up(value, unit):
    return -(-value // unit) * unit


def normalize(values):
    centered = values - jnp.mean(values, -1, keepdims=True)
    rstd = lax.rsqrt(jnp.mean(centered * centered, -1, keepdims=True) + 1e-05)
    return (centered * rstd, rstd)


def dot(left, right, contract):
    return lax.dot_general(left, right, (contract, ((), ())), preferred_element_type=F32)


def swap_lat(value, step, size):
    return lax.ppermute(value, "lat", [(i, i ^ step) for i in range(size)])


def swap_img(value, step, size):
    return lax.ppermute(value, "img", [(i, i ^ step) for i in range(size)])


def img_steps(size, turned=False):
    bits = [1 << k for k in reversed(range(size.bit_length() - 1))]
    return bits[1::-1] + bits[2:] if turned and len(bits) > 2 else bits


def img_gather(values, size):
    nearest, *others = [1 << k for k in range(size.bit_length() - 1)]
    blocks = [[value] for value in values]
    offsets = [0]
    for step in others:
        passed = offsets[1:]
        blocks = [held + [swap_img(held[0], step, size)] for held in blocks]
        offsets = offsets + [step]
        for offset in passed:
            for n, held in enumerate(blocks):
                turned = n % 2 == 1 and len(passed) == 1
                source = len(passed) + 1 if turned else offsets.index(offset)
                way = offset if turned else step
                blocks[n] = held + [swap_img(held[source], way, size)]
            offsets = offsets + [offset ^ step]
    blocks = [held + [swap_img(block, nearest, size) for block in held] for held in blocks]
    return blocks, offsets + [offset ^ nearest for offset in offsets]


def lat_gather(blocks, size):
    if blocks.ndim == 4:
        return [lax.all_to_all(blocks, "lat", 0, 0, tiled=True)]
    return [blocks] + [swap_lat(blocks, step, size) for step in range(1, size)]


def lat_return(blocks, size):
    if len(blocks) == 1:
        return [lax.all_to_all(blocks[0], "lat", 0, 0, tiled=True)]
    return [blocks[0]] + [swap_lat(blocks[step], step, size) for step in range(1, size)]


def sum_terms(terms):
    terms = [term.astype(F32) for term in terms]
    while len(terms) > 1:
        terms = [sum(terms[i : i + 2]) for i in range(0, len(terms), 2)]
    return terms[0]


def sum_img(pieces, imgs):
    pieces = lax.all_to_all(pieces, "img", 0, 0, tiled=True)
    return lax.reduce_precision(sum_terms([pieces[j] for j in range(imgs)]), 8, 7).astype(BF16)


def sum_lat_places(mine, lats):
    return sum_terms([mine] + [swap_lat(mine, step, lats) for step in range(1, lats)]).astype(BF16)


def side(pieces):
    return pieces.transpose(1, 0, 2).reshape(pieces.shape[1], -1)


def pixel_kernel(channels, raw_ref, bias_ref, gain_ref, wide_ref, tall_ref, work):
    raw = raw_ref[0].astype(F32)
    rows = work.shape[0]
    centered = raw - jnp.sum(raw, 0, keepdims=True) * (1.0 / channels)
    rstd = lax.rsqrt(jnp.sum(centered * centered, 0, keepdims=True) * (1.0 / channels) + 1e-05)
    base = channels // 8 * 8
    row = lax.broadcasted_iota(jnp.int32, (rows - base, raw.shape[1]), 0) + base
    work[base:rows] = jnp.where((row > channels) & (row < channels + 6), 1.0, 0.0).astype(F32)
    work[0:channels] = centered * rstd * gain_ref[...]
    work[channels : channels + 1] = bias_ref[0]
    whole = work[...]
    wide_ref[0] = whole[: wide_ref.shape[1]].astype(BF16)
    tall_ref[0] = whole.T.astype(BF16)


def pixel_prep(raw, bias, gain, rows):
    images, channels, pixels = raw.shape
    lanes = round_up(rows, 128)
    return pl.pallas_call(
        partial(pixel_kernel, channels),
        grid=(images,),
        in_specs=[
            pl.BlockSpec((1, channels, pixels), lambda b: (b, 0, 0)),
            pl.BlockSpec((1, 1, pixels), lambda b: (b, 0, 0)),
            pl.BlockSpec((channels, 1), lambda b: (0, 0)),
        ],
        out_specs=[
            pl.BlockSpec((1, rows, pixels), lambda b: (b, 0, 0)),
            pl.BlockSpec((1, pixels, lanes), lambda b: (b, 0, 0)),
        ],
        out_shape=[
            jax.ShapeDtypeStruct((images, rows, pixels), BF16),
            jax.ShapeDtypeStruct((images, pixels, lanes), BF16),
        ],
        scratch_shapes=[pltpu.VMEM((lanes, pixels), F32)],
        compiler_params=pltpu.CompilerParams(vmem_limit_bytes=VMEM),
        cost_estimate=pl.CostEstimate(flops=1, bytes_accessed=1, transcendentals=0),
    )(raw, bias, gain)


def split3(value):
    first = value.astype(BF16).astype(F32)
    second = (value - first).astype(BF16).astype(F32)
    return first, second, value - first - second


def whole(array):
    return pl.BlockSpec(array.shape, lambda *_: (0,) * array.ndim)


def near_by(arrays):
    return [pl.BlockSpec(memory_space=pltpu.VMEM)] * len(arrays)


def anywhere(arrays):
    return [pl.BlockSpec(memory_space=pl.ANY)] * len(arrays)


def params(limit=VMEM):
    return pltpu.CompilerParams(vmem_limit_bytes=limit)


def cost(flops, moved, exps=0):
    return pl.CostEstimate(flops=int(flops) * 4, bytes_accessed=int(moved) * 4, transcendentals=int(exps) * 4)


def attend_kernel(channels, extra, tile, turned, *refs):
    wide_ref, tall_ref, query_ref, place = refs[:4]
    blocks = query_ref.shape[0]
    order = [place[0] ^ k if turned else k for k in range(blocks)]
    out_refs, (weight, scores) = refs[4 + extra : -2], refs[-2:]
    rows = wide_ref.shape[1]
    pixels = wide_ref.shape[2]
    span = query_ref.shape[3]
    weight[:rows] = jnp.concatenate([query_ref[k, 0] for k in order], axis=1)
    weight[rows:] = jnp.zeros((weight.shape[0] - rows, weight.shape[1]), BF16)
    top = None
    for at in range(0, pixels, tile):
        part = dot(tall_ref[0, at : at + tile], weight[...], ((1,), (0,)))
        scores[at : at + tile] = part
        part_top = jnp.max(part, 0, keepdims=True)
        top = part_top if top is None else jnp.maximum(top, part_top)
    total = jnp.zeros((rows, weight.shape[1]), F32)
    for at in range(0, pixels, tile):
        expo = jnp.exp(scores[at : at + tile] - top).astype(BF16)
        total += dot(wide_ref[0, :, at : at + tile], expo, ((1,), (0,)))
    mass = total[channels + 1 : channels + 2]
    attended = message(channels, total * (1.0 / mass), split3(top + jnp.log(mass)))
    for k in range(blocks):
        part = attended[:, k * span : (k + 1) * span]
        if turned:
            out_refs[k][0] = part
        else:
            out_refs[0][k, 0] = part


def message(channels, body, lines):
    row = lax.broadcasted_iota(jnp.int32, body.shape, 0)
    body = jnp.where(row < channels, body, 0.0)
    for k, line in enumerate(lines):
        body = jnp.where(row == channels + 1 + k, line, body)
    return body.astype(BF16)


def block_specs(blocks, rows, span, turned):
    if turned:
        return [pl.BlockSpec((1, rows, span), lambda b: (b, 0, 0))] * blocks
    return [pl.BlockSpec((blocks, 1, rows, span), lambda b: (0, b, 0, 0))]


def block_shapes(blocks, images, rows, span, turned):
    if turned:
        return [jax.ShapeDtypeStruct((images, rows, span), BF16)] * blocks
    return [jax.ShapeDtypeStruct((blocks, images, rows, span), BF16)]


def attend(wide, tall, queries, place, channels, first, images, turned, after=()):
    _, rows, pixels = wide.shape
    blocks, _, _, span = queries.shape
    lanes = tall.shape[2]
    tile = min(256, pixels)
    return pl.pallas_call(
        partial(attend_kernel, channels, len(after), tile, turned),
        grid=(images,),
        in_specs=[
            pl.BlockSpec((1, rows, pixels), lambda b: (b + first, 0, 0)),
            pl.BlockSpec((1, pixels, lanes), lambda b: (b + first, 0, 0)),
            pl.BlockSpec((blocks, 1, rows, span), lambda b: (0, b + first, 0, 0)),
            pl.BlockSpec(memory_space=pltpu.SMEM),
        ]
        + anywhere(after),
        out_specs=block_specs(blocks, rows, span, turned),
        out_shape=block_shapes(blocks, images, rows, span, turned),
        scratch_shapes=[
            pltpu.VMEM((lanes, blocks * span), BF16),
            pltpu.VMEM((pixels, blocks * span), F32),
        ],
        compiler_params=params(),
        cost_estimate=cost(
            images * pixels * blocks * span * rows * 8,
            images * pixels * (rows + lanes) * 2 + images * rows * blocks * span * 4,
            images * pixels * blocks * span,
        ),
        name="attend",
    )(wide, tall, queries, place, *after)


def attend_back_kernel(channels, extra, tile, turned, *refs):
    wide_ref, tall_ref, raw_ref, gain_ref, query_ref, place = refs[:6]
    blocks = query_ref.shape[0]
    att_refs = refs[6 : 6 + blocks] if turned else refs[6:7]
    outs = refs[6 + len(att_refs) + extra :]
    grad_ref, out_refs, (query_weight, att_weight) = outs[0], outs[1:-2], outs[-2:]
    order = [place[0] ^ k if turned else k for k in range(blocks)]
    rows = wide_ref.shape[1]
    pixels = wide_ref.shape[2]
    span = query_ref.shape[3]
    width = blocks * span
    queries = jnp.concatenate([query_ref[k, 0] for k in order], axis=1)
    atts = [ref[0] for ref in att_refs] if turned else [att_refs[0][k, 0] for k in order]
    atts = jnp.concatenate(atts, axis=1)
    row = lax.broadcasted_iota(jnp.int32, (rows, width), 0)
    shifts = (row > channels) & (row < channels + 4)
    query_weight[:rows] = jnp.where(shifts, atts.astype(F32), queries.astype(F32)).astype(BF16)
    att_weight[:rows] = jnp.where(shifts, 0.0, atts.astype(F32)).astype(BF16)
    fill = jnp.zeros((query_weight.shape[0] - rows, width), BF16)
    query_weight[rows:] = fill
    att_weight[rows:] = fill
    total = jnp.zeros((rows, width), F32)
    for at in range(0, pixels, tile):
        tall = tall_ref[0, at : at + tile]
        probs = jnp.exp(dot(tall, query_weight[...], ((1,), (0,))))
        grad = probs * dot(tall, att_weight[...], ((1,), (0,)))
        grad_low = grad.astype(BF16)
        probs_low = probs.astype(BF16)
        total += dot(wide_ref[0, :, at : at + tile], grad_low, ((1,), (0,)))
        into = dot(query_weight[:rows], grad_low, ((1,), (1,)))
        into += dot(att_weight[:rows], probs_low, ((1,), (1,)))
        raw = raw_ref[0, :, at : at + tile].astype(F32)
        centered = raw - jnp.sum(raw, 0, keepdims=True) * (1.0 / channels)
        rstd = lax.rsqrt(
            jnp.sum(centered * centered, 0, keepdims=True) * (1.0 / channels) + 1e-05
        )
        hat = centered * rstd
        upstream = into[:channels] * gain_ref[...]
        mean = jnp.sum(upstream, 0, keepdims=True) * (1.0 / channels)
        along = jnp.sum(upstream * hat, 0, keepdims=True) * (1.0 / channels)
        grad_ref[0, :, at : at + tile] = (rstd * (upstream - mean - hat * along)).astype(BF16)
    total = total.astype(BF16)
    for k in range(blocks):
        term = total[:, k * span : (k + 1) * span]
        if turned:
            out_refs[k][0] = term
        else:
            out_refs[0][k, 0] = term


def attend_back(wide, tall, raw, gain, queries, atts, place, channels, first, grad, turned, after=()):
    all_images, rows, pixels = wide.shape
    blocks, _, _, span = queries.shape
    images = atts[0].shape[0 if turned else 1]
    lanes = tall.shape[2]
    tile = min(256, pixels)
    part = pl.BlockSpec((1, channels, pixels), lambda b: (b + first, 0, 0))
    earlier = [] if grad is None else [grad]
    extra = [*earlier, *after]
    results = pl.pallas_call(
        partial(attend_back_kernel, channels, len(extra), tile, turned),
        grid=(images,),
        in_specs=[
            pl.BlockSpec((1, rows, pixels), lambda b: (b + first, 0, 0)),
            pl.BlockSpec((1, pixels, lanes), lambda b: (b + first, 0, 0)),
            part,
            whole(gain),
        ]
        + [
            pl.BlockSpec((blocks, 1, rows, span), lambda b: (0, b + first, 0, 0)),
            pl.BlockSpec(memory_space=pltpu.SMEM),
        ]
        + block_specs(blocks, rows, span, turned)
        + anywhere(extra),
        out_specs=[part] + block_specs(blocks, rows, span, turned),
        out_shape=[jax.ShapeDtypeStruct((all_images, channels, pixels), BF16)]
        + block_shapes(blocks, images, rows, span, turned),
        scratch_shapes=[
            pltpu.VMEM((lanes, blocks * span), BF16),
            pltpu.VMEM((lanes, blocks * span), BF16),
        ],
        compiler_params=params(),
        cost_estimate=cost(
            images * pixels * blocks * span * rows * 16,
            images * pixels * (rows * 3 + lanes) * 2 + images * rows * blocks * span * 6,
            images * pixels * blocks * span,
        ),
        input_output_aliases={6 + len(atts): 0} if earlier else {},
        name="attend_back",
    )(wide, tall, raw, gain, queries, place, *atts, *extra)
    return results[0], results[1:]


def merged(channels, parts):
    parts = [part.astype(F32) for part in parts]
    at = channels + 1
    logs = [part[at : at + 1] + part[at + 1 : at + 2] + part[at + 2 : at + 3] for part in parts]
    top = logs[0]
    for log in logs[1:]:
        top = jnp.maximum(top, log)
    shares = [jnp.exp(log - top) for log in logs]
    mass = shares[0]
    for share in shares[1:]:
        mass = mass + share
    pooled = parts[0] * (shares[0] / mass)
    for part, share in zip(parts[1:], shares[1:]):
        pooled = pooled + part * (share / mass)
    return pooled, top + jnp.log(mass)


def rows_norm(values):
    depth = values.shape[1]
    centered = values - jnp.sum(values, 1, keepdims=True) * (1.0 / depth)
    rstd = lax.rsqrt(jnp.sum(centered * centered, 1, keepdims=True) * (1.0 / depth) + 1e-05)
    return centered * rstd, rstd


def rows_norm_back(upstream, hat, rstd):
    depth = hat.shape[1]
    mean = jnp.sum(upstream, 1, keepdims=True) * (1.0 / depth)
    along = jnp.sum(upstream * hat, 1, keepdims=True) * (1.0 / depth)
    return rstd * (upstream - mean - hat * along)


def terms_of(refs, k):
    if len(refs) > 1:
        return [ref[k] for ref in refs]
    return [refs[0][j, k] for j in range(refs[0].shape[0])]


def middle_kernel(channels, count, extra, *refs):
    parts, refs = refs[:count], refs[count:]
    (latents, cot, grad_act, value_out, hidden, gain) = refs[:6]
    (note, pooled_ref, act_ref, into_ref, pre_ref, middle_ref, branch_ref, gain_ref) = refs[
        6 + extra :
    ]
    images, rows, span = parts[0].shape[-3:]
    kept, flipped = [], []
    row = lax.broadcasted_iota(jnp.int32, (rows, span), 0)
    for k in range(images):
        pooled, logs = merged(channels, terms_of(parts, k))
        pooled = jnp.where(row < channels, pooled, 0.0)
        low = pooled.astype(BF16)
        pooled_ref[k] = low
        kept.append((pooled, logs))
        flipped.append(low.T)
    middle = latents[...].astype(F32) + dot(
        jnp.concatenate(flipped, axis=0), value_out[...], ((1,), (0,))
    )
    middle_ref[...] = middle
    hat, rstd = rows_norm(middle)
    into = (hat * gain[...]).astype(BF16)
    into_ref[...] = into
    pre = dot(into, hidden[...], ((1,), (0,)))
    below = 0.5 + 0.5 * lax.erf(pre * (0.5**0.5))
    act_ref[...] = (pre * below).astype(BF16)
    slope = below + pre * (jnp.exp(-0.5 * pre * pre) * (2.0 * jnp.pi) ** -0.5)
    grad_pre = (grad_act[...] * slope).astype(BF16)
    pre_ref[...] = grad_pre
    grad_into = dot(grad_pre, hidden[...], ((1,), (1,)))
    gain_ref[...] = jnp.sum(grad_into * hat, 0, keepdims=True)
    grad = cot[...].astype(F32) + rows_norm_back(grad_into * gain[...], hat, rstd)
    branch = grad.astype(BF16)
    branch_ref[...] = branch
    att = dot(value_out[...], branch, ((1,), (1,)))
    for k in range(images):
        pooled, logs = kept[k]
        mine = att[:, k * span : (k + 1) * span]
        inner = jnp.sum(mine.astype(BF16).astype(F32) * pooled, 0, keepdims=True)
        line = message(channels, mine, (*split3(-logs), *split3(-inner)[:2]))
        if len(note.shape) == 3:
            note[k] = line
        else:
            for j in range(note.shape[0]):
                note[j, k] = line


def middle_part(parts, latents, cot, grad_act, value_out, hidden, gain, channels, at, after=()):
    images, rows, span = parts[0].shape[-3:]
    depth = latents.shape[1]
    high = images * span
    own = pl.BlockSpec((high, depth), lambda i: (at, 0))
    shape = jax.ShapeDtypeStruct
    arrays = [*parts, latents, cot, grad_act, value_out, hidden, gain]
    outs = [
        shape(parts[0].shape, BF16),
        shape((images, rows, span), BF16),
        shape((high, depth), BF16),
        shape((high, depth), BF16),
        shape((high, depth), BF16),
        shape((high, depth), F32),
        shape((high, depth), BF16),
        shape((1, depth), F32),
    ]
    return pl.pallas_call(
        partial(middle_kernel, channels, len(parts), len(after)),
        grid=(1,),
        in_specs=[whole(part) for part in parts]
        + [own, own, own, whole(value_out), whole(hidden), whole(gain)]
        + anywhere(after),
        out_specs=[whole(out) for out in outs],
        out_shape=outs,
        compiler_params=params(),
        cost_estimate=cost(
            high * depth * (depth + rows) * 8, high * depth * 24 + depth * depth * 4, high * depth * 2
        ),
        name="middle_part",
    )(*arrays, *after)


def finish_kernel(channels, count, extra, last, *refs):
    parts, refs = refs[:count], refs[count:]
    lat_in, latents, branch, query_key, gain = refs[:5]
    out_ref, sum_ref = refs[-2:]
    images, rows, span = parts[0].shape[-3:]
    wide, tall = [], []
    row = lax.broadcasted_iota(jnp.int32, (rows, span), 0)
    for k in range(images):
        first, *others = terms_of(parts, k)
        term = first.astype(F32)
        for other in others:
            term = term + other.astype(F32)
        term = jnp.where(row < channels, term, 0.0).astype(BF16)
        wide.append(term)
        tall.append(term.T)
    total = dot(jnp.concatenate(wide, axis=1), lat_in[...], ((1,), (0,)))
    if extra:
        total = total + refs[5][...]
    if last:
        width = sum_ref.shape[2]
        low = total.astype(BF16)
        for k in range(sum_ref.shape[0]):
            sum_ref[k] = low[:, k * width : (k + 1) * width]
    else:
        sum_ref[...] = total
    grad_in = dot(jnp.concatenate(tall, axis=0), query_key[...], ((1,), (0,)))
    hat, rstd = rows_norm(latents[...].astype(F32))
    back = rows_norm_back(grad_in * gain[...], hat, rstd)
    out_ref[...] = (branch[...].astype(F32) + back).astype(BF16)


def finish(
    parts, lat_in, latents, branch, query_key, gain, channels, at, earlier, pieces, after=()
):
    images, rows, span = parts[0].shape[-3:]
    depth = latents.shape[1]
    high = images * span
    own = pl.BlockSpec((high, depth), lambda i: (at, 0))
    if pieces:
        total = jax.ShapeDtypeStruct((pieces, rows, depth // pieces), BF16)
    else:
        total = jax.ShapeDtypeStruct((rows, depth), F32)
    arrays = [*parts, lat_in, latents, branch, query_key, gain]
    before = [] if earlier is None else [earlier]
    return pl.pallas_call(
        partial(finish_kernel, channels, len(parts), len(before), bool(pieces)),
        grid=(1,),
        in_specs=[whole(part) for part in parts]
        + [own, own, whole(branch), whole(query_key), whole(gain)]
        + [whole(array) for array in before]
        + anywhere(after),
        out_specs=[pl.BlockSpec((high, depth), lambda i: (0, 0)), whole(total)],
        out_shape=[jax.ShapeDtypeStruct((high, depth), BF16), total],
        compiler_params=params(),
        cost_estimate=cost(high * depth * rows * 4, high * depth * 8 + depth * rows * 8),
        name="finish",
    )(*arrays, *before, *after)


def pack_kernel(counts, *refs):
    ins, outs = refs[: -len(counts)], list(refs[-len(counts) :])
    at = 0
    for out, count in zip(outs, counts):
        column = 0
        for ref in ins[at : at + count]:
            width = round_up(ref.shape[1], 128)
            if width > ref.shape[1]:
                out[:, column : column + width] = jnp.zeros((out.shape[0], width), BF16)
            out[:, column : column + ref.shape[1]] = ref[...]
            column += width
        at += count


def pack(*groups):
    arrays = [array for group in groups for array in group]
    shapes = [
        jax.ShapeDtypeStruct(
            (group[0].shape[0], sum(round_up(array.shape[1], 128) for array in group)), BF16
        )
        for group in groups
    ]
    return pl.pallas_call(
        partial(pack_kernel, [len(group) for group in groups]),
        out_shape=shapes,
        compiler_params=params(),
        name="pack",
    )(*arrays)


def weights_kernel(channels, groups, counts, orders, *refs):
    pooled, branch, gains, act, into, pre = (
        refs[k * groups : (k + 1) * groups] for k in range(6)
    )
    cot, place = refs[6 * groups : 6 * groups + 2]
    kept, sent, first, second, third = refs[-5:]
    high = act[0].shape[0]
    sums = [None] * 4
    for k in range(groups):
        wide = jnp.concatenate([pooled[k][j] for j in range(pooled[k].shape[0])], axis=1)
        own = cot[k * high : (k + 1) * high]
        terms = (
            dot(into[k][...], pre[k][...], ((0,), (0,))),
            dot(act[k][...], own, ((0,), (0,))),
            dot(wide, branch[k][...], ((1,), (0,))),
            gains[k][...],
        )
        sums = [term if total is None else total + term for total, term in zip(sums, terms)]
    row = lax.broadcasted_iota(jnp.int32, sums[2].shape, 0)
    first[...] = sums[0].astype(BF16)
    second[...] = sums[1].astype(BF16)
    rows = sums[2].shape[0]
    third[:rows] = jnp.where(row == channels, sums[3], sums[2]).astype(BF16)
    third[rows:] = jnp.zeros((third.shape[0] - rows, third.shape[1]), BF16)
    imgs, lats, share, part = counts
    turned = pl.program_id(0)
    for spot in range(imgs):
        differs = [
            sum(order[k] for k in range(len(order)) if spot & (imgs >> (k + 1))) for order in orders
        ]
        i = place[0] ^ (differs[0] + turned * (differs[1] - differs[0]))
        out, at = (kept, spot) if spot < imgs // 2 else (sent, spot - imgs // 2)
        for j in range(lats):
            lines = pl.ds(pl.multiple_of((i * lats + j) * share, share), share)
            out[at, 0, 2 * j * share : (2 * j + 1) * share] = first[lines]
            out[at, 0, (2 * j + 1) * share : (2 * j + 2) * share] = second[lines]
        out[at, 0, 2 * lats * share :] = third[pl.ds(pl.multiple_of(i * part, part), part)]


def weights_part(pooled, branch, gains, act, into, pre, cot, place, channels, counts, after):
    imgs, lats, share, part = counts
    depth = cot.shape[1]
    whole_rows = 2 * lats * share + part
    orders = [img_steps(imgs, turned)[::-1] for turned in (False, True)]
    out = jax.ShapeDtypeStruct((imgs // 2, 2, whole_rows, depth // 2), BF16)
    block = pl.BlockSpec((imgs // 2, 1, whole_rows, depth // 2), lambda n: (0, n, 0, 0))

    def half(array):
        return pl.BlockSpec((array.shape[0], depth // 2), lambda n: (0, n))

    return pl.pallas_call(
        partial(weights_kernel, channels, len(pooled), counts, orders),
        grid=(2,),
        in_specs=[whole(array) for array in pooled]
        + [half(array) for array in (*branch, *gains)]
        + [whole(array) for array in (*act, *into)]
        + [half(array) for array in (*pre, cot)]
        + [pl.BlockSpec(memory_space=pltpu.SMEM)]
        + anywhere(after),
        out_specs=[block, block],
        out_shape=[out, out],
        scratch_shapes=[
            pltpu.VMEM((depth, depth // 2), BF16),
            pltpu.VMEM((depth, depth // 2), BF16),
            pltpu.VMEM((imgs * part, depth // 2), BF16),
        ],
        compiler_params=params(),
        cost_estimate=cost(cot.shape[0] * depth * depth * 5, cot.shape[0] * depth * 14),
        name="weights_part",
    )(*pooled, *branch, *gains, *act, *into, *pre, cot, place, *after)


def order_kernel(blocks, widths, tails, extra, *refs):
    place = refs[blocks + len(tails)]
    rows = refs[0].shape[0]
    outs = refs[blocks + len(tails) + 1 + extra :]
    for k in range(blocks):
        lines = pl.ds(pl.multiple_of((place[0] ^ k) * rows, rows), rows)
        at = 0
        for out, width in zip(outs, widths):
            out[lines, :width] = refs[k][:, at : at + width]
            at += width
    for n, at in enumerate(tails):
        outs[at][:, widths[at] :] = refs[blocks + n][...]


def order_rows(blocks, place, widths, after=(), tails=None):
    rows, columns = blocks[0].shape
    tails = tails or {}
    outs = [
        jax.ShapeDtypeStruct(
            (len(blocks) * rows, width + (tails[k].shape[1] if k in tails else 0)), BF16
        )
        for k, width in enumerate(widths)
    ]
    return pl.pallas_call(
        partial(order_kernel, len(blocks), widths, list(tails), len(after)),
        grid=(1,),
        in_specs=[whole(block) for block in (*blocks, *tails.values())]
        + [pl.BlockSpec(memory_space=pltpu.SMEM)]
        + anywhere(after),
        out_specs=[whole(out) for out in outs],
        out_shape=outs,
        compiler_params=params(),
        cost_estimate=cost(1, len(blocks) * rows * columns * 4),
        name="order_rows",
    )(*blocks, *tails.values(), place, *after)


def add_kernel(groups, extra, *refs):
    for k in range(groups):
        own, got = refs[2 * k], refs[2 * k + 1]
        kept, sent = refs[2 * groups + extra + 2 * k : 2 * groups + extra + 2 * k + 2]
        total = (own[...].astype(F32) + got[...].astype(F32)).astype(BF16)
        half = total.shape[0] // 2
        kept[...] = total[:half].reshape(kept.shape)
        sent[...] = total[half:].reshape(sent.shape)


def add_blocks(groups, after):
    arrays, specs, outs = [], [], []
    for array, at, got in groups:
        if at is None:
            specs += [whole(array), whole(got)]
            shape = (array.shape[0] // 2, *array.shape[1:])
        else:
            block = (got.shape[0], 1, *got.shape[2:])
            specs += [pl.BlockSpec(block, lambda i, at=at: (0, at, 0, 0))] * 2
            shape = (got.shape[0] // 2, *got.shape[2:])
        arrays += [array, got]
        outs += [jax.ShapeDtypeStruct(shape, BF16)] * 2
    return pl.pallas_call(
        partial(add_kernel, len(groups), len(after)),
        grid=(1,),
        in_specs=specs + anywhere(after),
        out_specs=[whole(out) for out in outs],
        out_shape=outs,
        compiler_params=params(),
        cost_estimate=cost(1, sum(got.size for _, _, got in groups) * 6),
        name="add_blocks",
    )(*arrays, *after)


def last_blocks(firsts, gots, place, lats, share, after):
    _, rows, width = firsts[0].shape
    base = 2 * lats * share
    outs = [
        jax.ShapeDtypeStruct((lats, 2 * share, 2 * width), BF16),
        jax.ShapeDtypeStruct((rows - base, 2 * width), BF16),
    ]
    arrays = [*firsts, *gots]

    def kernel(*refs):
        spots, common = refs[-2:]
        for n in range(2):
            total = (refs[n][0].astype(F32) + refs[2 + n][0].astype(F32)).astype(BF16)
            lanes = slice(n * width, (n + 1) * width)
            for j in range(lats):
                spots[refs[4][0] ^ j, :, lanes] = total[2 * j * share : (2 * j + 2) * share]
            common[:, lanes] = total[base:]

    return pl.pallas_call(
        kernel,
        grid=(1,),
        in_specs=[whole(array) for array in arrays]
        + [pl.BlockSpec(memory_space=pltpu.SMEM)]
        + anywhere(after),
        out_specs=[whole(out) for out in outs],
        out_shape=outs,
        compiler_params=params(),
        cost_estimate=cost(1, rows * width * 12),
        name="last_blocks",
    )(*arrays, place, *after)


def early_kernel(depth, rows, offsets, *refs):
    count = len(offsets)
    place, cot = refs[:2]
    firsts, seconds = refs[2 : 2 + count], refs[2 + count : 2 + 2 * count]
    hidden, back, queries, grad_act, value_out, back_rows, values, outputs = refs[-8:]
    high, width = firsts[0].shape
    wide_rows = width - 2 * depth
    for first, second, offset in zip(firsts, seconds, offsets):
        lines = pl.ds(pl.multiple_of((place[0] ^ offset) * high, high), high)
        hidden[lines] = first[:, :depth]
        values[lines] = first[:, depth : depth + rows]
        queries[lines] = first[:, depth + wide_rows :]
        back_rows[lines] = second[:, :depth]
        outputs[lines] = second[:, depth:]
    back[...] = back_rows[...]
    grad_act[...] = dot(cot[...], back_rows[...], ((1,), (1,)))
    value_out[...] = dot(values[...], outputs[...], ((0,), (0,))).astype(BF16)


def early_part(place, cot, firsts, seconds, offsets, depth, rows, after):
    high = cot.shape[0]
    shape = jax.ShapeDtypeStruct
    arrays = [cot, *firsts, *seconds]
    outs = [shape((depth, depth), BF16)] * 3 + [shape((high, depth), F32), shape((rows, depth), BF16)]
    return pl.pallas_call(
        partial(early_kernel, depth, rows, offsets),
        grid=(1,),
        in_specs=[pl.BlockSpec(memory_space=pltpu.SMEM)]
        + [whole(array) for array in arrays]
        + anywhere(after),
        out_specs=[whole(out) for out in outs],
        out_shape=outs,
        scratch_shapes=[
            pltpu.VMEM((depth, depth), BF16),
            pltpu.VMEM((depth, rows), BF16),
            pltpu.VMEM((depth, depth), BF16),
        ],
        compiler_params=params(),
        cost_estimate=cost(0, 0),
        name="early_part",
    )(place, *arrays, *after)


def out_kernel(groups, extra, *refs):
    back, out = refs[2 * groups], refs[-1]
    half = pl.program_id(0)
    for k in range(groups):

        @pl.when(half == k)
        def _():
            total = refs[groups + k][...] + dot(refs[k][...], back[...], ((1,), (0,)))
            out[...] = total.astype(BF16)


def out_part(act, middle, back, after):
    high, depth = act[0].shape
    groups = len(act)
    return pl.pallas_call(
        partial(out_kernel, groups, len(after)),
        grid=(groups,),
        in_specs=[whole(array) for array in (*act, *middle, back)] + anywhere(after),
        out_specs=pl.BlockSpec((high, depth), lambda i: (i, 0)),
        out_shape=jax.ShapeDtypeStruct((groups * high, depth), BF16),
        compiler_params=params(),
        cost_estimate=cost(groups * high * depth * depth * 2, groups * high * depth * 8),
        name="out_part",
    )(*act, *middle, back, *after)


def relay_kernel(*refs):
    pass


def relay(values, after):
    values, after = list(values), list(after)
    return pl.pallas_call(
        relay_kernel,
        in_specs=anywhere(values) + anywhere(after),
        out_specs=anywhere(values),
        out_shape=[jax.ShapeDtypeStruct(value.shape, value.dtype) for value in values],
        input_output_aliases={k: k for k in range(len(values))},
        name="relay",
    )(*values, *after)


def local(
    imgs,
    lats,
    latents,
    pixels,
    keep_mask,
    cotangent,
    gain_latent,
    gain_pixel,
    gain_mlp,
    w_query,
    w_key,
    w_value,
    w_output,
    w_hidden,
    w_return,
):
    images, span, depth = latents.shape
    channels = pixels.shape[2]
    devices = imgs * lats
    share = depth // devices
    rows = round_up(channels + 6, 16)
    scale = depth ** (-0.5)
    me = lax.axis_index("img") * lats + lax.axis_index("lat")

    raw = jnp.swapaxes(pixels, 1, 2)
    bias = jnp.where(keep_mask > 0, 0.0, OUT_OF_SIGHT).astype(F32)[:, None, :]
    gain_column = gain_pixel[:, None]

    place = lax.axis_index("lat")[None]

    near, later = pack((w_query, w_key.T), (w_hidden, w_value.T, w_return, w_output))
    plain = share % 16 != 0
    if plain:
        near = lax.all_gather(near, "lat", axis=0, tiled=True)
        near_query, near_key = near[:, :depth], near[:, depth : depth + rows]
    else:
        near = [near] + [swap_lat(near, step, lats) for step in range(1, lats)]
        (later,) = relay([later], near[1:2])
        later = [later] + [swap_lat(later, step, lats) for step in range(1, lats)]
        near_query, near_key = order_rows(near, place, (depth, rows))
    key_rows = lax.all_gather(near_key, "img", axis=0, tiled=True)
    query_key = (dot(key_rows, near_query, ((0,), (1,))) * scale).astype(BF16)
    query_key = side(lax.all_gather(query_key, "img", axis=0, tiled=False))

    groups = 2 if images % 2 == 0 else 1
    size = images // groups
    flat = latents.reshape(images * span, depth)
    cot = cotangent.reshape(images * span, depth)
    gain_lat, gain_mid = gain_latent[None], gain_mlp[None]
    lat_in = (normalize(flat.astype(F32))[0] * gain_lat).astype(BF16)
    lat_blocks = lat_in.reshape(images, span, depth)
    row = lax.broadcasted_iota(jnp.int32, (1, rows, 1), 1)
    early_blocks = lat_blocks if plain else relay([lat_blocks], later[1:])[0]
    query = jnp.einsum("cd,bld->bcl", query_key, early_blocks, preferred_element_type=F32)
    query = jnp.where(row == channels, 1.0, query).astype(BF16)
    (queries,) = lat_gather(jnp.broadcast_to(query[None], (lats, *query.shape)), lats)
    (late_bias,) = relay([bias], [query])
    wide, tall = pixel_prep(raw, late_bias, gain_column, rows)

    wide_rows = round_up(rows, 128)
    img_place = lax.axis_index("img")[None]
    if not plain:
        first, second = order_rows(
            later, place, (depth + wide_rows, 2 * depth), [query], {0: near_query}
        )
        (first, second), offsets = img_gather([first, second], imgs)
    turned = [k % 2 == 0 for k in range(groups)]
    attended, parts = [], None
    for k in range(groups):
        after = [] if parts is None else parts[:1]
        parts = attend(wide, tall, queries, place, channels, k * size, size, turned[k], after)
        attended.append(lat_return(parts, lats))
    if plain:
        later = lax.all_gather(later, AXES, axis=0, tiled=True)
        query_rows = lax.all_gather(w_query, AXES, axis=0, tiled=True)
        hidden, back = later[:, :depth], later[:, depth + wide_rows : 2 * depth + wide_rows]
        grad_act = dot(cot, back, ((1,), (1,)))
        value_out = dot(
            later[:, depth : depth + rows], later[:, 2 * depth + wide_rows :], ((0,), (0,))
        ).astype(BF16)
    else:
        hidden, back, query_rows, grad_act, value_out = early_part(
            img_place, cot, first, second, offsets, depth, rows, parts[:1]
        )

    lines = [slice(k * size * span, (k + 1) * size * span) for k in range(groups)]
    middles, atts = [], []
    for k in range(groups):
        middles.append(
            middle_part(
                attended[k],
                flat,
                cot,
                grad_act,
                value_out,
                hidden,
                gain_mid,
                channels,
                k,
            )
        )
        atts.append(lat_gather(middles[k][0], lats))
    _, pooled, act, mlp_in, grad_pre, middle, branch, gain_grad = (
        [part[j] for part in middles] for j in range(8)
    )
    pin = []
    if not plain:
        part = round_up(-(-rows // imgs), 16)
        counts = (imgs, lats, share, part)
        orders = [img_steps(imgs, turned)[::-1] for turned in (False, True)]
        kept, sent = weights_part(
            pooled,
            branch,
            gain_grad,
            act,
            mlp_in,
            grad_pre,
            cot,
            img_place,
            channels,
            counts,
            [],
        )
        got = swap_img(sent, orders[0][0], imgs)
        pin = [sent]
    grad_raw, ends = None, []
    for k in range(groups):
        grad_raw, parts = attend_back(
            wide,
            tall,
            raw,
            gain_column,
            queries,
            atts[k],
            place,
            channels,
            k * size,
            grad_raw,
            turned[k],
            pin,
        )
        ends.append(lat_return(parts, lats))
        if k == 0 and not plain:
            split = add_blocks([(kept, n, got) for n in range(2)], parts[:1])
            kept, sent = split[0::2], split[1::2]
            pin = sent[:1]
    if not plain:
        for bit in range(1, len(orders[0]) - 1):
            gots = [swap_img(sent[n], orders[n][bit], imgs) for n in range(2)]
            split = add_blocks([(kept[n], None, gots[n]) for n in range(2)], parts[:1])
            kept, sent = split[0::2], split[1::2]

    grad_latents, latent_grad = [], None
    for k in range(groups):
        done, latent_grad = finish(
            ends[k],
            lat_in,
            flat,
            branch[k],
            query_key,
            gain_lat,
            channels,
            k,
            latent_grad,
            imgs if k == groups - 1 else 0,
            pin if plain else sent[:1],
        )
        grad_latents.append(done)
        if k == 0:
            output = out_part(act, middle, back, [done])
    if not plain:
        gots = [swap_img(sent[n], orders[n][-1], imgs) for n in range(2)]

    pieces = latent_grad
    latent_grad = sum_img(pieces, imgs)
    latent_terms = [latent_grad] + [swap_lat(latent_grad, step, lats) for step in range(1, lats)]
    latent_grad = sum_terms(latent_terms).astype(BF16)
    if plain:
        both = jnp.stack(
            [
                sum(dot(mlp_in[k], grad_pre[k], ((0,), (0,))) for k in range(groups)),
                sum(dot(act[k], cot[lines[k]], ((0,), (0,))) for k in range(groups)),
            ]
        ).astype(BF16)
        sums = lax.psum_scatter(both, AXES, scatter_dimension=1, tiled=True).astype(F32)
        shard_h, shard_r = sums[0], sums[1]
        common = sum(
            jnp.einsum(
                "bcl,bld->cd",
                pooled[k],
                branch[k].reshape(size, span, depth),
                preferred_element_type=F32,
            )
            for k in range(groups)
        )
        line = lax.broadcasted_iota(jnp.int32, (rows, 1), 0)
        common = jnp.where(line == channels, sum(gain_grad), common)
        pooled_grad = lax.psum(common, AXES).astype(BF16)
    else:
        blocks, common = last_blocks(kept, gots, place, lats, share, [pieces])
        sent = [common] * (lats - 1) + [blocks[step] for step in range(1, lats)]
        came = [swap_lat(block, 1 + k % (lats - 1), lats) for k, block in enumerate(sent)]
        came = list(relay(came, latent_terms[1:2]))
        common = sum_terms([common] + came[: lats - 1]).astype(BF16)
        sums = sum_terms([blocks[0]] + came[lats - 1 :])
        shard_h, shard_r = sums[:share], sums[share:]
        pooled_grad = lax.all_gather(common, "img", axis=0, tiled=True)
    sum_mlp = pooled_grad[channels].astype(F32)
    pooled_grad = pooled_grad[:channels]
    shard_o = dot(w_value, pooled_grad, ((0,), (0,)))
    shard_v = dot(pooled_grad, w_output, ((1,), (1,)))
    latent_grad = side(lax.all_gather(latent_grad, "img", axis=0, tiled=False))[:channels]
    mine = lax.dynamic_slice_in_dim(latent_grad, me * share, share, 1)
    shard_q = dot(mine, key_rows[:, :channels], ((0,), (1,))) * scale
    columns = lax.dynamic_slice_in_dim(query_rows, me * share, share, 1)
    shard_k = dot(latent_grad, columns, ((1,), (0,))) * scale
    with_key = query_key[:channels].astype(F32) * latent_grad.astype(F32)
    with_value = value_out[:channels].astype(F32) * pooled_grad.astype(F32)
    sum_lat = jnp.sum(with_key, 0) / gain_latent
    sum_pix = jnp.sum(with_key + with_value, 1) / gain_pixel
    return (
        output.reshape(images, span, depth),
        jnp.concatenate(grad_latents).reshape(images, span, depth),
        jnp.swapaxes(grad_raw, 1, 2),
        shard_q,
        shard_k,
        shard_v,
        shard_o,
        shard_h,
        shard_r,
        sum_lat,
        sum_pix,
        sum_mlp,
    )


def solution(mesh):
    in_specs = (
        P("img", "lat", None),
        P("img", "lat", None),
        P("img", "lat"),
        P("img", "lat", None),
        P(),
        P(),
        P(),
        P(("img", "lat"), None),
        P(None, ("img", "lat")),
        P(None, ("img", "lat")),
        P(("img", "lat"), None),
        P(("img", "lat"), None),
        P(("img", "lat"), None),
    )
    out_specs = (
        P("img", "lat", None),
        P("img", "lat", None),
        P("img", "lat", None),
        P(("img", "lat"), None),
        P(None, ("img", "lat")),
        P(None, ("img", "lat")),
        P(("img", "lat"), None),
        P(("img", "lat"), None),
        P(("img", "lat"), None),
        P(),
        P(),
        P(),
    )
    step = partial(local, mesh.shape["img"], mesh.shape["lat"])
    return jax.shard_map(step, mesh=mesh, in_specs=in_specs, out_specs=out_specs, check_vma=False)
```

```python
from functools import partial

import jax
import jax.numpy as jnp
from jax import lax
from jax.experimental import pallas as pl
from jax.experimental.pallas import tpu as pltpu
from jax.sharding import PartitionSpec as P

F32 = jnp.float32
BF16 = jnp.bfloat16
AXES = ("img", "lat")
OUT_OF_SIGHT = -1e30
VMEM = 56 * 1024 * 1024
LESS_VMEM = 28 * 1024 * 1024


def round_up(value, unit):
    return -(-value // unit) * unit


def normalize(values):
    centered = values - jnp.mean(values, -1, keepdims=True)
    rstd = lax.rsqrt(jnp.mean(centered * centered, -1, keepdims=True) + 1e-05)
    return (centered * rstd, rstd)


def dot(left, right, contract):
    return lax.dot_general(left, right, (contract, ((), ())), preferred_element_type=F32)


def swap_lat(value, step, size):
    return lax.ppermute(value, "lat", [(i, i ^ step) for i in range(size)])


def swap_img(value, step, size):
    return lax.ppermute(value, "img", [(i, i ^ step) for i in range(size)])


def img_steps(size, turned=False):
    bits = [1 << k for k in reversed(range(size.bit_length() - 1))]
    return bits[1::-1] + bits[2:] if turned and len(bits) > 2 else bits


def img_gather(values, size):
    nearest, *others = [1 << k for k in range(size.bit_length() - 1)]
    blocks = [[value] for value in values]
    offsets = [0]
    for step in others:
        passed = offsets[1:]
        blocks = [held + [swap_img(held[0], step, size)] for held in blocks]
        offsets = offsets + [step]
        for offset in passed:
            for n, held in enumerate(blocks):
                turned = n % 2 == 1 and len(passed) == 1
                source = len(passed) + 1 if turned else offsets.index(offset)
                way = offset if turned else step
                blocks[n] = held + [swap_img(held[source], way, size)]
            offsets = offsets + [offset ^ step]
    blocks = [held + [swap_img(block, nearest, size) for block in held] for held in blocks]
    return blocks, offsets + [offset ^ nearest for offset in offsets]


def lat_gather(blocks, size):
    if blocks.ndim == 4:
        return [lax.all_to_all(blocks, "lat", 0, 0, tiled=True)]
    return [blocks] + [swap_lat(blocks, step, size) for step in range(1, size)]


def lat_return(blocks, size):
    if len(blocks) == 1:
        return [lax.all_to_all(blocks[0], "lat", 0, 0, tiled=True)]
    return [blocks[0]] + [swap_lat(blocks[step], step, size) for step in range(1, size)]


def sum_terms(terms):
    terms = [term.astype(F32) for term in terms]
    while len(terms) > 1:
        terms = [sum(terms[i : i + 2]) for i in range(0, len(terms), 2)]
    return terms[0]


def sum_img(pieces, imgs):
    pieces = lax.all_to_all(pieces, "img", 0, 0, tiled=True)
    return lax.reduce_precision(sum_terms([pieces[j] for j in range(imgs)]), 8, 7).astype(BF16)


def sum_lat_places(mine, lats):
    return sum_terms([mine] + [swap_lat(mine, step, lats) for step in range(1, lats)]).astype(BF16)


def side(pieces):
    return pieces.transpose(1, 0, 2).reshape(pieces.shape[1], -1)


def pixel_kernel(channels, raw_ref, bias_ref, gain_ref, wide_ref, tall_ref, work):
    raw = raw_ref[0].astype(F32)
    rows = work.shape[0]
    centered = raw - jnp.sum(raw, 0, keepdims=True) * (1.0 / channels)
    rstd = lax.rsqrt(jnp.sum(centered * centered, 0, keepdims=True) * (1.0 / channels) + 1e-05)
    base = channels // 8 * 8
    row = lax.broadcasted_iota(jnp.int32, (rows - base, raw.shape[1]), 0) + base
    work[base:rows] = jnp.where((row > channels) & (row < channels + 6), 1.0, 0.0).astype(F32)
    work[0:channels] = centered * rstd * gain_ref[...]
    work[channels : channels + 1] = bias_ref[0]
    whole = work[...]
    wide_ref[0] = whole[: wide_ref.shape[1]].astype(BF16)
    tall_ref[0] = whole.T.astype(BF16)


def pixel_prep(raw, bias, gain, rows):
    images, channels, pixels = raw.shape
    lanes = round_up(rows, 128)
    return pl.pallas_call(
        partial(pixel_kernel, channels),
        grid=(images,),
        in_specs=[
            pl.BlockSpec((1, channels, pixels), lambda b: (b, 0, 0)),
            pl.BlockSpec((1, 1, pixels), lambda b: (b, 0, 0)),
            pl.BlockSpec((channels, 1), lambda b: (0, 0)),
        ],
        out_specs=[
            pl.BlockSpec((1, rows, pixels), lambda b: (b, 0, 0)),
            pl.BlockSpec((1, pixels, lanes), lambda b: (b, 0, 0)),
        ],
        out_shape=[
            jax.ShapeDtypeStruct((images, rows, pixels), BF16),
            jax.ShapeDtypeStruct((images, pixels, lanes), BF16),
        ],
        scratch_shapes=[pltpu.VMEM((lanes, pixels), F32)],
        compiler_params=pltpu.CompilerParams(vmem_limit_bytes=VMEM),
        cost_estimate=pl.CostEstimate(flops=1, bytes_accessed=1, transcendentals=0),
    )(raw, bias, gain)


def split3(value):
    first = value.astype(BF16).astype(F32)
    second = (value - first).astype(BF16).astype(F32)
    return first, second, value - first - second


def whole(array):
    return pl.BlockSpec(array.shape, lambda *_: (0,) * array.ndim)


def near_by(arrays):
    return [pl.BlockSpec(memory_space=pltpu.VMEM)] * len(arrays)


def anywhere(arrays):
    return [pl.BlockSpec(memory_space=pl.ANY)] * len(arrays)


def params(limit=VMEM):
    return pltpu.CompilerParams(vmem_limit_bytes=limit)


def cost(flops, moved, exps=0):
    return pl.CostEstimate(flops=int(flops) * 4, bytes_accessed=int(moved) * 4, transcendentals=int(exps) * 4)


def attend_kernel(channels, extra, tile, turned, *refs):
    wide_ref, tall_ref, query_ref, place = refs[:4]
    blocks = query_ref.shape[0]
    order = [place[0] ^ k if turned else k for k in range(blocks)]
    out_refs, (weight, scores) = refs[4 + extra : -2], refs[-2:]
    rows = wide_ref.shape[1]
    pixels = wide_ref.shape[2]
    span = query_ref.shape[3]
    weight[:rows] = jnp.concatenate([query_ref[k, 0] for k in order], axis=1)
    weight[rows:] = jnp.zeros((weight.shape[0] - rows, weight.shape[1]), BF16)
    top = None
    for at in range(0, pixels, tile):
        part = dot(tall_ref[0, at : at + tile], weight[...], ((1,), (0,)))
        scores[at : at + tile] = part
        part_top = jnp.max(part, 0, keepdims=True)
        top = part_top if top is None else jnp.maximum(top, part_top)
    total = jnp.zeros((rows, weight.shape[1]), F32)
    for at in range(0, pixels, tile):
        expo = jnp.exp(scores[at : at + tile] - top).astype(BF16)
        total += dot(wide_ref[0, :, at : at + tile], expo, ((1,), (0,)))
    mass = total[channels + 1 : channels + 2]
    attended = message(channels, total * (1.0 / mass), split3(top + jnp.log(mass)))
    for k in range(blocks):
        part = attended[:, k * span : (k + 1) * span]
        if turned:
            out_refs[k][0] = part
        else:
            out_refs[0][k, 0] = part


def message(channels, body, lines):
    row = lax.broadcasted_iota(jnp.int32, body.shape, 0)
    body = jnp.where(row < channels, body, 0.0)
    for k, line in enumerate(lines):
        body = jnp.where(row == channels + 1 + k, line, body)
    return body.astype(BF16)


def block_specs(blocks, rows, span, turned):
    if turned:
        return [pl.BlockSpec((1, rows, span), lambda b: (b, 0, 0))] * blocks
    return [pl.BlockSpec((blocks, 1, rows, span), lambda b: (0, b, 0, 0))]


def block_shapes(blocks, images, rows, span, turned):
    if turned:
        return [jax.ShapeDtypeStruct((images, rows, span), BF16)] * blocks
    return [jax.ShapeDtypeStruct((blocks, images, rows, span), BF16)]


def attend(wide, tall, queries, place, channels, first, images, turned, after=()):
    _, rows, pixels = wide.shape
    blocks, _, _, span = queries.shape
    lanes = tall.shape[2]
    tile = min(256, pixels)
    return pl.pallas_call(
        partial(attend_kernel, channels, len(after), tile, turned),
        grid=(images,),
        in_specs=[
            pl.BlockSpec((1, rows, pixels), lambda b: (b + first, 0, 0)),
            pl.BlockSpec((1, pixels, lanes), lambda b: (b + first, 0, 0)),
            pl.BlockSpec((blocks, 1, rows, span), lambda b: (0, b + first, 0, 0)),
            pl.BlockSpec(memory_space=pltpu.SMEM),
        ]
        + anywhere(after),
        out_specs=block_specs(blocks, rows, span, turned),
        out_shape=block_shapes(blocks, images, rows, span, turned),
        scratch_shapes=[
            pltpu.VMEM((lanes, blocks * span), BF16),
            pltpu.VMEM((pixels, blocks * span), F32),
        ],
        compiler_params=params(),
        cost_estimate=cost(
            images * pixels * blocks * span * rows * 8,
            images * pixels * (rows + lanes) * 2 + images * rows * blocks * span * 4,
            images * pixels * blocks * span,
        ),
        name="attend",
    )(wide, tall, queries, place, *after)


def attend_back_kernel(channels, extra, tile, turned, turned_out, *refs):
    wide_ref, tall_ref, raw_ref, gain_ref, query_ref, place = refs[:6]
    blocks = query_ref.shape[0]
    att_refs = refs[6 : 6 + blocks] if turned else refs[6:7]
    outs = refs[6 + len(att_refs) + extra :]
    grad_ref, out_refs, (query_weight, att_weight) = outs[0], outs[1:-2], outs[-2:]
    order = [place[0] ^ k for k in range(blocks)]
    rows = wide_ref.shape[1]
    pixels = wide_ref.shape[2]
    span = query_ref.shape[3]
    width = blocks * span
    queries = jnp.concatenate([query_ref[k, 0] for k in order], axis=1)
    atts = [ref[0] for ref in att_refs] if turned else [att_refs[0][k, 0] for k in order]
    atts = jnp.concatenate(atts, axis=1)
    row = lax.broadcasted_iota(jnp.int32, (rows, width), 0)
    shifts = (row > channels) & (row < channels + 4)
    query_weight[:rows] = jnp.where(shifts, atts.astype(F32), queries.astype(F32)).astype(BF16)
    att_weight[:rows] = jnp.where(shifts, 0.0, atts.astype(F32)).astype(BF16)
    fill = jnp.zeros((query_weight.shape[0] - rows, width), BF16)
    query_weight[rows:] = fill
    att_weight[rows:] = fill
    total = jnp.zeros((rows, width), F32)
    for at in range(0, pixels, tile):
        tall = tall_ref[0, at : at + tile]
        probs = jnp.exp(dot(tall, query_weight[...], ((1,), (0,))))
        grad = probs * dot(tall, att_weight[...], ((1,), (0,)))
        grad_low = grad.astype(BF16)
        probs_low = probs.astype(BF16)
        total += dot(wide_ref[0, :, at : at + tile], grad_low, ((1,), (0,)))
        into = dot(query_weight[:rows], grad_low, ((1,), (1,)))
        into += dot(att_weight[:rows], probs_low, ((1,), (1,)))
        raw = raw_ref[0, :, at : at + tile].astype(F32)
        centered = raw - jnp.sum(raw, 0, keepdims=True) * (1.0 / channels)
        rstd = lax.rsqrt(
            jnp.sum(centered * centered, 0, keepdims=True) * (1.0 / channels) + 1e-05
        )
        hat = centered * rstd
        upstream = into[:channels] * gain_ref[...]
        mean = jnp.sum(upstream, 0, keepdims=True) * (1.0 / channels)
        along = jnp.sum(upstream * hat, 0, keepdims=True) * (1.0 / channels)
        grad_ref[0, :, at : at + tile] = (rstd * (upstream - mean - hat * along)).astype(BF16)
    total = total.astype(BF16)
    for k in range(blocks):
        term = total[:, k * span : (k + 1) * span]
        if turned_out:
            out_refs[k][0] = term
        else:
            out_refs[0][order[k], 0] = term


def attend_back(wide, tall, raw, gain, queries, atts, place, channels, first, grad, turned, turned_out, after=()):
    all_images, rows, pixels = wide.shape
    blocks, _, _, span = queries.shape
    images = atts[0].shape[0 if turned else 1]
    lanes = tall.shape[2]
    tile = min(256, pixels)
    part = pl.BlockSpec((1, channels, pixels), lambda b: (b + first, 0, 0))
    earlier = [] if grad is None else [grad]
    extra = [*earlier, *after]
    results = pl.pallas_call(
        partial(attend_back_kernel, channels, len(extra), tile, turned, turned_out),
        grid=(images,),
        in_specs=[
            pl.BlockSpec((1, rows, pixels), lambda b: (b + first, 0, 0)),
            pl.BlockSpec((1, pixels, lanes), lambda b: (b + first, 0, 0)),
            part,
            whole(gain),
        ]
        + [
            pl.BlockSpec((blocks, 1, rows, span), lambda b: (0, b + first, 0, 0)),
            pl.BlockSpec(memory_space=pltpu.SMEM),
        ]
        + block_specs(blocks, rows, span, turned)
        + anywhere(extra),
        out_specs=[part] + block_specs(blocks, rows, span, turned_out),
        out_shape=[jax.ShapeDtypeStruct((all_images, channels, pixels), BF16)]
        + block_shapes(blocks, images, rows, span, turned_out),
        scratch_shapes=[
            pltpu.VMEM((lanes, blocks * span), BF16),
            pltpu.VMEM((lanes, blocks * span), BF16),
        ],
        compiler_params=params(),
        cost_estimate=cost(
            images * pixels * blocks * span * rows * 16,
            images * pixels * (rows * 3 + lanes) * 2 + images * rows * blocks * span * 6,
            images * pixels * blocks * span,
        ),
        input_output_aliases={6 + len(atts): 0} if earlier else {},
        name="attend_back",
    )(wide, tall, raw, gain, queries, place, *atts, *extra)
    return results[0], results[1:]


def merged(channels, parts):
    parts = [part.astype(F32) for part in parts]
    at = channels + 1
    logs = [part[at : at + 1] + part[at + 1 : at + 2] + part[at + 2 : at + 3] for part in parts]
    top = logs[0]
    for log in logs[1:]:
        top = jnp.maximum(top, log)
    shares = [jnp.exp(log - top) for log in logs]
    mass = shares[0]
    for share in shares[1:]:
        mass = mass + share
    pooled = parts[0] * (shares[0] / mass)
    for part, share in zip(parts[1:], shares[1:]):
        pooled = pooled + part * (share / mass)
    return pooled, top + jnp.log(mass)


def rows_norm(values):
    depth = values.shape[1]
    centered = values - jnp.sum(values, 1, keepdims=True) * (1.0 / depth)
    rstd = lax.rsqrt(jnp.sum(centered * centered, 1, keepdims=True) * (1.0 / depth) + 1e-05)
    return centered * rstd, rstd


def rows_norm_back(upstream, hat, rstd):
    depth = hat.shape[1]
    mean = jnp.sum(upstream, 1, keepdims=True) * (1.0 / depth)
    along = jnp.sum(upstream * hat, 1, keepdims=True) * (1.0 / depth)
    return rstd * (upstream - mean - hat * along)


def terms_of(refs, k):
    if len(refs) > 1:
        return [ref[k] for ref in refs]
    return [refs[0][j, k] for j in range(refs[0].shape[0])]


def middle_kernel(channels, count, extra, *refs):
    parts, refs = refs[:count], refs[count:]
    (latents, cot, grad_act, value_out, hidden, gain) = refs[:6]
    (note, pooled_ref, act_ref, into_ref, pre_ref, middle_ref, branch_ref, gain_ref) = refs[
        6 + extra :
    ]
    images, rows, span = parts[0].shape[-3:]
    kept, flipped = [], []
    row = lax.broadcasted_iota(jnp.int32, (rows, span), 0)
    for k in range(images):
        pooled, logs = merged(channels, terms_of(parts, k))
        pooled = jnp.where(row < channels, pooled, 0.0)
        low = pooled.astype(BF16)
        pooled_ref[k] = low
        kept.append((pooled, logs))
        flipped.append(low.T)
    middle = latents[...].astype(F32) + dot(
        jnp.concatenate(flipped, axis=0), value_out[...], ((1,), (0,))
    )
    middle_ref[...] = middle
    hat, rstd = rows_norm(middle)
    into = (hat * gain[...]).astype(BF16)
    into_ref[...] = into
    pre = dot(into, hidden[...], ((1,), (0,)))
    below = 0.5 + 0.5 * lax.erf(pre * (0.5**0.5))
    act_ref[...] = (pre * below).astype(BF16)
    slope = below + pre * (jnp.exp(-0.5 * pre * pre) * (2.0 * jnp.pi) ** -0.5)
    grad_pre = (grad_act[...] * slope).astype(BF16)
    pre_ref[...] = grad_pre
    grad_into = dot(grad_pre, hidden[...], ((1,), (1,)))
    gain_ref[...] = jnp.sum(grad_into * hat, 0, keepdims=True)
    grad = cot[...].astype(F32) + rows_norm_back(grad_into * gain[...], hat, rstd)
    branch = grad.astype(BF16)
    branch_ref[...] = branch
    att = dot(value_out[...], branch, ((1,), (1,)))
    for k in range(images):
        pooled, logs = kept[k]
        mine = att[:, k * span : (k + 1) * span]
        inner = jnp.sum(mine.astype(BF16).astype(F32) * pooled, 0, keepdims=True)
        line = message(channels, mine, (*split3(-logs), *split3(-inner)[:2]))
        if len(note.shape) == 3:
            note[k] = line
        else:
            for j in range(note.shape[0]):
                note[j, k] = line


def middle_part(parts, latents, cot, grad_act, value_out, hidden, gain, channels, at, after=()):
    images, rows, span = parts[0].shape[-3:]
    depth = latents.shape[1]
    high = images * span
    own = pl.BlockSpec((high, depth), lambda i: (at, 0))
    shape = jax.ShapeDtypeStruct
    arrays = [*parts, latents, cot, grad_act, value_out, hidden, gain]
    outs = [
        shape(parts[0].shape, BF16),
        shape((images, rows, span), BF16),
        shape((high, depth), BF16),
        shape((high, depth), BF16),
        shape((high, depth), BF16),
        shape((high, depth), F32),
        shape((high, depth), BF16),
        shape((1, depth), F32),
    ]
    return pl.pallas_call(
        partial(middle_kernel, channels, len(parts), len(after)),
        grid=(1,),
        in_specs=[whole(part) for part in parts]
        + [own, own, own, whole(value_out), whole(hidden), whole(gain)]
        + anywhere(after),
        out_specs=[whole(out) for out in outs],
        out_shape=outs,
        compiler_params=params(),
        cost_estimate=cost(
            high * depth * (depth + rows) * 8, high * depth * 24 + depth * depth * 4, high * depth * 2
        ),
        name="middle_part",
    )(*arrays, *after)


def finish_kernel(channels, count, extra, last, *refs):
    parts, refs = refs[:count], refs[count:]
    lat_in, latents, branch, query_key, gain = refs[:5]
    out_ref, sum_ref = refs[-2:]
    images, rows, span = parts[0].shape[-3:]
    wide, tall = [], []
    row = lax.broadcasted_iota(jnp.int32, (rows, span), 0)
    for k in range(images):
        first, *others = terms_of(parts, k)
        term = first.astype(F32)
        for other in others:
            term = term + other.astype(F32)
        term = jnp.where(row < channels, term, 0.0).astype(BF16)
        wide.append(term)
        tall.append(term.T)
    total = dot(jnp.concatenate(wide, axis=1), lat_in[...], ((1,), (0,)))
    if extra:
        total = total + refs[5][...]
    if last:
        width = sum_ref.shape[2]
        low = total.astype(BF16)
        for k in range(sum_ref.shape[0]):
            sum_ref[k] = low[:, k * width : (k + 1) * width]
    else:
        sum_ref[...] = total
    grad_in = dot(jnp.concatenate(tall, axis=0), query_key[...], ((1,), (0,)))
    hat, rstd = rows_norm(latents[...].astype(F32))
    back = rows_norm_back(grad_in * gain[...], hat, rstd)
    out_ref[...] = (branch[...].astype(F32) + back).astype(BF16)


def finish(
    parts, lat_in, latents, branch, query_key, gain, channels, at, earlier, pieces, after=()
):
    images, rows, span = parts[0].shape[-3:]
    depth = latents.shape[1]
    high = images * span
    own = pl.BlockSpec((high, depth), lambda i: (at, 0))
    if pieces:
        total = jax.ShapeDtypeStruct((pieces, rows, depth // pieces), BF16)
    else:
        total = jax.ShapeDtypeStruct((rows, depth), F32)
    arrays = [*parts, lat_in, latents, branch, query_key, gain]
    before = [] if earlier is None else [earlier]
    return pl.pallas_call(
        partial(finish_kernel, channels, len(parts), len(before), bool(pieces)),
        grid=(1,),
        in_specs=[whole(part) for part in parts]
        + [own, own, whole(branch), whole(query_key), whole(gain)]
        + [whole(array) for array in before]
        + anywhere(after),
        out_specs=[pl.BlockSpec((high, depth), lambda i: (0, 0)), whole(total)],
        out_shape=[jax.ShapeDtypeStruct((high, depth), BF16), total],
        compiler_params=params(),
        cost_estimate=cost(high * depth * rows * 4, high * depth * 8 + depth * rows * 8),
        name="finish",
    )(*arrays, *before, *after)


def pack_kernel(counts, *refs):
    ins, outs = refs[: -len(counts)], list(refs[-len(counts) :])
    at = 0
    for out, count in zip(outs, counts):
        column = 0
        for ref in ins[at : at + count]:
            width = round_up(ref.shape[1], 128)
            if width > ref.shape[1]:
                out[:, column : column + width] = jnp.zeros((out.shape[0], width), BF16)
            out[:, column : column + ref.shape[1]] = ref[...]
            column += width
        at += count


def pack(*groups):
    arrays = [array for group in groups for array in group]
    shapes = [
        jax.ShapeDtypeStruct(
            (group[0].shape[0], sum(round_up(array.shape[1], 128) for array in group)), BF16
        )
        for group in groups
    ]
    return pl.pallas_call(
        partial(pack_kernel, [len(group) for group in groups]),
        out_shape=shapes,
        compiler_params=params(),
        name="pack",
    )(*arrays)


def weights_kernel(channels, groups, counts, orders, *refs):
    pooled, branch, gains, act, into, pre = (
        refs[k * groups : (k + 1) * groups] for k in range(6)
    )
    cot, place = refs[6 * groups : 6 * groups + 2]
    kept, sent, first, second, third = refs[-5:]
    high = act[0].shape[0]
    sums = [None] * 4
    for k in range(groups):
        wide = jnp.concatenate([pooled[k][j] for j in range(pooled[k].shape[0])], axis=1)
        own = cot[k * high : (k + 1) * high]
        terms = (
            dot(into[k][...], pre[k][...], ((0,), (0,))),
            dot(act[k][...], own, ((0,), (0,))),
            dot(wide, branch[k][...], ((1,), (0,))),
            gains[k][...],
        )
        sums = [term if total is None else total + term for total, term in zip(sums, terms)]
    row = lax.broadcasted_iota(jnp.int32, sums[2].shape, 0)
    first[...] = sums[0].astype(BF16)
    second[...] = sums[1].astype(BF16)
    rows = sums[2].shape[0]
    third[:rows] = jnp.where(row == channels, sums[3], sums[2]).astype(BF16)
    third[rows:] = jnp.zeros((third.shape[0] - rows, third.shape[1]), BF16)
    imgs, lats, share, part = counts
    turned = pl.program_id(0)
    for spot in range(imgs):
        differs = [
            sum(order[k] for k in range(len(order)) if spot & (imgs >> (k + 1))) for order in orders
        ]
        i = place[0] ^ (differs[0] + turned * (differs[1] - differs[0]))
        out, at = (kept, spot) if spot < imgs // 2 else (sent, spot - imgs // 2)
        for j in range(lats):
            lines = pl.ds(pl.multiple_of((i * lats + j) * share, share), share)
            out[at, 0, 2 * j * share : (2 * j + 1) * share] = first[lines]
            out[at, 0, (2 * j + 1) * share : (2 * j + 2) * share] = second[lines]
        out[at, 0, 2 * lats * share :] = third[pl.ds(pl.multiple_of(i * part, part), part)]


def weights_part(pooled, branch, gains, act, into, pre, cot, place, channels, counts, after):
    imgs, lats, share, part = counts
    depth = cot.shape[1]
    whole_rows = 2 * lats * share + part
    orders = [img_steps(imgs, turned)[::-1] for turned in (False, True)]
    out = jax.ShapeDtypeStruct((imgs // 2, 2, whole_rows, depth // 2), BF16)
    block = pl.BlockSpec((imgs // 2, 1, whole_rows, depth // 2), lambda n: (0, n, 0, 0))

    def half(array):
        return pl.BlockSpec((array.shape[0], depth // 2), lambda n: (0, n))

    return pl.pallas_call(
        partial(weights_kernel, channels, len(pooled), counts, orders),
        grid=(2,),
        in_specs=[whole(array) for array in pooled]
        + [half(array) for array in (*branch, *gains)]
        + [whole(array) for array in (*act, *into)]
        + [half(array) for array in (*pre, cot)]
        + [pl.BlockSpec(memory_space=pltpu.SMEM)]
        + anywhere(after),
        out_specs=[block, block],
        out_shape=[out, out],
        scratch_shapes=[
            pltpu.VMEM((depth, depth // 2), BF16),
            pltpu.VMEM((depth, depth // 2), BF16),
            pltpu.VMEM((imgs * part, depth // 2), BF16),
        ],
        compiler_params=params(),
        cost_estimate=cost(cot.shape[0] * depth * depth * 5, cot.shape[0] * depth * 14),
        name="weights_part",
    )(*pooled, *branch, *gains, *act, *into, *pre, cot, place, *after)


def order_kernel(blocks, widths, tails, extra, *refs):
    place = refs[blocks + len(tails)]
    rows = refs[0].shape[0]
    outs = refs[blocks + len(tails) + 1 + extra :]
    for k in range(blocks):
        lines = pl.ds(pl.multiple_of((place[0] ^ k) * rows, rows), rows)
        at = 0
        for out, width in zip(outs, widths):
            out[lines, :width] = refs[k][:, at : at + width]
            at += width
    for n, at in enumerate(tails):
        outs[at][:, widths[at] :] = refs[blocks + n][...]


def order_rows(blocks, place, widths, after=(), tails=None):
    rows, columns = blocks[0].shape
    tails = tails or {}
    outs = [
        jax.ShapeDtypeStruct(
            (len(blocks) * rows, width + (tails[k].shape[1] if k in tails else 0)), BF16
        )
        for k, width in enumerate(widths)
    ]
    return pl.pallas_call(
        partial(order_kernel, len(blocks), widths, list(tails), len(after)),
        grid=(1,),
        in_specs=[whole(block) for block in (*blocks, *tails.values())]
        + [pl.BlockSpec(memory_space=pltpu.SMEM)]
        + anywhere(after),
        out_specs=[whole(out) for out in outs],
        out_shape=outs,
        compiler_params=params(),
        cost_estimate=cost(1, len(blocks) * rows * columns * 4),
        name="order_rows",
    )(*blocks, *tails.values(), place, *after)


def add_kernel(groups, extra, *refs):
    for k in range(groups):
        own, got = refs[2 * k], refs[2 * k + 1]
        kept, sent = refs[2 * groups + extra + 2 * k : 2 * groups + extra + 2 * k + 2]
        total = (own[...].astype(F32) + got[...].astype(F32)).astype(BF16)
        half = total.shape[0] // 2
        kept[...] = total[:half].reshape(kept.shape)
        sent[...] = total[half:].reshape(sent.shape)


def add_blocks(groups, after):
    arrays, specs, outs = [], [], []
    for array, at, got in groups:
        if at is None:
            specs += [whole(array), whole(got)]
            shape = (array.shape[0] // 2, *array.shape[1:])
        else:
            block = (got.shape[0], 1, *got.shape[2:])
            specs += [pl.BlockSpec(block, lambda i, at=at: (0, at, 0, 0))] * 2
            shape = (got.shape[0] // 2, *got.shape[2:])
        arrays += [array, got]
        outs += [jax.ShapeDtypeStruct(shape, BF16)] * 2
    return pl.pallas_call(
        partial(add_kernel, len(groups), len(after)),
        grid=(1,),
        in_specs=specs + anywhere(after),
        out_specs=[whole(out) for out in outs],
        out_shape=outs,
        compiler_params=params(),
        cost_estimate=cost(1, sum(got.size for _, _, got in groups) * 6),
        name="add_blocks",
    )(*arrays, *after)


def last_blocks(firsts, gots, place, lats, share, after):
    _, rows, width = firsts[0].shape
    base = 2 * lats * share
    outs = [
        jax.ShapeDtypeStruct((lats, 2 * share, 2 * width), BF16),
        jax.ShapeDtypeStruct((rows - base, 2 * width), BF16),
    ]
    arrays = [*firsts, *gots]

    def kernel(*refs):
        spots, common = refs[-2:]
        for n in range(2):
            total = (refs[n][0].astype(F32) + refs[2 + n][0].astype(F32)).astype(BF16)
            lanes = slice(n * width, (n + 1) * width)
            for j in range(lats):
                spots[refs[4][0] ^ j, :, lanes] = total[2 * j * share : (2 * j + 2) * share]
            common[:, lanes] = total[base:]

    return pl.pallas_call(
        kernel,
        grid=(1,),
        in_specs=[whole(array) for array in arrays]
        + [pl.BlockSpec(memory_space=pltpu.SMEM)]
        + anywhere(after),
        out_specs=[whole(out) for out in outs],
        out_shape=outs,
        compiler_params=params(),
        cost_estimate=cost(1, rows * width * 12),
        name="last_blocks",
    )(*arrays, place, *after)


def early_kernel(depth, rows, offsets, *refs):
    count = len(offsets)
    place, cot = refs[:2]
    firsts, seconds = refs[2 : 2 + count], refs[2 + count : 2 + 2 * count]
    hidden, back, queries, grad_act, value_out, back_rows, values, outputs = refs[-8:]
    high, width = firsts[0].shape
    wide_rows = width - 2 * depth
    for first, second, offset in zip(firsts, seconds, offsets):
        lines = pl.ds(pl.multiple_of((place[0] ^ offset) * high, high), high)
        hidden[lines] = first[:, :depth]
        values[lines] = first[:, depth : depth + rows]
        queries[lines] = first[:, depth + wide_rows :]
        back_rows[lines] = second[:, :depth]
        outputs[lines] = second[:, depth:]
    back[...] = back_rows[...]
    grad_act[...] = dot(cot[...], back_rows[...], ((1,), (1,)))
    value_out[...] = dot(values[...], outputs[...], ((0,), (0,))).astype(BF16)


def early_part(place, cot, firsts, seconds, offsets, depth, rows, after):
    high = cot.shape[0]
    shape = jax.ShapeDtypeStruct
    arrays = [cot, *firsts, *seconds]
    outs = [shape((depth, depth), BF16)] * 3 + [shape((high, depth), F32), shape((rows, depth), BF16)]
    return pl.pallas_call(
        partial(early_kernel, depth, rows, offsets),
        grid=(1,),
        in_specs=[pl.BlockSpec(memory_space=pltpu.SMEM)]
        + [whole(array) for array in arrays]
        + anywhere(after),
        out_specs=[whole(out) for out in outs],
        out_shape=outs,
        scratch_shapes=[
            pltpu.VMEM((depth, depth), BF16),
            pltpu.VMEM((depth, rows), BF16),
            pltpu.VMEM((depth, depth), BF16),
        ],
        compiler_params=params(),
        cost_estimate=cost(0, 0),
        name="early_part",
    )(place, *arrays, *after)


def out_kernel(groups, extra, *refs):
    back, out = refs[2 * groups], refs[-1]
    half = pl.program_id(0)
    for k in range(groups):

        @pl.when(half == k)
        def _():
            total = refs[groups + k][...] + dot(refs[k][...], back[...], ((1,), (0,)))
            out[...] = total.astype(BF16)


def out_part(act, middle, back, after):
    high, depth = act[0].shape
    groups = len(act)
    return pl.pallas_call(
        partial(out_kernel, groups, len(after)),
        grid=(groups,),
        in_specs=[whole(array) for array in (*act, *middle, back)] + anywhere(after),
        out_specs=pl.BlockSpec((high, depth), lambda i: (i, 0)),
        out_shape=jax.ShapeDtypeStruct((groups * high, depth), BF16),
        compiler_params=params(),
        cost_estimate=cost(groups * high * depth * depth * 2, groups * high * depth * 8),
        name="out_part",
    )(*act, *middle, back, *after)


def relay_kernel(*refs):
    pass


def relay(values, after):
    values, after = list(values), list(after)
    return pl.pallas_call(
        relay_kernel,
        in_specs=anywhere(values) + anywhere(after),
        out_specs=anywhere(values),
        out_shape=[jax.ShapeDtypeStruct(value.shape, value.dtype) for value in values],
        input_output_aliases={k: k for k in range(len(values))},
        name="relay",
    )(*values, *after)


def local(
    imgs,
    lats,
    latents,
    pixels,
    keep_mask,
    cotangent,
    gain_latent,
    gain_pixel,
    gain_mlp,
    w_query,
    w_key,
    w_value,
    w_output,
    w_hidden,
    w_return,
):
    images, span, depth = latents.shape
    channels = pixels.shape[2]
    devices = imgs * lats
    share = depth // devices
    rows = round_up(channels + 6, 16)
    scale = depth ** (-0.5)
    me = lax.axis_index("img") * lats + lax.axis_index("lat")

    raw = jnp.swapaxes(pixels, 1, 2)
    bias = jnp.where(keep_mask > 0, 0.0, OUT_OF_SIGHT).astype(F32)[:, None, :]
    gain_column = gain_pixel[:, None]

    place = lax.axis_index("lat")[None]

    near, later = pack((w_query, w_key.T), (w_hidden, w_value.T, w_return, w_output))
    plain = share % 16 != 0
    if plain:
        near = lax.all_gather(near, "lat", axis=0, tiled=True)
        near_query, near_key = near[:, :depth], near[:, depth : depth + rows]
    else:
        near = [near] + [swap_lat(near, step, lats) for step in range(1, lats)]
        (later,) = relay([later], near[1:2])
        later = [later] + [swap_lat(later, step, lats) for step in range(1, lats)]
        near_query, near_key = order_rows(near, place, (depth, rows))
    key_rows = lax.all_gather(near_key, "img", axis=0, tiled=True)
    query_key = (dot(key_rows, near_query, ((0,), (1,))) * scale).astype(BF16)
    query_key = side(lax.all_gather(query_key, "img", axis=0, tiled=False))

    groups = 2 if images % 2 == 0 else 1
    size = images // groups
    flat = latents.reshape(images * span, depth)
    cot = cotangent.reshape(images * span, depth)
    gain_lat, gain_mid = gain_latent[None], gain_mlp[None]
    lat_in = (normalize(flat.astype(F32))[0] * gain_lat).astype(BF16)
    lat_blocks = lat_in.reshape(images, span, depth)
    row = lax.broadcasted_iota(jnp.int32, (1, rows, 1), 1)
    early_blocks = lat_blocks if plain else relay([lat_blocks], later[1:])[0]
    query = jnp.einsum("cd,bld->bcl", query_key, early_blocks, preferred_element_type=F32)
    query = jnp.where(row == channels, 1.0, query).astype(BF16)
    (queries,) = lat_gather(jnp.broadcast_to(query[None], (lats, *query.shape)), lats)
    (late_bias,) = relay([bias], [query])
    wide, tall = pixel_prep(raw, late_bias, gain_column, rows)

    wide_rows = round_up(rows, 128)
    img_place = lax.axis_index("img")[None]
    if not plain:
        first, second = order_rows(
            later, place, (depth + wide_rows, 2 * depth), [query], {0: near_query}
        )
        (first, second), offsets = img_gather([first, second], imgs)
    turned = [k % 2 == 0 for k in range(groups)]
    attended, parts = [], None
    for k in range(groups):
        after = [] if parts is None else parts[:1]
        parts = attend(wide, tall, queries, place, channels, k * size, size, turned[k], after)
        attended.append(lat_return(parts, lats))
    if plain:
        later = lax.all_gather(later, AXES, axis=0, tiled=True)
        query_rows = lax.all_gather(w_query, AXES, axis=0, tiled=True)
        hidden, back = later[:, :depth], later[:, depth + wide_rows : 2 * depth + wide_rows]
        grad_act = dot(cot, back, ((1,), (1,)))
        value_out = dot(
            later[:, depth : depth + rows], later[:, 2 * depth + wide_rows :], ((0,), (0,))
        ).astype(BF16)
    else:
        hidden, back, query_rows, grad_act, value_out = early_part(
            img_place, cot, first, second, offsets, depth, rows, parts[:1]
        )

    lines = [slice(k * size * span, (k + 1) * size * span) for k in range(groups)]
    middles, atts = [], []
    for k in range(groups):
        middles.append(
            middle_part(
                attended[k],
                flat,
                cot,
                grad_act,
                value_out,
                hidden,
                gain_mid,
                channels,
                k,
            )
        )
        atts.append(lat_gather(middles[k][0], lats))
    _, pooled, act, mlp_in, grad_pre, middle, branch, gain_grad = (
        [part[j] for part in middles] for j in range(8)
    )
    pin = []
    if not plain:
        part = round_up(-(-rows // imgs), 16)
        counts = (imgs, lats, share, part)
        orders = [img_steps(imgs, turned)[::-1] for turned in (False, True)]
        kept, sent = weights_part(
            pooled,
            branch,
            gain_grad,
            act,
            mlp_in,
            grad_pre,
            cot,
            img_place,
            channels,
            counts,
            [],
        )
        got = swap_img(sent, orders[0][0], imgs)
        pin = [sent]
    grad_raw, ends = None, []
    for k in range(groups):
        grad_raw, parts = attend_back(
            wide,
            tall,
            raw,
            gain_column,
            queries,
            atts[k],
            place,
            channels,
            k * size,
            grad_raw,
            turned[k],
            not turned[k],
            pin,
        )
        ends.append(lat_return(parts, lats))
        if k == 0 and not plain:
            split = add_blocks([(kept, n, got) for n in range(2)], parts[:1])
            kept, sent = split[0::2], split[1::2]
            pin = sent[:1]
    if not plain:
        for bit in range(1, len(orders[0]) - 1):
            gots = [swap_img(sent[n], orders[n][bit], imgs) for n in range(2)]
            split = add_blocks([(kept[n], None, gots[n]) for n in range(2)], parts[:1])
            kept, sent = split[0::2], split[1::2]

    grad_latents, latent_grad = [], None
    for k in range(groups):
        done, latent_grad = finish(
            ends[k],
            lat_in,
            flat,
            branch[k],
            query_key,
            gain_lat,
            channels,
            k,
            latent_grad,
            imgs if k == groups - 1 else 0,
            pin if plain else sent[:1],
        )
        grad_latents.append(done)
        if k == 0:
            output = out_part(act, middle, back, [done])
    if not plain:
        gots = [swap_img(sent[n], orders[n][-1], imgs) for n in range(2)]

    pieces = latent_grad
    latent_grad = sum_img(pieces, imgs)
    latent_terms = [latent_grad] + [swap_lat(latent_grad, step, lats) for step in range(1, lats)]
    latent_grad = sum_terms(latent_terms).astype(BF16)
    if plain:
        both = jnp.stack(
            [
                sum(dot(mlp_in[k], grad_pre[k], ((0,), (0,))) for k in range(groups)),
                sum(dot(act[k], cot[lines[k]], ((0,), (0,))) for k in range(groups)),
            ]
        ).astype(BF16)
        sums = lax.psum_scatter(both, AXES, scatter_dimension=1, tiled=True).astype(F32)
        shard_h, shard_r = sums[0], sums[1]
        common = sum(
            jnp.einsum(
                "bcl,bld->cd",
                pooled[k],
                branch[k].reshape(size, span, depth),
                preferred_element_type=F32,
            )
            for k in range(groups)
        )
        line = lax.broadcasted_iota(jnp.int32, (rows, 1), 0)
        common = jnp.where(line == channels, sum(gain_grad), common)
        pooled_grad = lax.psum(common, AXES).astype(BF16)
    else:
        blocks, common = last_blocks(kept, gots, place, lats, share, latent_terms[1:2])
        sent = [common] * (lats - 1) + [blocks[step] for step in range(1, lats)]
        came = [swap_lat(block, 1 + k % (lats - 1), lats) for k, block in enumerate(sent)]
        common = sum_terms([common] + came[: lats - 1]).astype(BF16)
        sums = sum_terms([blocks[0]] + came[lats - 1 :])
        shard_h, shard_r = sums[:share], sums[share:]
        pooled_grad = lax.all_gather(common, "img", axis=0, tiled=True)
    sum_mlp = pooled_grad[channels].astype(F32)
    pooled_grad = pooled_grad[:channels]
    shard_o = dot(w_value, pooled_grad, ((0,), (0,)))
    shard_v = dot(pooled_grad, w_output, ((1,), (1,)))
    latent_grad = side(lax.all_gather(latent_grad, "img", axis=0, tiled=False))[:channels]
    mine = lax.dynamic_slice_in_dim(latent_grad, me * share, share, 1)
    shard_q = dot(mine, key_rows[:, :channels], ((0,), (1,))) * scale
    columns = lax.dynamic_slice_in_dim(query_rows, me * share, share, 1)
    shard_k = dot(latent_grad, columns, ((1,), (0,))) * scale
    with_key = query_key[:channels].astype(F32) * latent_grad.astype(F32)
    with_value = value_out[:channels].astype(F32) * pooled_grad.astype(F32)
    sum_lat = jnp.sum(with_key, 0) / gain_latent
    sum_pix = jnp.sum(with_key + with_value, 1) / gain_pixel
    return (
        output.reshape(images, span, depth),
        jnp.concatenate(grad_latents).reshape(images, span, depth),
        jnp.swapaxes(grad_raw, 1, 2),
        shard_q,
        shard_k,
        shard_v,
        shard_o,
        shard_h,
        shard_r,
        sum_lat,
        sum_pix,
        sum_mlp,
    )


def solution(mesh):
    in_specs = (
        P("img", "lat", None),
        P("img", "lat", None),
        P("img", "lat"),
        P("img", "lat", None),
        P(),
        P(),
        P(),
        P(("img", "lat"), None),
        P(None, ("img", "lat")),
        P(None, ("img", "lat")),
        P(("img", "lat"), None),
        P(("img", "lat"), None),
        P(("img", "lat"), None),
    )
    out_specs = (
        P("img", "lat", None),
        P("img", "lat", None),
        P("img", "lat", None),
        P(("img", "lat"), None),
        P(None, ("img", "lat")),
        P(None, ("img", "lat")),
        P(("img", "lat"), None),
        P(("img", "lat"), None),
        P(("img", "lat"), None),
        P(),
        P(),
        P(),
    )
    step = partial(local, mesh.shape["img"], mesh.shape["lat"])
    return jax.shard_map(step, mesh=mesh, in_specs=in_specs, out_specs=out_specs, check_vma=False)
```

```python
from functools import partial

import jax
import jax.numpy as jnp
from jax import lax
from jax.experimental import pallas as pl
from jax.experimental.pallas import tpu as pltpu
from jax.sharding import PartitionSpec as P

F32 = jnp.float32
BF16 = jnp.bfloat16
AXES = ("img", "lat")
OUT_OF_SIGHT = -1e30
VMEM = 56 * 1024 * 1024
LESS_VMEM = 28 * 1024 * 1024


def round_up(value, unit):
    return -(-value // unit) * unit


def normalize(values):
    centered = values - jnp.mean(values, -1, keepdims=True)
    rstd = lax.rsqrt(jnp.mean(centered * centered, -1, keepdims=True) + 1e-05)
    return (centered * rstd, rstd)


def dot(left, right, contract):
    return lax.dot_general(left, right, (contract, ((), ())), preferred_element_type=F32)


def swap_lat(value, step, size):
    return lax.ppermute(value, "lat", [(i, i ^ step) for i in range(size)])


def swap_img(value, step, size):
    return lax.ppermute(value, "img", [(i, i ^ step) for i in range(size)])


def img_steps(size, turned=False):
    bits = [1 << k for k in reversed(range(size.bit_length() - 1))]
    return bits[1::-1] + bits[2:] if turned and len(bits) > 2 else bits


def img_gather(values, size):
    nearest, *others = [1 << k for k in range(size.bit_length() - 1)]
    blocks = [[value] for value in values]
    offsets = [0]
    for step in others:
        passed = offsets[1:]
        blocks = [held + [swap_img(held[0], step, size)] for held in blocks]
        offsets = offsets + [step]
        for offset in passed:
            for n, held in enumerate(blocks):
                turned = n % 2 == 1 and len(passed) == 1
                source = len(passed) + 1 if turned else offsets.index(offset)
                way = offset if turned else step
                blocks[n] = held + [swap_img(held[source], way, size)]
            offsets = offsets + [offset ^ step]
    blocks = [held + [swap_img(block, nearest, size) for block in held] for held in blocks]
    return blocks, offsets + [offset ^ nearest for offset in offsets]


def lat_gather(blocks, size):
    if blocks.ndim == 4:
        return [lax.all_to_all(blocks, "lat", 0, 0, tiled=True)]
    return [blocks] + [swap_lat(blocks, step, size) for step in range(1, size)]


def lat_return(blocks, size):
    if len(blocks) == 1:
        return [lax.all_to_all(blocks[0], "lat", 0, 0, tiled=True)]
    return [blocks[0]] + [swap_lat(blocks[step], step, size) for step in range(1, size)]


def sum_terms(terms):
    terms = [term.astype(F32) for term in terms]
    while len(terms) > 1:
        terms = [sum(terms[i : i + 2]) for i in range(0, len(terms), 2)]
    return terms[0]


def sum_img(pieces, imgs):
    pieces = lax.all_to_all(pieces, "img", 0, 0, tiled=True)
    return lax.reduce_precision(sum_terms([pieces[j] for j in range(imgs)]), 8, 7).astype(BF16)


def sum_lat_places(mine, lats):
    return sum_terms([mine] + [swap_lat(mine, step, lats) for step in range(1, lats)]).astype(BF16)


def side(pieces):
    return pieces.transpose(1, 0, 2).reshape(pieces.shape[1], -1)


def pixel_kernel(channels, raw_ref, bias_ref, gain_ref, wide_ref, tall_ref, work):
    raw = raw_ref[0].astype(F32)
    rows = work.shape[0]
    centered = raw - jnp.sum(raw, 0, keepdims=True) * (1.0 / channels)
    rstd = lax.rsqrt(jnp.sum(centered * centered, 0, keepdims=True) * (1.0 / channels) + 1e-05)
    base = channels // 8 * 8
    row = lax.broadcasted_iota(jnp.int32, (rows - base, raw.shape[1]), 0) + base
    work[base:rows] = jnp.where((row > channels) & (row < channels + 6), 1.0, 0.0).astype(F32)
    work[0:channels] = centered * rstd * gain_ref[...]
    work[channels : channels + 1] = bias_ref[0]
    whole = work[...]
    wide_ref[0] = whole[: wide_ref.shape[1]].astype(BF16)
    tall_ref[0] = whole.T.astype(BF16)


def pixel_prep(raw, bias, gain, rows):
    images, channels, pixels = raw.shape
    lanes = round_up(rows, 128)
    return pl.pallas_call(
        partial(pixel_kernel, channels),
        grid=(images,),
        in_specs=[
            pl.BlockSpec((1, channels, pixels), lambda b: (b, 0, 0)),
            pl.BlockSpec((1, 1, pixels), lambda b: (b, 0, 0)),
            pl.BlockSpec((channels, 1), lambda b: (0, 0)),
        ],
        out_specs=[
            pl.BlockSpec((1, rows, pixels), lambda b: (b, 0, 0)),
            pl.BlockSpec((1, pixels, lanes), lambda b: (b, 0, 0)),
        ],
        out_shape=[
            jax.ShapeDtypeStruct((images, rows, pixels), BF16),
            jax.ShapeDtypeStruct((images, pixels, lanes), BF16),
        ],
        scratch_shapes=[pltpu.VMEM((lanes, pixels), F32)],
        compiler_params=pltpu.CompilerParams(vmem_limit_bytes=VMEM),
        cost_estimate=pl.CostEstimate(flops=1, bytes_accessed=1, transcendentals=0),
    )(raw, bias, gain)


def split3(value):
    first = value.astype(BF16).astype(F32)
    second = (value - first).astype(BF16).astype(F32)
    return first, second, value - first - second


def whole(array):
    return pl.BlockSpec(array.shape, lambda *_: (0,) * array.ndim)


def near_by(arrays):
    return [pl.BlockSpec(memory_space=pltpu.VMEM)] * len(arrays)


def anywhere(arrays):
    return [pl.BlockSpec(memory_space=pl.ANY)] * len(arrays)


def params(limit=VMEM):
    return pltpu.CompilerParams(vmem_limit_bytes=limit)


def cost(flops, moved, exps=0):
    return pl.CostEstimate(flops=int(flops) * 4, bytes_accessed=int(moved) * 4, transcendentals=int(exps) * 4)


def terms_of_block(refs):
    if len(refs) > 1:
        return [ref[0] for ref in refs]
    return [refs[0][j, 0] for j in range(refs[0].shape[0])]


def attend_kernel(channels, count, extra, tile, turned, *refs):
    wide_ref, tall_ref, place = refs[:3]
    out_refs, (weight, scores) = refs[3 + count + extra : -2], refs[-2:]
    queries = terms_of_block(refs[3 : 3 + count])
    blocks, span = len(queries), queries[0].shape[1]
    rows = wide_ref.shape[1]
    pixels = wide_ref.shape[2]
    weight[:rows] = jnp.concatenate(queries, axis=1)
    weight[rows:] = jnp.zeros((weight.shape[0] - rows, weight.shape[1]), BF16)
    top = None
    for at in range(0, pixels, tile):
        part = dot(tall_ref[0, at : at + tile], weight[...], ((1,), (0,)))
        scores[at : at + tile] = part
        part_top = jnp.max(part, 0, keepdims=True)
        top = part_top if top is None else jnp.maximum(top, part_top)
    total = jnp.zeros((rows, weight.shape[1]), F32)
    for at in range(0, pixels, tile):
        expo = jnp.exp(scores[at : at + tile] - top).astype(BF16)
        total += dot(wide_ref[0, :, at : at + tile], expo, ((1,), (0,)))
    mass = total[channels + 1 : channels + 2]
    attended = message(channels, total * (1.0 / mass), split3(top + jnp.log(mass)))
    for k in range(blocks):
        part = attended[:, k * span : (k + 1) * span]
        if turned:
            out_refs[k][0] = part
        else:
            out_refs[0][k, 0] = part


def message(channels, body, lines):
    row = lax.broadcasted_iota(jnp.int32, body.shape, 0)
    body = jnp.where(row < channels, body, 0.0)
    for k, line in enumerate(lines):
        body = jnp.where(row == channels + 1 + k, line, body)
    return body.astype(BF16)


def block_specs(blocks, rows, span, turned):
    if turned:
        return [pl.BlockSpec((1, rows, span), lambda b: (b, 0, 0))] * blocks
    return [pl.BlockSpec((blocks, 1, rows, span), lambda b: (0, b, 0, 0))]


def block_shapes(blocks, images, rows, span, turned):
    if turned:
        return [jax.ShapeDtypeStruct((images, rows, span), BF16)] * blocks
    return [jax.ShapeDtypeStruct((blocks, images, rows, span), BF16)]


def attend(wide, tall, queries, place, channels, first, turned, after=()):
    _, rows, pixels = wide.shape
    images, _, span = queries[0].shape[-3:]
    blocks = len(queries) if turned else queries[0].shape[0]
    lanes = tall.shape[2]
    tile = min(256, pixels)
    return pl.pallas_call(
        partial(attend_kernel, channels, len(queries), len(after), tile, turned),
        grid=(images,),
        in_specs=[
            pl.BlockSpec((1, rows, pixels), lambda b: (b + first, 0, 0)),
            pl.BlockSpec((1, pixels, lanes), lambda b: (b + first, 0, 0)),
            pl.BlockSpec(memory_space=pltpu.SMEM),
        ]
        + block_specs(blocks, rows, span, turned)
        + anywhere(after),
        out_specs=block_specs(blocks, rows, span, turned),
        out_shape=block_shapes(blocks, images, rows, span, turned),
        scratch_shapes=[
            pltpu.VMEM((lanes, blocks * span), BF16),
            pltpu.VMEM((pixels, blocks * span), F32),
        ],
        compiler_params=params(),
        cost_estimate=cost(
            images * pixels * blocks * span * rows * 8,
            images * pixels * (rows + lanes) * 2 + images * rows * blocks * span * 4,
            images * pixels * blocks * span,
        ),
        name="attend",
    )(wide, tall, place, *queries, *after)


def attend_back_kernel(channels, count, extra, tile, turned, *refs):
    wide_ref, tall_ref, raw_ref, gain_ref, place = refs[:5]
    queries, atts = terms_of_block(refs[5 : 5 + count]), terms_of_block(refs[5 + count : 5 + 2 * count])
    outs = refs[5 + 2 * count + extra :]
    grad_ref, out_refs, (query_weight, att_weight) = outs[0], outs[1:-2], outs[-2:]
    blocks, span = len(queries), queries[0].shape[1]
    rows = wide_ref.shape[1]
    pixels = wide_ref.shape[2]
    width = blocks * span
    queries = jnp.concatenate(queries, axis=1)
    atts = jnp.concatenate(atts, axis=1)
    row = lax.broadcasted_iota(jnp.int32, (rows, width), 0)
    shifts = (row > channels) & (row < channels + 4)
    query_weight[:rows] = jnp.where(shifts, atts.astype(F32), queries.astype(F32)).astype(BF16)
    att_weight[:rows] = jnp.where(shifts, 0.0, atts.astype(F32)).astype(BF16)
    fill = jnp.zeros((query_weight.shape[0] - rows, width), BF16)
    query_weight[rows:] = fill
    att_weight[rows:] = fill
    total = jnp.zeros((rows, width), F32)
    for at in range(0, pixels, tile):
        tall = tall_ref[0, at : at + tile]
        probs = jnp.exp(dot(tall, query_weight[...], ((1,), (0,))))
        grad = probs * dot(tall, att_weight[...], ((1,), (0,)))
        grad_low = grad.astype(BF16)
        probs_low = probs.astype(BF16)
        total += dot(wide_ref[0, :, at : at + tile], grad_low, ((1,), (0,)))
        into = dot(query_weight[:rows], grad_low, ((1,), (1,)))
        into += dot(att_weight[:rows], probs_low, ((1,), (1,)))
        raw = raw_ref[0, :, at : at + tile].astype(F32)
        centered = raw - jnp.sum(raw, 0, keepdims=True) * (1.0 / channels)
        rstd = lax.rsqrt(
            jnp.sum(centered * centered, 0, keepdims=True) * (1.0 / channels) + 1e-05
        )
        hat = centered * rstd
        upstream = into[:channels] * gain_ref[...]
        mean = jnp.sum(upstream, 0, keepdims=True) * (1.0 / channels)
        along = jnp.sum(upstream * hat, 0, keepdims=True) * (1.0 / channels)
        grad_ref[0, :, at : at + tile] = (rstd * (upstream - mean - hat * along)).astype(BF16)
    total = total.astype(BF16)
    terms = [total[:, k * span : (k + 1) * span] for k in range(blocks)]
    if turned:
        for k in range(blocks):
            out_refs[0][place[0] ^ k, 0] = terms[k]
    else:
        for k in range(blocks):
            at = place[0] ^ k
            chosen = terms[0]
            for j in range(1, blocks):
                chosen = jnp.where(at == j, terms[j], chosen)
            out_refs[k][0] = chosen


def attend_back(wide, tall, raw, gain, queries, atts, place, channels, first, grad, turned, after=()):
    all_images, rows, pixels = wide.shape
    images, _, span = queries[0].shape[-3:]
    blocks = len(queries) if turned else queries[0].shape[0]
    lanes = tall.shape[2]
    tile = min(256, pixels)
    part = pl.BlockSpec((1, channels, pixels), lambda b: (b + first, 0, 0))
    earlier = [] if grad is None else [grad]
    extra = [*earlier, *after]
    results = pl.pallas_call(
        partial(attend_back_kernel, channels, len(queries), len(extra), tile, turned),
        grid=(images,),
        in_specs=[
            pl.BlockSpec((1, rows, pixels), lambda b: (b + first, 0, 0)),
            pl.BlockSpec((1, pixels, lanes), lambda b: (b + first, 0, 0)),
            part,
            whole(gain),
        ]
        + [
            pl.BlockSpec(memory_space=pltpu.SMEM),
        ]
        + block_specs(blocks, rows, span, turned) * 2
        + anywhere(extra),
        out_specs=[part] + block_specs(blocks, rows, span, not turned),
        out_shape=[jax.ShapeDtypeStruct((all_images, channels, pixels), BF16)]
        + block_shapes(blocks, images, rows, span, not turned),
        scratch_shapes=[
            pltpu.VMEM((lanes, blocks * span), BF16),
            pltpu.VMEM((lanes, blocks * span), BF16),
        ],
        compiler_params=params(),
        cost_estimate=cost(
            images * pixels * blocks * span * rows * 16,
            images * pixels * (rows * 3 + lanes) * 2 + images * rows * blocks * span * 6,
            images * pixels * blocks * span,
        ),
        input_output_aliases={5 + 2 * len(atts): 0} if earlier else {},
        name="attend_back",
    )(wide, tall, raw, gain, place, *queries, *atts, *extra)
    return results[0], results[1:]


def merged(channels, parts):
    parts = [part.astype(F32) for part in parts]
    at = channels + 1
    logs = [part[at : at + 1] + part[at + 1 : at + 2] + part[at + 2 : at + 3] for part in parts]
    top = logs[0]
    for log in logs[1:]:
        top = jnp.maximum(top, log)
    shares = [jnp.exp(log - top) for log in logs]
    mass = shares[0]
    for share in shares[1:]:
        mass = mass + share
    pooled = parts[0] * (shares[0] / mass)
    for part, share in zip(parts[1:], shares[1:]):
        pooled = pooled + part * (share / mass)
    return pooled, top + jnp.log(mass)


def rows_norm(values):
    depth = values.shape[1]
    centered = values - jnp.sum(values, 1, keepdims=True) * (1.0 / depth)
    rstd = lax.rsqrt(jnp.sum(centered * centered, 1, keepdims=True) * (1.0 / depth) + 1e-05)
    return centered * rstd, rstd


def rows_norm_back(upstream, hat, rstd):
    depth = hat.shape[1]
    mean = jnp.sum(upstream, 1, keepdims=True) * (1.0 / depth)
    along = jnp.sum(upstream * hat, 1, keepdims=True) * (1.0 / depth)
    return rstd * (upstream - mean - hat * along)


def terms_of(refs, k):
    if len(refs) > 1:
        return [ref[k] for ref in refs]
    return [refs[0][j, k] for j in range(refs[0].shape[0])]


def middle_kernel(channels, count, extra, *refs):
    parts, refs = refs[:count], refs[count:]
    (latents, cot, grad_act, value_out, hidden, gain) = refs[:6]
    (note, pooled_ref, act_ref, into_ref, pre_ref, middle_ref, branch_ref, gain_ref) = refs[
        6 + extra :
    ]
    images, rows, span = parts[0].shape[-3:]
    kept, flipped = [], []
    row = lax.broadcasted_iota(jnp.int32, (rows, span), 0)
    for k in range(images):
        pooled, logs = merged(channels, terms_of(parts, k))
        pooled = jnp.where(row < channels, pooled, 0.0)
        low = pooled.astype(BF16)
        pooled_ref[k] = low
        kept.append((pooled, logs))
        flipped.append(low.T)
    middle = latents[...].astype(F32) + dot(
        jnp.concatenate(flipped, axis=0), value_out[...], ((1,), (0,))
    )
    middle_ref[...] = middle
    hat, rstd = rows_norm(middle)
    into = (hat * gain[...]).astype(BF16)
    into_ref[...] = into
    pre = dot(into, hidden[...], ((1,), (0,)))
    below = 0.5 + 0.5 * lax.erf(pre * (0.5**0.5))
    act_ref[...] = (pre * below).astype(BF16)
    slope = below + pre * (jnp.exp(-0.5 * pre * pre) * (2.0 * jnp.pi) ** -0.5)
    grad_pre = (grad_act[...] * slope).astype(BF16)
    pre_ref[...] = grad_pre
    grad_into = dot(grad_pre, hidden[...], ((1,), (1,)))
    gain_ref[...] = jnp.sum(grad_into * hat, 0, keepdims=True)
    grad = cot[...].astype(F32) + rows_norm_back(grad_into * gain[...], hat, rstd)
    branch = grad.astype(BF16)
    branch_ref[...] = branch
    att = dot(value_out[...], branch, ((1,), (1,)))
    for k in range(images):
        pooled, logs = kept[k]
        mine = att[:, k * span : (k + 1) * span]
        inner = jnp.sum(mine.astype(BF16).astype(F32) * pooled, 0, keepdims=True)
        line = message(channels, mine, (*split3(-logs), *split3(-inner)[:2]))
        if len(note.shape) == 3:
            note[k] = line
        else:
            for j in range(note.shape[0]):
                note[j, k] = line


def middle_part(parts, latents, cot, grad_act, value_out, hidden, gain, channels, at, after=()):
    images, rows, span = parts[0].shape[-3:]
    depth = latents.shape[1]
    high = images * span
    own = pl.BlockSpec((high, depth), lambda i: (at, 0))
    shape = jax.ShapeDtypeStruct
    arrays = [*parts, latents, cot, grad_act, value_out, hidden, gain]
    outs = [
        shape(parts[0].shape, BF16),
        shape((images, rows, span), BF16),
        shape((high, depth), BF16),
        shape((high, depth), BF16),
        shape((high, depth), BF16),
        shape((high, depth), F32),
        shape((high, depth), BF16),
        shape((1, depth), F32),
    ]
    return pl.pallas_call(
        partial(middle_kernel, channels, len(parts), len(after)),
        grid=(1,),
        in_specs=[whole(part) for part in parts]
        + [own, own, own, whole(value_out), whole(hidden), whole(gain)]
        + anywhere(after),
        out_specs=[whole(out) for out in outs],
        out_shape=outs,
        compiler_params=params(),
        cost_estimate=cost(
            high * depth * (depth + rows) * 8, high * depth * 24 + depth * depth * 4, high * depth * 2
        ),
        name="middle_part",
    )(*arrays, *after)


def terms_kernel(channels, count, extra, last, *refs):
    parts, lat_in = refs[:count], refs[count]
    term_ref, sum_ref = refs[-2:]
    images, rows, span = parts[0].shape[-3:]
    row = lax.broadcasted_iota(jnp.int32, (rows, span), 0)
    terms = []
    for k in range(images):
        first, *others = terms_of(parts, k)
        term = first.astype(F32)
        for other in others:
            term = term + other.astype(F32)
        terms.append(jnp.where(row < channels, term, 0.0).astype(BF16))
        term_ref[k] = terms[k]
    total = dot(jnp.concatenate(terms, axis=1), lat_in[...], ((1,), (0,)))
    if extra:
        total = total + refs[count + 1][...]
    if last:
        width = sum_ref.shape[2]
        low = total.astype(BF16)
        for k in range(sum_ref.shape[0]):
            sum_ref[k] = low[:, k * width : (k + 1) * width]
    else:
        sum_ref[...] = total


def terms_part(parts, lat_in, channels, at, earlier, pieces, after):
    images, rows, span = parts[0].shape[-3:]
    depth = lat_in.shape[1]
    if pieces:
        total = jax.ShapeDtypeStruct((pieces, rows, depth // pieces), BF16)
    else:
        total = jax.ShapeDtypeStruct((rows, depth), F32)
    outs = [jax.ShapeDtypeStruct((images, rows, span), BF16), total]
    before = [] if earlier is None else [earlier]
    return pl.pallas_call(
        partial(terms_kernel, channels, len(parts), len(before), bool(pieces)),
        grid=(1,),
        in_specs=[whole(part) for part in parts]
        + [pl.BlockSpec((images * span, depth), lambda i: (at, 0))]
        + [whole(array) for array in before]
        + anywhere(after),
        out_specs=[whole(out) for out in outs],
        out_shape=outs,
        compiler_params=params(),
        cost_estimate=cost(images * span * depth * rows * 2, images * span * depth * 4),
        name="terms_part",
    )(*parts, lat_in, *before, *after)


def finish_kernel(extra, *refs):
    terms, latents, branch, query_key, gain = refs[:5]
    out_ref = refs[-1]
    tall = jnp.concatenate([terms[k].T for k in range(terms.shape[0])], axis=0)
    grad_in = dot(tall, query_key[...], ((1,), (0,)))
    hat, rstd = rows_norm(latents[...].astype(F32))
    back = rows_norm_back(grad_in * gain[...], hat, rstd)
    out_ref[...] = (branch[...].astype(F32) + back).astype(BF16)


def finish(terms, latents, branch, query_key, gain, at, after):
    images, rows, span = terms.shape
    high, depth = images * span, latents.shape[1]
    out = jax.ShapeDtypeStruct((high, depth), BF16)
    return pl.pallas_call(
        partial(finish_kernel, len(after)),
        grid=(1,),
        in_specs=[
            whole(terms),
            pl.BlockSpec((high, depth), lambda i: (at, 0)),
            whole(branch),
            whole(query_key),
            whole(gain),
        ]
        + anywhere(after),
        out_specs=whole(out),
        out_shape=out,
        compiler_params=params(),
        cost_estimate=cost(high * depth * rows * 2, high * depth * 8),
        name="finish",
    )(terms, latents, branch, query_key, gain, *after)


def pack_kernel(counts, *refs):
    ins, outs = refs[: -len(counts)], list(refs[-len(counts) :])
    at = 0
    for out, count in zip(outs, counts):
        column = 0
        for ref in ins[at : at + count]:
            width = round_up(ref.shape[1], 128)
            if width > ref.shape[1]:
                out[:, column : column + width] = jnp.zeros((out.shape[0], width), BF16)
            out[:, column : column + ref.shape[1]] = ref[...]
            column += width
        at += count


def pack(*groups):
    arrays = [array for group in groups for array in group]
    shapes = [
        jax.ShapeDtypeStruct(
            (group[0].shape[0], sum(round_up(array.shape[1], 128) for array in group)), BF16
        )
        for group in groups
    ]
    return pl.pallas_call(
        partial(pack_kernel, [len(group) for group in groups]),
        out_shape=shapes,
        compiler_params=params(),
        name="pack",
    )(*arrays)


def weights_kernel(channels, groups, counts, orders, *refs):
    pooled, branch, gains, act, into, pre = (
        refs[k * groups : (k + 1) * groups] for k in range(6)
    )
    cot, place = refs[6 * groups : 6 * groups + 2]
    kept, sent, first, second, third = refs[-5:]
    high = act[0].shape[0]
    sums = [None] * 4
    for k in range(groups):
        wide = jnp.concatenate([pooled[k][j] for j in range(pooled[k].shape[0])], axis=1)
        own = cot[k * high : (k + 1) * high]
        terms = (
            dot(into[k][...], pre[k][...], ((0,), (0,))),
            dot(act[k][...], own, ((0,), (0,))),
            dot(wide, branch[k][...], ((1,), (0,))),
            gains[k][...],
        )
        sums = [term if total is None else total + term for total, term in zip(sums, terms)]
    row = lax.broadcasted_iota(jnp.int32, sums[2].shape, 0)
    first[...] = sums[0].astype(BF16)
    second[...] = sums[1].astype(BF16)
    rows = sums[2].shape[0]
    third[:rows] = jnp.where(row == channels, sums[3], sums[2]).astype(BF16)
    third[rows:] = jnp.zeros((third.shape[0] - rows, third.shape[1]), BF16)
    imgs, lats, share, part = counts
    turned = pl.program_id(0)
    for spot in range(imgs):
        differs = [
            sum(order[k] for k in range(len(order)) if spot & (imgs >> (k + 1))) for order in orders
        ]
        i = place[0] ^ (differs[0] + turned * (differs[1] - differs[0]))
        out, at = (kept, spot) if spot < imgs // 2 else (sent, spot - imgs // 2)
        for j in range(lats):
            lines = pl.ds(pl.multiple_of((i * lats + j) * share, share), share)
            out[at, 0, 2 * j * share : (2 * j + 1) * share] = first[lines]
            out[at, 0, (2 * j + 1) * share : (2 * j + 2) * share] = second[lines]
        out[at, 0, 2 * lats * share :] = third[pl.ds(pl.multiple_of(i * part, part), part)]


def weights_part(pooled, branch, gains, act, into, pre, cot, place, channels, counts, after):
    imgs, lats, share, part = counts
    depth = cot.shape[1]
    whole_rows = 2 * lats * share + part
    orders = [img_steps(imgs, turned)[::-1] for turned in (False, True)]
    out = jax.ShapeDtypeStruct((imgs // 2, 2, whole_rows, depth // 2), BF16)
    block = pl.BlockSpec((imgs // 2, 1, whole_rows, depth // 2), lambda n: (0, n, 0, 0))

    def half(array):
        return pl.BlockSpec((array.shape[0], depth // 2), lambda n: (0, n))

    return pl.pallas_call(
        partial(weights_kernel, channels, len(pooled), counts, orders),
        grid=(2,),
        in_specs=[whole(array) for array in pooled]
        + [half(array) for array in (*branch, *gains)]
        + [whole(array) for array in (*act, *into)]
        + [half(array) for array in (*pre, cot)]
        + [pl.BlockSpec(memory_space=pltpu.SMEM)]
        + anywhere(after),
        out_specs=[block, block],
        out_shape=[out, out],
        scratch_shapes=[
            pltpu.VMEM((depth, depth // 2), BF16),
            pltpu.VMEM((depth, depth // 2), BF16),
            pltpu.VMEM((imgs * part, depth // 2), BF16),
        ],
        compiler_params=params(),
        cost_estimate=cost(cot.shape[0] * depth * depth * 5, cot.shape[0] * depth * 14),
        name="weights_part",
    )(*pooled, *branch, *gains, *act, *into, *pre, cot, place, *after)


def order_kernel(blocks, widths, tails, extra, *refs):
    place = refs[blocks + len(tails)]
    rows = refs[0].shape[0]
    outs = refs[blocks + len(tails) + 1 + extra :]
    for k in range(blocks):
        lines = pl.ds(pl.multiple_of((place[0] ^ k) * rows, rows), rows)
        at = 0
        for out, width in zip(outs, widths):
            out[lines, :width] = refs[k][:, at : at + width]
            at += width
    for n, at in enumerate(tails):
        outs[at][:, widths[at] :] = refs[blocks + n][...]


def order_rows(blocks, place, widths, after=(), tails=None):
    rows, columns = blocks[0].shape
    tails = tails or {}
    outs = [
        jax.ShapeDtypeStruct(
            (len(blocks) * rows, width + (tails[k].shape[1] if k in tails else 0)), BF16
        )
        for k, width in enumerate(widths)
    ]
    return pl.pallas_call(
        partial(order_kernel, len(blocks), widths, list(tails), len(after)),
        grid=(1,),
        in_specs=[whole(block) for block in (*blocks, *tails.values())]
        + [pl.BlockSpec(memory_space=pltpu.SMEM)]
        + anywhere(after),
        out_specs=[whole(out) for out in outs],
        out_shape=outs,
        compiler_params=params(),
        cost_estimate=cost(1, len(blocks) * rows * columns * 4),
        name="order_rows",
    )(*blocks, *tails.values(), place, *after)


def add_kernel(groups, extra, *refs):
    for k in range(groups):
        own, got = refs[2 * k], refs[2 * k + 1]
        kept, sent = refs[2 * groups + extra + 2 * k : 2 * groups + extra + 2 * k + 2]
        total = (own[...].astype(F32) + got[...].astype(F32)).astype(BF16)
        half = total.shape[0] // 2
        kept[...] = total[:half].reshape(kept.shape)
        sent[...] = total[half:].reshape(sent.shape)


def add_blocks(groups, after):
    arrays, specs, outs = [], [], []
    for array, at, got in groups:
        if at is None:
            specs += [whole(array), whole(got)]
            shape = (array.shape[0] // 2, *array.shape[1:])
        else:
            block = (got.shape[0], 1, *got.shape[2:])
            specs += [pl.BlockSpec(block, lambda i, at=at: (0, at, 0, 0))] * 2
            shape = (got.shape[0] // 2, *got.shape[2:])
        arrays += [array, got]
        outs += [jax.ShapeDtypeStruct(shape, BF16)] * 2
    return pl.pallas_call(
        partial(add_kernel, len(groups), len(after)),
        grid=(1,),
        in_specs=specs + anywhere(after),
        out_specs=[whole(out) for out in outs],
        out_shape=outs,
        compiler_params=params(),
        cost_estimate=cost(1, sum(got.size for _, _, got in groups) * 6),
        name="add_blocks",
    )(*arrays, *after)


def last_blocks(firsts, gots, place, lats, share, after):
    _, rows, width = firsts[0].shape
    base = 2 * lats * share
    outs = [
        jax.ShapeDtypeStruct((lats, 2 * share, 2 * width), BF16),
        jax.ShapeDtypeStruct((rows - base, 2 * width), BF16),
    ]
    arrays = [*firsts, *gots]

    def kernel(*refs):
        spots, common = refs[-2:]
        for n in range(2):
            total = (refs[n][0].astype(F32) + refs[2 + n][0].astype(F32)).astype(BF16)
            lanes = slice(n * width, (n + 1) * width)
            for j in range(lats):
                spots[refs[4][0] ^ j, :, lanes] = total[2 * j * share : (2 * j + 2) * share]
            common[:, lanes] = total[base:]

    return pl.pallas_call(
        kernel,
        grid=(1,),
        in_specs=[whole(array) for array in arrays]
        + [pl.BlockSpec(memory_space=pltpu.SMEM)]
        + anywhere(after),
        out_specs=[whole(out) for out in outs],
        out_shape=outs,
        compiler_params=params(),
        cost_estimate=cost(1, rows * width * 12),
        name="last_blocks",
    )(*arrays, place, *after)


def early_kernel(depth, rows, offsets, *refs):
    count = len(offsets)
    place, cot = refs[:2]
    firsts, seconds = refs[2 : 2 + count], refs[2 + count : 2 + 2 * count]
    hidden, back, queries, grad_act, value_out, back_rows, values, outputs = refs[-8:]
    high, width = firsts[0].shape
    wide_rows = width - 2 * depth
    for first, second, offset in zip(firsts, seconds, offsets):
        lines = pl.ds(pl.multiple_of((place[0] ^ offset) * high, high), high)
        hidden[lines] = first[:, :depth]
        values[lines] = first[:, depth : depth + rows]
        queries[lines] = first[:, depth + wide_rows :]
        back_rows[lines] = second[:, :depth]
        outputs[lines] = second[:, depth:]
    back[...] = back_rows[...]
    grad_act[...] = dot(cot[...], back_rows[...], ((1,), (1,)))
    value_out[...] = dot(values[...], outputs[...], ((0,), (0,))).astype(BF16)


def early_part(place, cot, firsts, seconds, offsets, depth, rows, after):
    high = cot.shape[0]
    shape = jax.ShapeDtypeStruct
    arrays = [cot, *firsts, *seconds]
    outs = [shape((depth, depth), BF16)] * 3 + [shape((high, depth), F32), shape((rows, depth), BF16)]
    return pl.pallas_call(
        partial(early_kernel, depth, rows, offsets),
        grid=(1,),
        in_specs=[pl.BlockSpec(memory_space=pltpu.SMEM)]
        + [whole(array) for array in arrays]
        + anywhere(after),
        out_specs=[whole(out) for out in outs],
        out_shape=outs,
        scratch_shapes=[
            pltpu.VMEM((depth, depth), BF16),
            pltpu.VMEM((depth, rows), BF16),
            pltpu.VMEM((depth, depth), BF16),
        ],
        compiler_params=params(),
        cost_estimate=cost(0, 0),
        name="early_part",
    )(place, *arrays, *after)


def ask_kernel(channels, extra, pieces, lat_in, *refs):
    *messages, query_key = refs[extra:]
    whole_key = jnp.concatenate([pieces[k] for k in range(pieces.shape[0])], axis=1)
    query_key[...] = whole_key
    query = dot(whole_key, lat_in[...], ((1,), (1,)))
    row = lax.broadcasted_iota(jnp.int32, query.shape, 0)
    query = jnp.where(row == channels, 1.0, query).astype(BF16)
    span = messages[0].shape[-1]
    at = 0
    for out in messages:
        for k in range(out.shape[-3]):
            block = query[:, at : at + span]
            at += span
            if len(out.shape) == 3:
                out[k] = block
            else:
                for j in range(out.shape[0]):
                    out[j, k] = block


def ask(pieces, lat_in, channels, lats, images, turned, after):
    count, rows, columns = pieces.shape
    size = images // len(turned)
    shape = (size, rows, lat_in.shape[0] // images)
    outs = [jax.ShapeDtypeStruct(shape if turn else (lats, *shape), BF16) for turn in turned]
    outs.append(jax.ShapeDtypeStruct((rows, count * columns), BF16))
    return pl.pallas_call(
        partial(ask_kernel, channels, len(after)),
        grid=(1,),
        in_specs=[whole(pieces), whole(lat_in)] + anywhere(after),
        out_specs=[whole(out) for out in outs],
        out_shape=outs,
        compiler_params=params(),
        cost_estimate=cost(lat_in.size * rows * 2, lat_in.size * 4),
        name="ask",
    )(pieces, lat_in, *after)


def out_kernel(groups, extra, *refs):
    back, out = refs[2 * groups], refs[-1]
    half = pl.program_id(0)
    for k in range(groups):

        @pl.when(half == k)
        def _():
            total = refs[groups + k][...] + dot(refs[k][...], back[...], ((1,), (0,)))
            out[...] = total.astype(BF16)


def out_part(act, middle, back, after):
    high, depth = act[0].shape
    groups = len(act)
    return pl.pallas_call(
        partial(out_kernel, groups, len(after)),
        grid=(groups,),
        in_specs=[whole(array) for array in (*act, *middle, back)] + anywhere(after),
        out_specs=pl.BlockSpec((high, depth), lambda i: (i, 0)),
        out_shape=jax.ShapeDtypeStruct((groups * high, depth), BF16),
        compiler_params=params(),
        cost_estimate=cost(groups * high * depth * depth * 2, groups * high * depth * 8),
        name="out_part",
    )(*act, *middle, back, *after)


def relay_kernel(*refs):
    pass


def relay(values, after):
    values, after = list(values), list(after)
    return pl.pallas_call(
        relay_kernel,
        in_specs=anywhere(values) + anywhere(after),
        out_specs=anywhere(values),
        out_shape=[jax.ShapeDtypeStruct(value.shape, value.dtype) for value in values],
        input_output_aliases={k: k for k in range(len(values))},
        name="relay",
    )(*values, *after)


def local(
    imgs,
    lats,
    latents,
    pixels,
    keep_mask,
    cotangent,
    gain_latent,
    gain_pixel,
    gain_mlp,
    w_query,
    w_key,
    w_value,
    w_output,
    w_hidden,
    w_return,
):
    images, span, depth = latents.shape
    channels = pixels.shape[2]
    devices = imgs * lats
    share = depth // devices
    rows = round_up(channels + 6, 16)
    scale = depth ** (-0.5)
    me = lax.axis_index("img") * lats + lax.axis_index("lat")

    raw = jnp.swapaxes(pixels, 1, 2)
    bias = jnp.where(keep_mask > 0, 0.0, OUT_OF_SIGHT).astype(F32)[:, None, :]
    gain_column = gain_pixel[:, None]

    place = lax.axis_index("lat")[None]

    near, later = pack((w_query, w_key.T), (w_hidden, w_value.T, w_return, w_output))
    plain = share % 16 != 0
    if plain:
        near = lax.all_gather(near, "lat", axis=0, tiled=True)
        near_query, near_key = near[:, :depth], near[:, depth : depth + rows]
    else:
        near = [near] + [swap_lat(near, step, lats) for step in range(1, lats)]
        (later,) = relay([later], near[1:2])
        later = [later] + [swap_lat(later, step, lats) for step in range(1, lats)]
        near_query, near_key = order_rows(near, place, (depth, rows))
    key_rows = lax.all_gather(near_key, "img", axis=0, tiled=True)
    query_key = (dot(key_rows, near_query, ((0,), (1,))) * scale).astype(BF16)
    key_pieces = lax.all_gather(query_key, "img", axis=0, tiled=False)

    groups = 2 if images % 2 == 0 else 1
    size = images // groups
    flat = latents.reshape(images * span, depth)
    cot = cotangent.reshape(images * span, depth)
    gain_lat, gain_mid = gain_latent[None], gain_mlp[None]
    lat_in = (normalize(flat.astype(F32))[0] * gain_lat).astype(BF16)
    lat_blocks = lat_in.reshape(images, span, depth)
    row = lax.broadcasted_iota(jnp.int32, (1, rows, 1), 1)
    turned = [k % 2 == 0 for k in range(groups)]
    if plain:
        query_key = side(key_pieces)
        query = jnp.einsum("cd,bld->bcl", query_key, lat_blocks, preferred_element_type=F32)
        query = jnp.where(row == channels, 1.0, query).astype(BF16)
        messages = []
        for k in range(groups):
            part = query[k * size : (k + 1) * size]
            messages.append(part if turned[k] else jnp.broadcast_to(part[None], (lats, *part.shape)))
    else:
        *messages, query_key = ask(key_pieces, lat_in, channels, lats, images, turned, later[1:])
    query = messages[0]
    queries = [lat_gather(part, lats) for part in messages]
    (late_bias,) = relay([bias], [query])
    wide, tall = pixel_prep(raw, late_bias, gain_column, rows)

    wide_rows = round_up(rows, 128)
    img_place = lax.axis_index("img")[None]
    if not plain:
        first, second = order_rows(
            later, place, (depth + wide_rows, 2 * depth), [query], {0: near_query}
        )
        (first, second), offsets = img_gather([first, second], imgs)
    attended, parts = [], None
    for k in range(groups):
        after = [] if parts is None else parts[:1]
        parts = attend(wide, tall, queries[k], place, channels, k * size, turned[k], after)
        attended.append(lat_return(parts, lats))
    if plain:
        later = lax.all_gather(later, AXES, axis=0, tiled=True)
        query_rows = lax.all_gather(w_query, AXES, axis=0, tiled=True)
        hidden, back = later[:, :depth], later[:, depth + wide_rows : 2 * depth + wide_rows]
        grad_act = dot(cot, back, ((1,), (1,)))
        value_out = dot(
            later[:, depth : depth + rows], later[:, 2 * depth + wide_rows :], ((0,), (0,))
        ).astype(BF16)
    else:
        hidden, back, query_rows, grad_act, value_out = early_part(
            img_place, cot, first, second, offsets, depth, rows, parts[:1]
        )

    lines = [slice(k * size * span, (k + 1) * size * span) for k in range(groups)]
    middles, atts = [], []
    for k in range(groups):
        middles.append(
            middle_part(
                attended[k],
                flat,
                cot,
                grad_act,
                value_out,
                hidden,
                gain_mid,
                channels,
                k,
            )
        )
        atts.append(lat_gather(middles[k][0], lats))
    _, pooled, act, mlp_in, grad_pre, middle, branch, gain_grad = (
        [part[j] for part in middles] for j in range(8)
    )
    pin = []
    if not plain:
        part = round_up(-(-rows // imgs), 16)
        counts = (imgs, lats, share, part)
        orders = [img_steps(imgs, turned)[::-1] for turned in (False, True)]
        kept, sent = weights_part(
            pooled,
            branch,
            gain_grad,
            act,
            mlp_in,
            grad_pre,
            cot,
            img_place,
            channels,
            counts,
            [],
        )
        got = swap_img(sent, orders[0][0], imgs)
        pin = [sent]
    grad_raw, ends = None, []
    for k in range(groups):
        grad_raw, parts = attend_back(
            wide,
            tall,
            raw,
            gain_column,
            queries[k],
            atts[k],
            place,
            channels,
            k * size,
            grad_raw,
            turned[k],
            pin,
        )
        ends.append(lat_return(parts, lats))
        if k == 0 and not plain:
            split = add_blocks([(kept, n, got) for n in range(2)], parts[:1])
            kept, sent = split[0::2], split[1::2]
            pin = sent[:1]
    if not plain:
        for bit in range(1, len(orders[0]) - 1):
            gots = [swap_img(sent[n], orders[n][bit], imgs) for n in range(2)]
            split = add_blocks([(kept[n], None, gots[n]) for n in range(2)], parts[:1])
            kept, sent = split[0::2], split[1::2]

    output = out_part(act, middle, back, pin if plain else sent[:1])
    grad_latents, latent_grad = [], None
    for k in range(groups):
        terms, latent_grad = terms_part(
            ends[k],
            lat_in,
            channels,
            k,
            latent_grad,
            imgs if k == groups - 1 else 0,
            [output],
        )
        done = finish(terms, flat, branch[k], query_key, gain_lat, k, [latent_grad])
        grad_latents.append(done)
    if not plain:
        gots = [swap_img(sent[n], orders[n][-1], imgs) for n in range(2)]

    pieces = latent_grad
    latent_grad = sum_img(pieces, imgs)
    latent_terms = [latent_grad] + [swap_lat(latent_grad, step, lats) for step in range(1, lats)]
    latent_grad = sum_terms(latent_terms).astype(BF16)
    if plain:
        both = jnp.stack(
            [
                sum(dot(mlp_in[k], grad_pre[k], ((0,), (0,))) for k in range(groups)),
                sum(dot(act[k], cot[lines[k]], ((0,), (0,))) for k in range(groups)),
            ]
        ).astype(BF16)
        sums = lax.psum_scatter(both, AXES, scatter_dimension=1, tiled=True).astype(F32)
        shard_h, shard_r = sums[0], sums[1]
        common = sum(
            jnp.einsum(
                "bcl,bld->cd",
                pooled[k],
                branch[k].reshape(size, span, depth),
                preferred_element_type=F32,
            )
            for k in range(groups)
        )
        line = lax.broadcasted_iota(jnp.int32, (rows, 1), 0)
        common = jnp.where(line == channels, sum(gain_grad), common)
        pooled_grad = lax.psum(common, AXES).astype(BF16)
    else:
        blocks, common = last_blocks(kept, gots, place, lats, share, latent_terms[1:2])
        sent = [common] * (lats - 1) + [blocks[step] for step in range(1, lats)]
        came = [swap_lat(block, 1 + k % (lats - 1), lats) for k, block in enumerate(sent)]
        common = sum_terms([common] + came[: lats - 1]).astype(BF16)
        sums = sum_terms([blocks[0]] + came[lats - 1 :])
        shard_h, shard_r = sums[:share], sums[share:]
        pooled_grad = lax.all_gather(common, "img", axis=0, tiled=True)
    sum_mlp = pooled_grad[channels].astype(F32)
    pooled_grad = pooled_grad[:channels]
    latent_grad = side(lax.all_gather(latent_grad, "img", axis=0, tiled=False))[:channels]
    shard_o = dot(w_value, pooled_grad, ((0,), (0,)))
    shard_v = dot(pooled_grad, w_output, ((1,), (1,)))
    mine = lax.dynamic_slice_in_dim(latent_grad, me * share, share, 1)
    shard_q = dot(mine, key_rows[:, :channels], ((0,), (1,))) * scale
    columns = lax.dynamic_slice_in_dim(query_rows, me * share, share, 1)
    shard_k = dot(latent_grad, columns, ((1,), (0,))) * scale
    with_key = query_key[:channels].astype(F32) * latent_grad.astype(F32)
    with_value = value_out[:channels].astype(F32) * pooled_grad.astype(F32)
    sum_lat = jnp.sum(with_key, 0) / gain_latent
    sum_pix = jnp.sum(with_key + with_value, 1) / gain_pixel
    return (
        output.reshape(images, span, depth),
        jnp.concatenate(grad_latents).reshape(images, span, depth),
        jnp.swapaxes(grad_raw, 1, 2),
        shard_q,
        shard_k,
        shard_v,
        shard_o,
        shard_h,
        shard_r,
        sum_lat,
        sum_pix,
        sum_mlp,
    )


def solution(mesh):
    in_specs = (
        P("img", "lat", None),
        P("img", "lat", None),
        P("img", "lat"),
        P("img", "lat", None),
        P(),
        P(),
        P(),
        P(("img", "lat"), None),
        P(None, ("img", "lat")),
        P(None, ("img", "lat")),
        P(("img", "lat"), None),
        P(("img", "lat"), None),
        P(("img", "lat"), None),
    )
    out_specs = (
        P("img", "lat", None),
        P("img", "lat", None),
        P("img", "lat", None),
        P(("img", "lat"), None),
        P(None, ("img", "lat")),
        P(None, ("img", "lat")),
        P(("img", "lat"), None),
        P(("img", "lat"), None),
        P(("img", "lat"), None),
        P(),
        P(),
        P(),
    )
    step = partial(local, mesh.shape["img"], mesh.shape["lat"])
    return jax.shard_map(step, mesh=mesh, in_specs=in_specs, out_specs=out_specs, check_vma=False)
```

```python
from functools import partial

import jax
import jax.numpy as jnp
from jax import lax
from jax.experimental import pallas as pl
from jax.experimental.pallas import tpu as pltpu
from jax.sharding import PartitionSpec as P

F32 = jnp.float32
BF16 = jnp.bfloat16
AXES = ("img", "lat")
OUT_OF_SIGHT = -1e30
VMEM = 56 * 1024 * 1024
LESS_VMEM = 28 * 1024 * 1024


def round_up(value, unit):
    return -(-value // unit) * unit


def normalize(values):
    centered = values - jnp.mean(values, -1, keepdims=True)
    rstd = lax.rsqrt(jnp.mean(centered * centered, -1, keepdims=True) + 1e-05)
    return (centered * rstd, rstd)


def dot(left, right, contract):
    return lax.dot_general(left, right, (contract, ((), ())), preferred_element_type=F32)


def swap_lat(value, step, size):
    return lax.ppermute(value, "lat", [(i, i ^ step) for i in range(size)])


def swap_img(value, step, size):
    return lax.ppermute(value, "img", [(i, i ^ step) for i in range(size)])


def img_steps(size, turned=False):
    bits = [1 << k for k in reversed(range(size.bit_length() - 1))]
    return bits[1::-1] + bits[2:] if turned and len(bits) > 2 else bits


def img_gather(values, size):
    nearest, *others = [1 << k for k in range(size.bit_length() - 1)]
    blocks = [[value] for value in values]
    offsets = [0]
    for step in others:
        passed = offsets[1:]
        blocks = [held + [swap_img(held[0], step, size)] for held in blocks]
        offsets = offsets + [step]
        for offset in passed:
            for n, held in enumerate(blocks):
                turned = n % 2 == 1 and len(passed) == 1
                source = len(passed) + 1 if turned else offsets.index(offset)
                way = offset if turned else step
                blocks[n] = held + [swap_img(held[source], way, size)]
            offsets = offsets + [offset ^ step]
    blocks = [held + [swap_img(block, nearest, size) for block in held] for held in blocks]
    return blocks, offsets + [offset ^ nearest for offset in offsets]


def lat_gather(blocks, size):
    if blocks.ndim == 4:
        return [lax.all_to_all(blocks, "lat", 0, 0, tiled=True)]
    return [blocks] + [swap_lat(blocks, step, size) for step in range(1, size)]


def lat_return(blocks, size):
    if len(blocks) == 1:
        return [lax.all_to_all(blocks[0], "lat", 0, 0, tiled=True)]
    return [blocks[0]] + [swap_lat(blocks[step], step, size) for step in range(1, size)]


def sum_terms(terms):
    terms = [term.astype(F32) for term in terms]
    while len(terms) > 1:
        terms = [sum(terms[i : i + 2]) for i in range(0, len(terms), 2)]
    return terms[0]


def sum_img(pieces, imgs):
    pieces = lax.all_to_all(pieces, "img", 0, 0, tiled=True)
    return lax.reduce_precision(sum_terms([pieces[j] for j in range(imgs)]), 8, 7).astype(BF16)


def sum_lat_places(mine, lats):
    return sum_terms([mine] + [swap_lat(mine, step, lats) for step in range(1, lats)]).astype(BF16)


def side(pieces):
    return pieces.transpose(1, 0, 2).reshape(pieces.shape[1], -1)


def pixel_kernel(channels, raw_ref, bias_ref, gain_ref, wide_ref, tall_ref, work):
    raw = raw_ref[0].astype(F32)
    rows = work.shape[0]
    centered = raw - jnp.sum(raw, 0, keepdims=True) * (1.0 / channels)
    rstd = lax.rsqrt(jnp.sum(centered * centered, 0, keepdims=True) * (1.0 / channels) + 1e-05)
    base = channels // 8 * 8
    row = lax.broadcasted_iota(jnp.int32, (rows - base, raw.shape[1]), 0) + base
    work[base:rows] = jnp.where((row > channels) & (row < channels + 6), 1.0, 0.0).astype(F32)
    work[0:channels] = centered * rstd * gain_ref[...]
    work[channels : channels + 1] = bias_ref[0]
    whole = work[...]
    wide_ref[0] = whole[: wide_ref.shape[1]].astype(BF16)
    tall_ref[0] = whole.T.astype(BF16)


def pixel_prep(raw, bias, gain, rows):
    images, channels, pixels = raw.shape
    lanes = round_up(rows, 128)
    return pl.pallas_call(
        partial(pixel_kernel, channels),
        grid=(images,),
        in_specs=[
            pl.BlockSpec((1, channels, pixels), lambda b: (b, 0, 0)),
            pl.BlockSpec((1, 1, pixels), lambda b: (b, 0, 0)),
            pl.BlockSpec((channels, 1), lambda b: (0, 0)),
        ],
        out_specs=[
            pl.BlockSpec((1, rows, pixels), lambda b: (b, 0, 0)),
            pl.BlockSpec((1, pixels, lanes), lambda b: (b, 0, 0)),
        ],
        out_shape=[
            jax.ShapeDtypeStruct((images, rows, pixels), BF16),
            jax.ShapeDtypeStruct((images, pixels, lanes), BF16),
        ],
        scratch_shapes=[pltpu.VMEM((lanes, pixels), F32)],
        compiler_params=pltpu.CompilerParams(vmem_limit_bytes=VMEM),
        cost_estimate=pl.CostEstimate(flops=1, bytes_accessed=1, transcendentals=0),
    )(raw, bias, gain)


def split3(value):
    first = value.astype(BF16).astype(F32)
    second = (value - first).astype(BF16).astype(F32)
    return first, second, value - first - second


def whole(array):
    return pl.BlockSpec(array.shape, lambda *_: (0,) * array.ndim)


def near_by(arrays):
    return [pl.BlockSpec(memory_space=pltpu.VMEM)] * len(arrays)


def anywhere(arrays):
    return [pl.BlockSpec(memory_space=pl.ANY)] * len(arrays)


def params(limit=VMEM):
    return pltpu.CompilerParams(vmem_limit_bytes=limit)


def cost(flops, moved, exps=0):
    return pl.CostEstimate(flops=int(flops) * 4, bytes_accessed=int(moved) * 4, transcendentals=int(exps) * 4)


def terms_of_block(refs):
    if len(refs) > 1:
        return [ref[0] for ref in refs]
    return [refs[0][j, 0] for j in range(refs[0].shape[0])]


def attend_kernel(channels, count, extra, tile, turned, *refs):
    wide_ref, tall_ref, place = refs[:3]
    out_refs, (weight, scores) = refs[3 + count + extra : -2], refs[-2:]
    queries = terms_of_block(refs[3 : 3 + count])
    blocks, span = len(queries), queries[0].shape[1]
    rows = wide_ref.shape[1]
    pixels = wide_ref.shape[2]
    weight[:rows] = jnp.concatenate(queries, axis=1)
    weight[rows:] = jnp.zeros((weight.shape[0] - rows, weight.shape[1]), BF16)
    top = None
    for at in range(0, pixels, tile):
        part = dot(tall_ref[0, at : at + tile], weight[...], ((1,), (0,)))
        scores[at : at + tile] = part
        part_top = jnp.max(part, 0, keepdims=True)
        top = part_top if top is None else jnp.maximum(top, part_top)
    total = jnp.zeros((rows, weight.shape[1]), F32)
    for at in range(0, pixels, tile):
        expo = jnp.exp(scores[at : at + tile] - top).astype(BF16)
        total += dot(wide_ref[0, :, at : at + tile], expo, ((1,), (0,)))
    mass = total[channels + 1 : channels + 2]
    attended = message(channels, total * (1.0 / mass), split3(top + jnp.log(mass)))
    for k in range(blocks):
        part = attended[:, k * span : (k + 1) * span]
        if turned:
            out_refs[k][0] = part
        else:
            out_refs[0][k, 0] = part


def message(channels, body, lines):
    row = lax.broadcasted_iota(jnp.int32, body.shape, 0)
    body = jnp.where(row < channels, body, 0.0)
    for k, line in enumerate(lines):
        body = jnp.where(row == channels + 1 + k, line, body)
    return body.astype(BF16)


def block_specs(blocks, rows, span, turned):
    if turned:
        return [pl.BlockSpec((1, rows, span), lambda b: (b, 0, 0))] * blocks
    return [pl.BlockSpec((blocks, 1, rows, span), lambda b: (0, b, 0, 0))]


def block_shapes(blocks, images, rows, span, turned):
    if turned:
        return [jax.ShapeDtypeStruct((images, rows, span), BF16)] * blocks
    return [jax.ShapeDtypeStruct((blocks, images, rows, span), BF16)]


def attend(wide, tall, queries, place, channels, first, turned, after=()):
    _, rows, pixels = wide.shape
    images, _, span = queries[0].shape[-3:]
    blocks = len(queries) if turned else queries[0].shape[0]
    lanes = tall.shape[2]
    tile = min(256, pixels)
    return pl.pallas_call(
        partial(attend_kernel, channels, len(queries), len(after), tile, turned),
        grid=(images,),
        in_specs=[
            pl.BlockSpec((1, rows, pixels), lambda b: (b + first, 0, 0)),
            pl.BlockSpec((1, pixels, lanes), lambda b: (b + first, 0, 0)),
            pl.BlockSpec(memory_space=pltpu.SMEM),
        ]
        + block_specs(blocks, rows, span, turned)
        + anywhere(after),
        out_specs=block_specs(blocks, rows, span, turned),
        out_shape=block_shapes(blocks, images, rows, span, turned),
        scratch_shapes=[
            pltpu.VMEM((lanes, blocks * span), BF16),
            pltpu.VMEM((pixels, blocks * span), F32),
        ],
        compiler_params=params(),
        cost_estimate=cost(
            images * pixels * blocks * span * rows * 8,
            images * pixels * (rows + lanes) * 2 + images * rows * blocks * span * 4,
            images * pixels * blocks * span,
        ),
        name="attend",
    )(wide, tall, place, *queries, *after)


def attend_back_kernel(channels, count, extra, tile, turned, *refs):
    wide_ref, tall_ref, raw_ref, gain_ref, place = refs[:5]
    queries, atts = terms_of_block(refs[5 : 5 + count]), terms_of_block(refs[5 + count : 5 + 2 * count])
    outs = refs[5 + 2 * count + extra :]
    grad_ref, out_refs, (query_weight, att_weight) = outs[0], outs[1:-2], outs[-2:]
    blocks, span = len(queries), queries[0].shape[1]
    rows = wide_ref.shape[1]
    pixels = wide_ref.shape[2]
    width = blocks * span
    queries = jnp.concatenate(queries, axis=1)
    atts = jnp.concatenate(atts, axis=1)
    row = lax.broadcasted_iota(jnp.int32, (rows, width), 0)
    shifts = (row > channels) & (row < channels + 4)
    query_weight[:rows] = jnp.where(shifts, atts.astype(F32), queries.astype(F32)).astype(BF16)
    att_weight[:rows] = jnp.where(shifts, 0.0, atts.astype(F32)).astype(BF16)
    fill = jnp.zeros((query_weight.shape[0] - rows, width), BF16)
    query_weight[rows:] = fill
    att_weight[rows:] = fill
    total = jnp.zeros((rows, width), F32)
    for at in range(0, pixels, tile):
        tall = tall_ref[0, at : at + tile]
        probs = jnp.exp(dot(tall, query_weight[...], ((1,), (0,))))
        grad = probs * dot(tall, att_weight[...], ((1,), (0,)))
        grad_low = grad.astype(BF16)
        probs_low = probs.astype(BF16)
        total += dot(wide_ref[0, :, at : at + tile], grad_low, ((1,), (0,)))
        into = dot(query_weight[:rows], grad_low, ((1,), (1,)))
        into += dot(att_weight[:rows], probs_low, ((1,), (1,)))
        raw = raw_ref[0, :, at : at + tile].astype(F32)
        centered = raw - jnp.sum(raw, 0, keepdims=True) * (1.0 / channels)
        rstd = lax.rsqrt(
            jnp.sum(centered * centered, 0, keepdims=True) * (1.0 / channels) + 1e-05
        )
        hat = centered * rstd
        upstream = into[:channels] * gain_ref[...]
        mean = jnp.sum(upstream, 0, keepdims=True) * (1.0 / channels)
        along = jnp.sum(upstream * hat, 0, keepdims=True) * (1.0 / channels)
        grad_ref[0, :, at : at + tile] = (rstd * (upstream - mean - hat * along)).astype(BF16)
    total = total.astype(BF16)
    terms = [total[:, k * span : (k + 1) * span] for k in range(blocks)]
    if turned:
        for k in range(blocks):
            out_refs[0][place[0] ^ k, 0] = terms[k]
    else:
        for k in range(blocks):
            at = place[0] ^ k
            chosen = terms[0]
            for j in range(1, blocks):
                chosen = jnp.where(at == j, terms[j], chosen)
            out_refs[k][0] = chosen


def attend_back(wide, tall, raw, gain, queries, atts, place, channels, first, grad, turned, after=()):
    all_images, rows, pixels = wide.shape
    images, _, span = queries[0].shape[-3:]
    blocks = len(queries) if turned else queries[0].shape[0]
    lanes = tall.shape[2]
    tile = min(256, pixels)
    part = pl.BlockSpec((1, channels, pixels), lambda b: (b + first, 0, 0))
    earlier = [] if grad is None else [grad]
    extra = [*earlier, *after]
    results = pl.pallas_call(
        partial(attend_back_kernel, channels, len(queries), len(extra), tile, turned),
        grid=(images,),
        in_specs=[
            pl.BlockSpec((1, rows, pixels), lambda b: (b + first, 0, 0)),
            pl.BlockSpec((1, pixels, lanes), lambda b: (b + first, 0, 0)),
            part,
            whole(gain),
        ]
        + [
            pl.BlockSpec(memory_space=pltpu.SMEM),
        ]
        + block_specs(blocks, rows, span, turned) * 2
        + anywhere(extra),
        out_specs=[part] + block_specs(blocks, rows, span, not turned),
        out_shape=[jax.ShapeDtypeStruct((all_images, channels, pixels), BF16)]
        + block_shapes(blocks, images, rows, span, not turned),
        scratch_shapes=[
            pltpu.VMEM((lanes, blocks * span), BF16),
            pltpu.VMEM((lanes, blocks * span), BF16),
        ],
        compiler_params=params(),
        cost_estimate=cost(
            images * pixels * blocks * span * rows * 16,
            images * pixels * (rows * 3 + lanes) * 2 + images * rows * blocks * span * 6,
            images * pixels * blocks * span,
        ),
        input_output_aliases={5 + 2 * len(atts): 0} if earlier else {},
        name="attend_back",
    )(wide, tall, raw, gain, place, *queries, *atts, *extra)
    return results[0], results[1:]


def merged(channels, parts):
    parts = [part.astype(F32) for part in parts]
    at = channels + 1
    logs = [part[at : at + 1] + part[at + 1 : at + 2] + part[at + 2 : at + 3] for part in parts]
    top = logs[0]
    for log in logs[1:]:
        top = jnp.maximum(top, log)
    shares = [jnp.exp(log - top) for log in logs]
    mass = shares[0]
    for share in shares[1:]:
        mass = mass + share
    pooled = parts[0] * (shares[0] / mass)
    for part, share in zip(parts[1:], shares[1:]):
        pooled = pooled + part * (share / mass)
    return pooled, top + jnp.log(mass)


def rows_norm(values):
    depth = values.shape[1]
    centered = values - jnp.sum(values, 1, keepdims=True) * (1.0 / depth)
    rstd = lax.rsqrt(jnp.sum(centered * centered, 1, keepdims=True) * (1.0 / depth) + 1e-05)
    return centered * rstd, rstd


def rows_norm_back(upstream, hat, rstd):
    depth = hat.shape[1]
    mean = jnp.sum(upstream, 1, keepdims=True) * (1.0 / depth)
    along = jnp.sum(upstream * hat, 1, keepdims=True) * (1.0 / depth)
    return rstd * (upstream - mean - hat * along)


def terms_of(refs, k):
    if len(refs) > 1:
        return [ref[k] for ref in refs]
    return [refs[0][j, k] for j in range(refs[0].shape[0])]


def middle_kernel(channels, count, extra, *refs):
    parts, refs = refs[:count], refs[count:]
    (latents, cot, grad_act, value_out, hidden, gain) = refs[:6]
    (note, pooled_ref, act_ref, into_ref, pre_ref, middle_ref, branch_ref, gain_ref) = refs[
        6 + extra :
    ]
    images, rows, span = parts[0].shape[-3:]
    kept, flipped = [], []
    row = lax.broadcasted_iota(jnp.int32, (rows, span), 0)
    for k in range(images):
        pooled, logs = merged(channels, terms_of(parts, k))
        pooled = jnp.where(row < channels, pooled, 0.0)
        low = pooled.astype(BF16)
        pooled_ref[k] = low
        kept.append((pooled, logs))
        flipped.append(low.T)
    middle = latents[...].astype(F32) + dot(
        jnp.concatenate(flipped, axis=0), value_out[...], ((1,), (0,))
    )
    middle_ref[...] = middle
    hat, rstd = rows_norm(middle)
    into = (hat * gain[...]).astype(BF16)
    into_ref[...] = into
    pre = dot(into, hidden[...], ((1,), (0,)))
    below = 0.5 + 0.5 * lax.erf(pre * (0.5**0.5))
    act_ref[...] = (pre * below).astype(BF16)
    slope = below + pre * (jnp.exp(-0.5 * pre * pre) * (2.0 * jnp.pi) ** -0.5)
    grad_pre = (grad_act[...] * slope).astype(BF16)
    pre_ref[...] = grad_pre
    grad_into = dot(grad_pre, hidden[...], ((1,), (1,)))
    gain_ref[...] = jnp.sum(grad_into * hat, 0, keepdims=True)
    grad = cot[...].astype(F32) + rows_norm_back(grad_into * gain[...], hat, rstd)
    branch = grad.astype(BF16)
    branch_ref[...] = branch
    att = dot(value_out[...], branch, ((1,), (1,)))
    for k in range(images):
        pooled, logs = kept[k]
        mine = att[:, k * span : (k + 1) * span]
        inner = jnp.sum(mine.astype(BF16).astype(F32) * pooled, 0, keepdims=True)
        line = message(channels, mine, (*split3(-logs), *split3(-inner)[:2]))
        if len(note.shape) == 3:
            note[k] = line
        else:
            for j in range(note.shape[0]):
                note[j, k] = line


def middle_part(parts, latents, cot, grad_act, value_out, hidden, gain, channels, at, after=()):
    images, rows, span = parts[0].shape[-3:]
    depth = latents.shape[1]
    high = images * span
    own = pl.BlockSpec((high, depth), lambda i: (at, 0))
    shape = jax.ShapeDtypeStruct
    arrays = [*parts, latents, cot, grad_act, value_out, hidden, gain]
    outs = [
        shape(parts[0].shape, BF16),
        shape((images, rows, span), BF16),
        shape((high, depth), BF16),
        shape((high, depth), BF16),
        shape((high, depth), BF16),
        shape((high, depth), F32),
        shape((high, depth), BF16),
        shape((1, depth), F32),
    ]
    return pl.pallas_call(
        partial(middle_kernel, channels, len(parts), len(after)),
        grid=(1,),
        in_specs=[whole(part) for part in parts]
        + [own, own, own, whole(value_out), whole(hidden), whole(gain)]
        + anywhere(after),
        out_specs=[whole(out) for out in outs],
        out_shape=outs,
        compiler_params=params(),
        cost_estimate=cost(
            high * depth * (depth + rows) * 8, high * depth * 24 + depth * depth * 4, high * depth * 2
        ),
        name="middle_part",
    )(*arrays, *after)


def terms_kernel(channels, count, extra, last, *refs):
    parts, lat_in = refs[:count], refs[count]
    term_ref, sum_ref = refs[-2:]
    images, rows, span = parts[0].shape[-3:]
    row = lax.broadcasted_iota(jnp.int32, (rows, span), 0)
    terms = []
    for k in range(images):
        first, *others = terms_of(parts, k)
        term = first.astype(F32)
        for other in others:
            term = term + other.astype(F32)
        terms.append(jnp.where(row < channels, term, 0.0).astype(BF16))
        term_ref[k] = terms[k]
    total = dot(jnp.concatenate(terms, axis=1), lat_in[...], ((1,), (0,)))
    if extra:
        total = total + refs[count + 1][...]
    if last:
        width = sum_ref.shape[2]
        low = total.astype(BF16)
        for k in range(sum_ref.shape[0]):
            sum_ref[k] = low[:, k * width : (k + 1) * width]
    else:
        sum_ref[...] = total


def terms_part(parts, lat_in, channels, at, earlier, pieces, after):
    images, rows, span = parts[0].shape[-3:]
    depth = lat_in.shape[1]
    if pieces:
        total = jax.ShapeDtypeStruct((pieces, rows, depth // pieces), BF16)
    else:
        total = jax.ShapeDtypeStruct((rows, depth), F32)
    outs = [jax.ShapeDtypeStruct((images, rows, span), BF16), total]
    before = [] if earlier is None else [earlier]
    return pl.pallas_call(
        partial(terms_kernel, channels, len(parts), len(before), bool(pieces)),
        grid=(1,),
        in_specs=[whole(part) for part in parts]
        + [pl.BlockSpec((images * span, depth), lambda i: (at, 0))]
        + [whole(array) for array in before]
        + anywhere(after),
        out_specs=[whole(out) for out in outs],
        out_shape=outs,
        compiler_params=params(),
        cost_estimate=cost(images * span * depth * rows * 2, images * span * depth * 4),
        name="terms_part",
    )(*parts, lat_in, *before, *after)


def finish_kernel(extra, *refs):
    terms, latents, branch, query_key, gain = refs[:5]
    out_ref = refs[-1]
    tall = jnp.concatenate([terms[k].T for k in range(terms.shape[0])], axis=0)
    grad_in = dot(tall, query_key[...], ((1,), (0,)))
    hat, rstd = rows_norm(latents[...].astype(F32))
    back = rows_norm_back(grad_in * gain[...], hat, rstd)
    out_ref[...] = (branch[...].astype(F32) + back).astype(BF16)


def finish(terms, latents, branch, query_key, gain, at, earlier, after):
    images, rows, span = terms.shape
    high, depth = images * span, latents.shape[1]
    before = [] if earlier is None else [earlier]
    extra = [*before, *after]
    return pl.pallas_call(
        partial(finish_kernel, len(extra)),
        grid=(1,),
        in_specs=[
            whole(terms),
            pl.BlockSpec((high, depth), lambda i: (at, 0)),
            whole(branch),
            whole(query_key),
            whole(gain),
        ]
        + anywhere(extra),
        out_specs=pl.BlockSpec((high, depth), lambda i: (at, 0)),
        out_shape=jax.ShapeDtypeStruct(latents.shape, BF16),
        input_output_aliases={5: 0} if before else {},
        compiler_params=params(),
        cost_estimate=cost(high * depth * rows * 2, high * depth * 8),
        name="finish",
    )(terms, latents, branch, query_key, gain, *extra)


def pack_kernel(counts, *refs):
    ins, outs = refs[: -len(counts)], list(refs[-len(counts) :])
    at = 0
    for out, count in zip(outs, counts):
        column = 0
        for ref in ins[at : at + count]:
            width = round_up(ref.shape[1], 128)
            if width > ref.shape[1]:
                out[:, column : column + width] = jnp.zeros((out.shape[0], width), BF16)
            out[:, column : column + ref.shape[1]] = ref[...]
            column += width
        at += count


def pack(*groups):
    arrays = [array for group in groups for array in group]
    shapes = [
        jax.ShapeDtypeStruct(
            (group[0].shape[0], sum(round_up(array.shape[1], 128) for array in group)), BF16
        )
        for group in groups
    ]
    return pl.pallas_call(
        partial(pack_kernel, [len(group) for group in groups]),
        out_shape=shapes,
        compiler_params=params(),
        name="pack",
    )(*arrays)


def weights_kernel(channels, groups, counts, orders, *refs):
    pooled, branch, gains, act, into, pre = (
        refs[k * groups : (k + 1) * groups] for k in range(6)
    )
    cot, place = refs[6 * groups : 6 * groups + 2]
    kept, sent, first, second, third = refs[-5:]
    high = act[0].shape[0]
    sums = [None] * 4
    for k in range(groups):
        wide = jnp.concatenate([pooled[k][j] for j in range(pooled[k].shape[0])], axis=1)
        own = cot[k * high : (k + 1) * high]
        terms = (
            dot(into[k][...], pre[k][...], ((0,), (0,))),
            dot(act[k][...], own, ((0,), (0,))),
            dot(wide, branch[k][...], ((1,), (0,))),
            gains[k][...],
        )
        sums = [term if total is None else total + term for total, term in zip(sums, terms)]
    row = lax.broadcasted_iota(jnp.int32, sums[2].shape, 0)
    first[...] = sums[0].astype(BF16)
    second[...] = sums[1].astype(BF16)
    rows = sums[2].shape[0]
    third[:rows] = jnp.where(row == channels, sums[3], sums[2]).astype(BF16)
    third[rows:] = jnp.zeros((third.shape[0] - rows, third.shape[1]), BF16)
    imgs, lats, share, part = counts
    turned = pl.program_id(0)
    for spot in range(imgs):
        differs = [
            sum(order[k] for k in range(len(order)) if spot & (imgs >> (k + 1))) for order in orders
        ]
        i = place[0] ^ (differs[0] + turned * (differs[1] - differs[0]))
        out, at = (kept, spot) if spot < imgs // 2 else (sent, spot - imgs // 2)
        for j in range(lats):
            lines = pl.ds(pl.multiple_of((i * lats + j) * share, share), share)
            out[at, 0, 2 * j * share : (2 * j + 1) * share] = first[lines]
            out[at, 0, (2 * j + 1) * share : (2 * j + 2) * share] = second[lines]
        out[at, 0, 2 * lats * share :] = third[pl.ds(pl.multiple_of(i * part, part), part)]


def weights_part(pooled, branch, gains, act, into, pre, cot, place, channels, counts, after):
    imgs, lats, share, part = counts
    depth = cot.shape[1]
    whole_rows = 2 * lats * share + part
    orders = [img_steps(imgs, turned)[::-1] for turned in (False, True)]
    out = jax.ShapeDtypeStruct((imgs // 2, 2, whole_rows, depth // 2), BF16)
    block = pl.BlockSpec((imgs // 2, 1, whole_rows, depth // 2), lambda n: (0, n, 0, 0))

    def half(array):
        return pl.BlockSpec((array.shape[0], depth // 2), lambda n: (0, n))

    return pl.pallas_call(
        partial(weights_kernel, channels, len(pooled), counts, orders),
        grid=(2,),
        in_specs=[whole(array) for array in pooled]
        + [half(array) for array in (*branch, *gains)]
        + [whole(array) for array in (*act, *into)]
        + [half(array) for array in (*pre, cot)]
        + [pl.BlockSpec(memory_space=pltpu.SMEM)]
        + anywhere(after),
        out_specs=[block, block],
        out_shape=[out, out],
        scratch_shapes=[
            pltpu.VMEM((depth, depth // 2), BF16),
            pltpu.VMEM((depth, depth // 2), BF16),
            pltpu.VMEM((imgs * part, depth // 2), BF16),
        ],
        compiler_params=params(),
        cost_estimate=cost(cot.shape[0] * depth * depth * 5, cot.shape[0] * depth * 14),
        name="weights_part",
    )(*pooled, *branch, *gains, *act, *into, *pre, cot, place, *after)


def order_kernel(blocks, widths, tails, extra, *refs):
    place = refs[blocks + len(tails)]
    rows = refs[0].shape[0]
    outs = refs[blocks + len(tails) + 1 + extra :]
    for k in range(blocks):
        lines = pl.ds(pl.multiple_of((place[0] ^ k) * rows, rows), rows)
        at = 0
        for out, width in zip(outs, widths):
            out[lines, :width] = refs[k][:, at : at + width]
            at += width
    for n, at in enumerate(tails):
        outs[at][:, widths[at] :] = refs[blocks + n][...]


def order_rows(blocks, place, widths, after=(), tails=None):
    rows, columns = blocks[0].shape
    tails = tails or {}
    outs = [
        jax.ShapeDtypeStruct(
            (len(blocks) * rows, width + (tails[k].shape[1] if k in tails else 0)), BF16
        )
        for k, width in enumerate(widths)
    ]
    return pl.pallas_call(
        partial(order_kernel, len(blocks), widths, list(tails), len(after)),
        grid=(1,),
        in_specs=[whole(block) for block in (*blocks, *tails.values())]
        + [pl.BlockSpec(memory_space=pltpu.SMEM)]
        + anywhere(after),
        out_specs=[whole(out) for out in outs],
        out_shape=outs,
        compiler_params=params(),
        cost_estimate=cost(1, len(blocks) * rows * columns * 4),
        name="order_rows",
    )(*blocks, *tails.values(), place, *after)


def add_kernel(groups, extra, *refs):
    for k in range(groups):
        own, got = refs[2 * k], refs[2 * k + 1]
        kept, sent = refs[2 * groups + extra + 2 * k : 2 * groups + extra + 2 * k + 2]
        total = (own[...].astype(F32) + got[...].astype(F32)).astype(BF16)
        half = total.shape[0] // 2
        kept[...] = total[:half].reshape(kept.shape)
        sent[...] = total[half:].reshape(sent.shape)


def add_blocks(groups, after):
    arrays, specs, outs = [], [], []
    for array, at, got in groups:
        if at is None:
            specs += [whole(array), whole(got)]
            shape = (array.shape[0] // 2, *array.shape[1:])
        else:
            block = (got.shape[0], 1, *got.shape[2:])
            specs += [pl.BlockSpec(block, lambda i, at=at: (0, at, 0, 0))] * 2
            shape = (got.shape[0] // 2, *got.shape[2:])
        arrays += [array, got]
        outs += [jax.ShapeDtypeStruct(shape, BF16)] * 2
    return pl.pallas_call(
        partial(add_kernel, len(groups), len(after)),
        grid=(1,),
        in_specs=specs + anywhere(after),
        out_specs=[whole(out) for out in outs],
        out_shape=outs,
        compiler_params=params(),
        cost_estimate=cost(1, sum(got.size for _, _, got in groups) * 6),
        name="add_blocks",
    )(*arrays, *after)


def last_blocks(firsts, gots, place, lats, share, after):
    _, rows, width = firsts[0].shape
    base = 2 * lats * share
    outs = [
        jax.ShapeDtypeStruct((lats, 2 * share, 2 * width), BF16),
        jax.ShapeDtypeStruct((rows - base, 2 * width), BF16),
    ]
    arrays = [*firsts, *gots]

    def kernel(*refs):
        spots, common = refs[-2:]
        for n in range(2):
            total = (refs[n][0].astype(F32) + refs[2 + n][0].astype(F32)).astype(BF16)
            lanes = slice(n * width, (n + 1) * width)
            for j in range(lats):
                spots[refs[4][0] ^ j, :, lanes] = total[2 * j * share : (2 * j + 2) * share]
            common[:, lanes] = total[base:]

    return pl.pallas_call(
        kernel,
        grid=(1,),
        in_specs=[whole(array) for array in arrays]
        + [pl.BlockSpec(memory_space=pltpu.SMEM)]
        + anywhere(after),
        out_specs=[whole(out) for out in outs],
        out_shape=outs,
        compiler_params=params(),
        cost_estimate=cost(1, rows * width * 12),
        name="last_blocks",
    )(*arrays, place, *after)


def early_kernel(depth, rows, offsets, *refs):
    count = len(offsets)
    place, cot = refs[:2]
    firsts, seconds = refs[2 : 2 + count], refs[2 + count : 2 + 2 * count]
    hidden, back, queries, grad_act, value_out, back_rows, values, outputs = refs[-8:]
    high, width = firsts[0].shape
    wide_rows = width - 2 * depth
    for first, second, offset in zip(firsts, seconds, offsets):
        lines = pl.ds(pl.multiple_of((place[0] ^ offset) * high, high), high)
        hidden[lines] = first[:, :depth]
        values[lines] = first[:, depth : depth + rows]
        queries[lines] = first[:, depth + wide_rows :]
        back_rows[lines] = second[:, :depth]
        outputs[lines] = second[:, depth:]
    back[...] = back_rows[...]
    grad_act[...] = dot(cot[...], back_rows[...], ((1,), (1,)))
    value_out[...] = dot(values[...], outputs[...], ((0,), (0,))).astype(BF16)


def early_part(place, cot, firsts, seconds, offsets, depth, rows, after):
    high = cot.shape[0]
    shape = jax.ShapeDtypeStruct
    arrays = [cot, *firsts, *seconds]
    outs = [shape((depth, depth), BF16)] * 3 + [shape((high, depth), F32), shape((rows, depth), BF16)]
    return pl.pallas_call(
        partial(early_kernel, depth, rows, offsets),
        grid=(1,),
        in_specs=[pl.BlockSpec(memory_space=pltpu.SMEM)]
        + [whole(array) for array in arrays]
        + anywhere(after),
        out_specs=[whole(out) for out in outs],
        out_shape=outs,
        scratch_shapes=[
            pltpu.VMEM((depth, depth), BF16),
            pltpu.VMEM((depth, rows), BF16),
            pltpu.VMEM((depth, depth), BF16),
        ],
        compiler_params=params(),
        cost_estimate=cost(0, 0),
        name="early_part",
    )(place, *arrays, *after)


def ask_kernel(channels, extra, pieces, lat_in, *refs):
    *messages, query_key = refs[extra:]
    whole_key = jnp.concatenate([pieces[k] for k in range(pieces.shape[0])], axis=1)
    query_key[...] = whole_key
    query = dot(whole_key, lat_in[...], ((1,), (1,)))
    row = lax.broadcasted_iota(jnp.int32, query.shape, 0)
    query = jnp.where(row == channels, 1.0, query).astype(BF16)
    span = messages[0].shape[-1]
    at = 0
    for out in messages:
        for k in range(out.shape[-3]):
            block = query[:, at : at + span]
            at += span
            if len(out.shape) == 3:
                out[k] = block
            else:
                for j in range(out.shape[0]):
                    out[j, k] = block


def ask(pieces, lat_in, channels, lats, images, turned, after):
    count, rows, columns = pieces.shape
    size = images // len(turned)
    shape = (size, rows, lat_in.shape[0] // images)
    outs = [jax.ShapeDtypeStruct(shape if turn else (lats, *shape), BF16) for turn in turned]
    outs.append(jax.ShapeDtypeStruct((rows, count * columns), BF16))
    return pl.pallas_call(
        partial(ask_kernel, channels, len(after)),
        grid=(1,),
        in_specs=[whole(pieces), whole(lat_in)] + anywhere(after),
        out_specs=[whole(out) for out in outs],
        out_shape=outs,
        compiler_params=params(),
        cost_estimate=cost(lat_in.size * rows * 2, lat_in.size * 4),
        name="ask",
    )(pieces, lat_in, *after)


def out_kernel(groups, extra, *refs):
    back, out = refs[2 * groups], refs[-1]
    half = pl.program_id(0)
    for k in range(groups):

        @pl.when(half == k)
        def _():
            total = refs[groups + k][...] + dot(refs[k][...], back[...], ((1,), (0,)))
            out[...] = total.astype(BF16)


def out_part(act, middle, back, after):
    high, depth = act[0].shape
    groups = len(act)
    return pl.pallas_call(
        partial(out_kernel, groups, len(after)),
        grid=(groups,),
        in_specs=[whole(array) for array in (*act, *middle, back)] + anywhere(after),
        out_specs=pl.BlockSpec((high, depth), lambda i: (i, 0)),
        out_shape=jax.ShapeDtypeStruct((groups * high, depth), BF16),
        compiler_params=params(),
        cost_estimate=cost(groups * high * depth * depth * 2, groups * high * depth * 8),
        name="out_part",
    )(*act, *middle, back, *after)


def relay_kernel(*refs):
    pass


def relay(values, after):
    values, after = list(values), list(after)
    return pl.pallas_call(
        relay_kernel,
        in_specs=anywhere(values) + anywhere(after),
        out_specs=anywhere(values),
        out_shape=[jax.ShapeDtypeStruct(value.shape, value.dtype) for value in values],
        input_output_aliases={k: k for k in range(len(values))},
        name="relay",
    )(*values, *after)


def local(
    imgs,
    lats,
    latents,
    pixels,
    keep_mask,
    cotangent,
    gain_latent,
    gain_pixel,
    gain_mlp,
    w_query,
    w_key,
    w_value,
    w_output,
    w_hidden,
    w_return,
):
    images, span, depth = latents.shape
    channels = pixels.shape[2]
    devices = imgs * lats
    share = depth // devices
    rows = round_up(channels + 6, 16)
    scale = depth ** (-0.5)
    me = lax.axis_index("img") * lats + lax.axis_index("lat")

    raw = jnp.swapaxes(pixels, 1, 2)
    bias = jnp.where(keep_mask > 0, 0.0, OUT_OF_SIGHT).astype(F32)[:, None, :]
    gain_column = gain_pixel[:, None]

    place = lax.axis_index("lat")[None]

    near, later = pack((w_query, w_key.T), (w_hidden, w_value.T, w_return, w_output))
    plain = share % 16 != 0
    if plain:
        near = lax.all_gather(near, "lat", axis=0, tiled=True)
        near_query, near_key = near[:, :depth], near[:, depth : depth + rows]
    else:
        near = [near] + [swap_lat(near, step, lats) for step in range(1, lats)]
        (later,) = relay([later], near[1:2])
        later = [later] + [swap_lat(later, step, lats) for step in range(1, lats)]
        near_query, near_key = order_rows(near, place, (depth, rows))
    key_rows = lax.all_gather(near_key, "img", axis=0, tiled=True)
    query_key = (dot(key_rows, near_query, ((0,), (1,))) * scale).astype(BF16)
    key_pieces = lax.all_gather(query_key, "img", axis=0, tiled=False)

    groups = 2 if images % 2 == 0 else 1
    size = images // groups
    flat = latents.reshape(images * span, depth)
    cot = cotangent.reshape(images * span, depth)
    gain_lat, gain_mid = gain_latent[None], gain_mlp[None]
    lat_in = (normalize(flat.astype(F32))[0] * gain_lat).astype(BF16)
    lat_blocks = lat_in.reshape(images, span, depth)
    row = lax.broadcasted_iota(jnp.int32, (1, rows, 1), 1)
    turned = [k % 2 == 0 for k in range(groups)]
    if plain:
        query_key = side(key_pieces)
        query = jnp.einsum("cd,bld->bcl", query_key, lat_blocks, preferred_element_type=F32)
        query = jnp.where(row == channels, 1.0, query).astype(BF16)
        messages = []
        for k in range(groups):
            part = query[k * size : (k + 1) * size]
            messages.append(part if turned[k] else jnp.broadcast_to(part[None], (lats, *part.shape)))
    else:
        *messages, query_key = ask(key_pieces, lat_in, channels, lats, images, turned, later[1:])
    query = messages[0]
    queries = [lat_gather(part, lats) for part in messages]
    (late_bias,) = relay([bias], [query])
    wide, tall = pixel_prep(raw, late_bias, gain_column, rows)

    wide_rows = round_up(rows, 128)
    img_place = lax.axis_index("img")[None]
    if not plain:
        first, second = order_rows(
            later, place, (depth + wide_rows, 2 * depth), [query], {0: near_query}
        )
        (first, second), offsets = img_gather([first, second], imgs)
    attended, parts = [], None
    for k in range(groups):
        after = [] if parts is None else parts[:1]
        parts = attend(wide, tall, queries[k], place, channels, k * size, turned[k], after)
        attended.append(lat_return(parts, lats))
    if plain:
        later = lax.all_gather(later, AXES, axis=0, tiled=True)
        query_rows = lax.all_gather(w_query, AXES, axis=0, tiled=True)
        hidden, back = later[:, :depth], later[:, depth + wide_rows : 2 * depth + wide_rows]
        grad_act = dot(cot, back, ((1,), (1,)))
        value_out = dot(
            later[:, depth : depth + rows], later[:, 2 * depth + wide_rows :], ((0,), (0,))
        ).astype(BF16)
    else:
        hidden, back, query_rows, grad_act, value_out = early_part(
            img_place, cot, first, second, offsets, depth, rows, parts[:1]
        )

    lines = [slice(k * size * span, (k + 1) * size * span) for k in range(groups)]
    middles, atts = [], []
    for k in range(groups):
        middles.append(
            middle_part(
                attended[k],
                flat,
                cot,
                grad_act,
                value_out,
                hidden,
                gain_mid,
                channels,
                k,
            )
        )
        atts.append(lat_gather(middles[k][0], lats))
    _, pooled, act, mlp_in, grad_pre, middle, branch, gain_grad = (
        [part[j] for part in middles] for j in range(8)
    )
    pin = []
    if not plain:
        part = round_up(-(-rows // imgs), 16)
        counts = (imgs, lats, share, part)
        orders = [img_steps(imgs, turned)[::-1] for turned in (False, True)]
        kept, sent = weights_part(
            pooled,
            branch,
            gain_grad,
            act,
            mlp_in,
            grad_pre,
            cot,
            img_place,
            channels,
            counts,
            [],
        )
        got = swap_img(sent, orders[0][0], imgs)
        pin = [sent]
    grad_raw, ends = None, []
    for k in range(groups):
        grad_raw, parts = attend_back(
            wide,
            tall,
            raw,
            gain_column,
            queries[k],
            atts[k],
            place,
            channels,
            k * size,
            grad_raw,
            turned[k],
            pin,
        )
        ends.append(lat_return(parts, lats))
        if k == 0 and not plain:
            split = add_blocks([(kept, n, got) for n in range(2)], parts[:1])
            kept, sent = split[0::2], split[1::2]
            pin = sent[:1]
    if not plain:
        for bit in range(1, len(orders[0]) - 1):
            gots = [swap_img(sent[n], orders[n][bit], imgs) for n in range(2)]
            split = add_blocks([(kept[n], None, gots[n]) for n in range(2)], parts[:1])
            kept, sent = split[0::2], split[1::2]

    output = out_part(act, middle, back, pin if plain else sent[:1])
    grad_latents, latent_grad = None, None
    for k in range(groups):
        terms, latent_grad = terms_part(
            ends[k],
            lat_in,
            channels,
            k,
            latent_grad,
            imgs if k == groups - 1 else 0,
            [output],
        )
        grad_latents = finish(
            terms, flat, branch[k], query_key, gain_lat, k, grad_latents, [latent_grad]
        )
    if not plain:
        gots = [swap_img(sent[n], orders[n][-1], imgs) for n in range(2)]

    pieces = latent_grad
    latent_grad = sum_img(pieces, imgs)
    latent_terms = [latent_grad] + [swap_lat(latent_grad, step, lats) for step in range(1, lats)]
    latent_grad = sum_terms(latent_terms).astype(BF16)
    if plain:
        both = jnp.stack(
            [
                sum(dot(mlp_in[k], grad_pre[k], ((0,), (0,))) for k in range(groups)),
                sum(dot(act[k], cot[lines[k]], ((0,), (0,))) for k in range(groups)),
            ]
        ).astype(BF16)
        sums = lax.psum_scatter(both, AXES, scatter_dimension=1, tiled=True).astype(F32)
        shard_h, shard_r = sums[0], sums[1]
        common = sum(
            jnp.einsum(
                "bcl,bld->cd",
                pooled[k],
                branch[k].reshape(size, span, depth),
                preferred_element_type=F32,
            )
            for k in range(groups)
        )
        line = lax.broadcasted_iota(jnp.int32, (rows, 1), 0)
        common = jnp.where(line == channels, sum(gain_grad), common)
        pooled_grad = lax.psum(common, AXES).astype(BF16)
    else:
        blocks, common = last_blocks(kept, gots, place, lats, share, latent_terms[1:2])
        sent = [common] * (lats - 1) + [blocks[step] for step in range(1, lats)]
        came = [swap_lat(block, 1 + k % (lats - 1), lats) for k, block in enumerate(sent)]
        common = sum_terms([common] + came[: lats - 1]).astype(BF16)
        sums = sum_terms([blocks[0]] + came[lats - 1 :])
        shard_h, shard_r = sums[:share], sums[share:]
        pooled_grad = lax.all_gather(common, "img", axis=0, tiled=True)
    sum_mlp = pooled_grad[channels].astype(F32)
    pooled_grad = pooled_grad[:channels]
    latent_grad = side(lax.all_gather(latent_grad, "img", axis=0, tiled=False))[:channels]
    shard_o = dot(w_value, pooled_grad, ((0,), (0,)))
    shard_v = dot(pooled_grad, w_output, ((1,), (1,)))
    mine = lax.dynamic_slice_in_dim(latent_grad, me * share, share, 1)
    shard_q = dot(mine, key_rows[:, :channels], ((0,), (1,))) * scale
    columns = lax.dynamic_slice_in_dim(query_rows, me * share, share, 1)
    shard_k = dot(latent_grad, columns, ((1,), (0,))) * scale
    with_key = query_key[:channels].astype(F32) * latent_grad.astype(F32)
    with_value = value_out[:channels].astype(F32) * pooled_grad.astype(F32)
    sum_lat = jnp.sum(with_key, 0) / gain_latent
    sum_pix = jnp.sum(with_key + with_value, 1) / gain_pixel
    return (
        output.reshape(images, span, depth),
        grad_latents.reshape(images, span, depth),
        jnp.swapaxes(grad_raw, 1, 2),
        shard_q,
        shard_k,
        shard_v,
        shard_o,
        shard_h,
        shard_r,
        sum_lat,
        sum_pix,
        sum_mlp,
    )


def solution(mesh):
    in_specs = (
        P("img", "lat", None),
        P("img", "lat", None),
        P("img", "lat"),
        P("img", "lat", None),
        P(),
        P(),
        P(),
        P(("img", "lat"), None),
        P(None, ("img", "lat")),
        P(None, ("img", "lat")),
        P(("img", "lat"), None),
        P(("img", "lat"), None),
        P(("img", "lat"), None),
    )
    out_specs = (
        P("img", "lat", None),
        P("img", "lat", None),
        P("img", "lat", None),
        P(("img", "lat"), None),
        P(None, ("img", "lat")),
        P(None, ("img", "lat")),
        P(("img", "lat"), None),
        P(("img", "lat"), None),
        P(("img", "lat"), None),
        P(),
        P(),
        P(),
    )
    step = partial(local, mesh.shape["img"], mesh.shape["lat"])
    return jax.shard_map(step, mesh=mesh, in_specs=in_specs, out_specs=out_specs, check_vma=False)
```
